32 devices in a mesh: group: 2 (over x), ep: 16 (over z, y, core).
Axes of the slice: x: 2, y: 2, z: 4, core: 2. Of those that a mesh axis runs over, the one named last changes fastest.
Arguments:
- hidden_rows: bfloat16 [256, 7168], P(('group', 'ep')), parts along dimension 0, may hold values from -6 to 6
- group_ids: int32 [256, 2], P(('group', 'ep')), parts along dimension 0, may hold values from 0 to 1, all different within a row; in each aligned block of 8 rows (0 to 7, 8 to 15, ...) at most 8 rows name the same one
- route_gates: float32 [256, 2], P(('group', 'ep')), parts along dimension 0, may hold values from 0.1 to 1
- w_gate: bfloat16 [16, 7168, 128], P('ep'), may hold values from -0.0625 to 0.0625
- w_up: bfloat16 [16, 7168, 128], P('ep'), may hold values from -0.0625 to 0.0625
- w_down: bfloat16 [16, 128, 7168], P('ep'), may hold values from -0.1875 to 0.1875
- queries: bfloat16 [128, 128, 576], P(('group', 'ep')), parts along dimension 0, may hold values from -24 to 24
- new_latent: bfloat16 [128, 576], P(('group', 'ep')), parts along dimension 0, may hold values from -4 to 4
- latent_cache: bfloat16 [128, 1024, 576], P(('group', 'ep')), parts along dimension 0, may hold values from -4 to 4
- cache_lengths: int32 [128], P('group'), parts along dimension 0, may hold values from 2 to 1024, as said below
- moved_slot: int32 [32], P('group'), parts along dimension 0, may hold values from 0 to 3, as said below
Outputs:
- moe_out: bfloat16 [256, 7168], P(('group', 'ep')), parts along dimension 0
- attn_out: bfloat16 [128, 128, 512], P(('group', 'ep')), parts along dimension 0
The draws below stay inside these ranges and needn't reach their ends.
There are 2 independent parts, one for each index of `group`. The reference program is written for one: setup_inputs(seed, part) draws one part's arguments, and reference() takes and returns one part's arrays. A program takes and returns all parts, laid end to end along the dimension named above; an argument that names none is the same for every part. Nothing has to cross between parts.
Inputs may be any that keep to these rules, and one draw needn't show every extreme that they name: `group_ids`: each row names 2 different groups; no group is named by more than 8 rows of one device. The request in slot moved_slot[d] of device d moves to device d + 1 (the last to the first) and takes slot moved_slot[d + 1] there. `cache_lengths`: some request holds 1024 positions in every draw.
All inputs are finite; a program needn't handle non-finite values.
Results may differ from the reference program's by a relative error of at most 0.0065.
Values may be sent and summed in bfloat16 or wider, within the bound.
No kernel may reach another device: no remote copies, remote signals or barrier semaphores. Data moves between devices by JAX's collectives and lax.ppermute only.
A program may use at most 128 MiB of HBM per device.

```python
import math
import jax
import jax.numpy as jnp
import numpy as np
from jax import lax

D = 7168
HEADS = 128
NOPE = 512
LAT = 576
HID = 1024
SPLIT = 8
TOK_DEV = 8
REQ_DEV = 4
CACHE = 1024
EP_RANKS = 16
NG = 2
TOPK = 2
TOKENS = 128
SLOTS = 64


def shared_cache(key):
    raw_cache = jax.random.normal(jax.random.fold_in(key, 101), (SLOTS, CACHE, LAT), jnp.float32)
    return jnp.clip(raw_cache, -4.0, 4.0)


def shared_moves(key):
    return jax.random.randint(jax.random.fold_in(key, 202), (EP_RANKS,), 0, REQ_DEV).astype(jnp.int32)


def draw_moved_slot(key, part):
    return shared_moves(key)


def draw_latent_cache(key, part):
    base_cache = shared_cache(key)
    return base_cache.astype(jnp.bfloat16)


def draw_queries(key, part):
    key = jax.random.fold_in(key, 2)
    drawn_rows = jnp.clip(jax.random.normal(key, (SLOTS, HEADS, LAT), jnp.float32), -4.0, 4.0)
    return drawn_rows.astype(jnp.bfloat16)


def draw_cache_lengths(key, part):
    key = jax.random.fold_in(key, 3)
    spread_lengths = jax.random.randint(key, (SLOTS,), 2, CACHE + 1)
    longest = jax.random.randint(jax.random.fold_in(key, 4), (), 0, SLOTS)
    return spread_lengths.at[longest].set(CACHE).astype(jnp.int32)


def block_levels(key, extent, split, least, top_value):
    def one(position, blocks):
        steps = jax.random.uniform(jax.random.fold_in(jax.random.fold_in(key, 6), position), (blocks,), jnp.float32, least / len(split), top_value / len(split))
        return jnp.repeat(jnp.exp(steps), extent[position] // blocks).reshape((-1,) + (1,) * (len(extent) - position - 1))

    gain = one(*split[0])
    for cut in split[1:]:
        gain = gain * one(*cut)
    return gain


def deal_out(rng, own, number, rows, count, top, most, lean):
    ranking = jax.random.permutation(rng, count)
    heavy_load, common = portions_of(count, rows * top, most, lean, True), portions_of(count, rows * top, most, lean, False)
    places = jnp.arange(count)

    def named(sizes, rotation):
        used = int((sizes > 0).sum())
        fixed = max(1, used // 4)
        shifted = fixed + (places - fixed + rotation * (used - fixed)) % max(1, count - fixed)
        return jnp.zeros((count,), jnp.int32).at[ranking[jnp.where(places < fixed, places, shifted)]].set(jnp.asarray(sizes, jnp.int32))

    sizes = jnp.where(number % 4 == 0, named(heavy_load, number // 4), named(common, number - number // 4 - 1))
    mixed = jax.random.permutation(jax.random.fold_in(own, 3), count)
    giver, taker = mixed[0:count // 2 * 2:2], mixed[1:count // 2 * 2:2]
    slack = jnp.minimum(sizes[giver] - 1, most - sizes[taker]) // 2
    slack = jnp.where((giver == ranking[0]) | (taker == ranking[0]) | (sizes[taker] == 0), 0, jnp.maximum(slack, 0))
    shifted = jax.random.randint(jax.random.fold_in(own, 4), (count // 2,), 0, 1 << 20) % (slack + 1)
    sizes = sizes.at[giver].add(-shifted).at[taker].add(shifted)
    members = jnp.searchsorted(jnp.cumsum(sizes), jnp.arange(rows * top), side="right").astype(jnp.int32)
    listing = members.reshape(top, rows).T
    listing = listing[jax.random.permutation(jax.random.fold_in(own, 1), rows)]
    rotation = jax.random.randint(jax.random.fold_in(own, 2), (rows, 1), 0, top)
    return jnp.take_along_axis(listing, (jnp.arange(top)[None, :] + rotation) % top, axis=1)


def portions_of(count, total, most, skew, full):
    weights = [(1 << 20) // math.isqrt(rank ** skew) + 1 for rank in range(1, count + 1)]
    largest = most if full else min(most, max(-(-total // count), total * weights[0] // sum(weights)))
    least = 1 if total - largest >= count - 1 else 0
    counts, spare = [largest] + [least] * (count - 1), total - largest - least * (count - 1)
    while spare > 0:
        candidates = [i for i in range(1, count) if counts[i] < largest] or [i for i in range(1, count) if counts[i] < most]
        mass, budget = sum([weights[i] for i in candidates]), spare
        for i in candidates:
            extra = min(most - counts[i], max(1, budget * weights[i] // mass), spare)
            counts[i] = counts[i] + extra
            spare = spare - extra
    return np.array(counts)


def gaussian(key, dims, spread, limit, shards=(), held_as=jnp.bfloat16):
    factor_of = block_levels(key, dims, shards, -0.22, 0.18) if shards else 1.0
    result = jax.random.normal(key, dims, jnp.float32) * spread * factor_of
    return jnp.minimum(jnp.maximum(result, -limit), limit).astype(held_as)


def setup_inputs(seed: int = 0, part: int = 0) -> dict:
    key_list = jax.random.split(jax.random.key(seed), 12)
    own_keys = jax.random.split(jax.random.fold_in(key_list[11], part), 12)
    hidden_rows = gaussian(own_keys[0], (TOKENS, D), 1.0, 6.0, ((0, 16),))
    group_ids_keys = jax.random.split(jax.random.fold_in(own_keys[1], 1), TOKENS // TOK_DEV)
    group_ids_turns = jax.random.permutation(jax.random.fold_in(own_keys[1], 3), TOKENS // TOK_DEV)
    group_ids = jax.vmap(lambda own, number: deal_out(jax.random.fold_in(own_keys[1], 2), own, number, TOK_DEV, NG, TOPK, TOK_DEV, 2))(group_ids_keys, group_ids_turns).reshape((TOKENS, TOPK))
    route_gates = jnp.clip(jnp.exp(math.log(1.0) - 2.3025851 * jax.random.uniform(own_keys[2], (TOKENS, TOPK), jnp.float32) ** block_levels(own_keys[2], (TOKENS, TOPK), ((0, 16),), -0.2, 0.2)), 0.1, 1.0)
    w_gate = gaussian(key_list[3], (NG * SPLIT, D, HID // SPLIT), D ** -0.5, 0.0625, ((0, 16),))
    w_up = gaussian(key_list[4], (NG * SPLIT, D, HID // SPLIT), D ** -0.5, 0.0625, ((0, 16),))
    w_down = gaussian(key_list[5], (NG * SPLIT, HID // SPLIT, D), HID ** -0.5, 0.1875, ((0, 16),))
    queries = draw_queries(jax.random.fold_in(jax.random.fold_in(key_list[11], part), 71), part)
    new_latent = gaussian(own_keys[7], (SLOTS, LAT), 1.0, 4.0, ((0, 16),))
    latent_cache = draw_latent_cache(jax.random.fold_in(jax.random.fold_in(key_list[11], part), 71), part)
    cache_lengths = draw_cache_lengths(jax.random.fold_in(jax.random.fold_in(key_list[11], part), 71), part)
    moved_slot = draw_moved_slot(jax.random.fold_in(jax.random.fold_in(key_list[11], part), 71), part)
    return {"hidden_rows": hidden_rows, "group_ids": group_ids, "route_gates": route_gates, "w_gate": w_gate, "w_up": w_up, "w_down": w_down, "queries": queries, "new_latent": new_latent, "latent_cache": latent_cache, "cache_lengths": cache_lengths, "moved_slot": moved_slot}


score_scale = 1.0 / math.sqrt(192.0)

def attend_one(query, own_key, keys, valid):
    scores = jnp.dot(query, keys.T, preferred_element_type=jnp.float32) * score_scale
    own_score = jnp.dot(query, own_key, preferred_element_type=jnp.float32) * score_scale
    live_mask = jnp.arange(keys.shape[0], dtype=jnp.int32)[None, :] < valid
    scores = jnp.where(live_mask, scores, -jnp.inf)
    top_score = jnp.maximum(lax.optimization_barrier(jnp.max(scores, axis=1)), own_score)
    raised = jnp.exp(scores - top_score[:, None])
    raised_own = jnp.exp(own_score - top_score)
    totals = lax.optimization_barrier(jnp.sum(raised, axis=1)) + raised_own
    weights = (raised / totals[:, None]).astype(jnp.bfloat16)
    weight_own = (raised_own / totals).astype(jnp.bfloat16)
    mixed = jnp.dot(weights, keys[:, :NOPE], preferred_element_type=jnp.float32)
    mixed = mixed + weight_own.astype(jnp.float32)[:, None] * own_key[None, :NOPE].astype(jnp.float32)
    return mixed.astype(jnp.bfloat16)

def reference(hidden_rows, group_ids, route_gates, w_gate, w_up, w_down, queries, new_latent, latent_cache, cache_lengths, moved_slot):
    expert_iota = jnp.arange(NG, dtype=jnp.int32)
    chosen = group_ids[:, :, None] == expert_iota[None, None, :]
    coefficient = lax.optimization_barrier(jnp.sum(jnp.where(chosen, route_gates[:, :, None], jnp.zeros((), route_gates.dtype)), axis=1))

    def add_expert(running, expert):
        first_slice = expert * SPLIT
        gate_cols = jnp.transpose(lax.dynamic_slice_in_dim(w_gate, first_slice, SPLIT, 0), (1, 0, 2)).reshape(D, HID)
        up_cols = jnp.transpose(lax.dynamic_slice_in_dim(w_up, first_slice, SPLIT, 0), (1, 0, 2)).reshape(D, HID)
        down_rows = lax.dynamic_slice_in_dim(w_down, first_slice, SPLIT, 0).reshape(HID, D)
        gate_part = jnp.dot(hidden_rows, gate_cols, preferred_element_type=jnp.float32)
        up_part = jnp.dot(hidden_rows, up_cols, preferred_element_type=jnp.float32)
        activated = (jax.nn.silu(gate_part) * up_part).astype(jnp.bfloat16)
        projected = jnp.dot(activated, down_rows, preferred_element_type=jnp.float32)
        scale_col = lax.dynamic_index_in_dim(coefficient, expert, 1, keepdims=True)
        return (running + scale_col * projected, expert)
    moe_total, leftover = lax.scan(add_expert, jnp.zeros((TOKENS, D), jnp.float32), expert_iota)
    slot_iota = jnp.arange(SLOTS, dtype=jnp.int32)
    device_of = slot_iota // REQ_DEV
    within = slot_iota % REQ_DEV
    prior = (device_of + EP_RANKS - 1) % EP_RANKS
    moved_here = within == moved_slot[device_of]
    source = jnp.where(moved_here, prior * REQ_DEV + moved_slot[prior], slot_iota).astype(jnp.int32)

    def one_slot(items):
        query, own_key, anchor = items
        keys = lax.dynamic_index_in_dim(latent_cache, anchor, 0, keepdims=False)
        valid = lax.dynamic_index_in_dim(cache_lengths, anchor, 0, keepdims=False)
        return attend_one(query, own_key, keys, valid)
    attn_out = lax.map(one_slot, (queries, new_latent, source))
    return (moe_total.astype(jnp.bfloat16), attn_out)
```

```python
import functools
import math

import jax
import jax.numpy as jnp
from jax import lax
from jax.experimental import pallas as pl
from jax.experimental.pallas import tpu as pltpu
from jax.sharding import PartitionSpec as P

NOPE = 512
SPLIT = 8
LANES = 128

score_scale = 1.0 / math.sqrt(192.0)


def shifted(value, axis, steps):
    count = lax.axis_size(axis)
    pairs = [(source, (source + steps) % count) for source in range(count)]
    return lax.ppermute(value, axis, pairs)


def attend_body(slots, valid, query_ref, own_ref, cache_ref, out_ref):
    step = pl.program_id(0)
    query = query_ref[0].T
    keys = cache_ref[0]
    own = own_ref[0]
    scores = jnp.dot(query, keys, preferred_element_type=jnp.float32) * score_scale
    own_score = (
        jnp.sum(query.astype(jnp.float32) * own.astype(jnp.float32), axis=1, keepdims=True)
        * score_scale
    )
    places = lax.broadcasted_iota(jnp.int32, scores.shape, 1)
    scores = jnp.where(places < valid[step], scores, -jnp.inf)
    top_score = jnp.maximum(jnp.max(scores, axis=1, keepdims=True), own_score)
    raised = jnp.exp(scores - top_score)
    raised_own = jnp.exp(own_score - top_score)
    totals = jnp.sum(raised, axis=1, keepdims=True) + raised_own
    weights = (raised / totals).astype(jnp.bfloat16)
    weight_own = (raised_own / totals).astype(jnp.bfloat16).astype(jnp.float32)
    mixed = lax.dot_general(
        weights, keys[:NOPE], (((1,), (1,)), ((), ())), preferred_element_type=jnp.float32
    )
    mixed = mixed + weight_own * own[:, :NOPE].astype(jnp.float32)
    out_ref[0] = mixed.astype(jnp.bfloat16)


def attend(slots, valid, query_t, own_keys, cache_t, query_slots, out_count):
    steps = slots.shape[0]
    width, heads = query_t.shape[1:]
    positions = cache_t.shape[2]
    if query_slots:
        place = lambda i, s, v: (s[i], 0, 0)
    else:
        place = lambda i, s, v: (i, 0, 0)
    return pl.pallas_call(
        attend_body,
        out_shape=jax.ShapeDtypeStruct((out_count, heads, NOPE), jnp.bfloat16),
        grid_spec=pltpu.PrefetchScalarGridSpec(
            num_scalar_prefetch=2,
            grid=(steps,),
            in_specs=[
                pl.BlockSpec((1, width, heads), place),
                pl.BlockSpec((1, 1, width), place),
                pl.BlockSpec((1, width, positions), lambda i, s, v: (s[i], 0, 0)),
            ],
            out_specs=pl.BlockSpec((1, heads, NOPE), place),
        ),
        compiler_params=pltpu.CompilerParams(vmem_limit_bytes=24 * 1024 * 1024),
        cost_estimate=pl.CostEstimate(
            flops=2 * steps * heads * positions * (width + NOPE),
            bytes_accessed=2 * steps * width * positions,
            transcendentals=steps * heads * positions,
        ),
    )(slots, valid, query_t, own_keys[:, None, :], cache_t)


def per_device(
    hidden_rows,
    group_ids,
    route_gates,
    w_gate,
    w_up,
    w_down,
    queries,
    new_latent,
    latent_cache,
    cache_lengths,
    moved_slot,
):
    model_width = hidden_rows.shape[1]
    rank_count = lax.axis_size("ep")
    position = lax.axis_index("ep")
    groups = rank_count // SPLIT
    requests = latent_cache.shape[0]

    leaving = lax.dynamic_index_in_dim(moved_slot, position, 0, keepdims=False)
    query_t = jnp.swapaxes(queries, 1, 2)
    cache_t = jnp.swapaxes(latent_cache, 1, 2)
    sent_query = lax.dynamic_index_in_dim(query_t, leaving, 0, keepdims=True)
    sent_own = lax.dynamic_index_in_dim(new_latent, leaving, 0, keepdims=True)
    visiting_query = shifted(sent_query, "ep", -1)
    visiting_own = shifted(sent_own, "ep", -1)

    chosen = group_ids[:, :, None] == jnp.arange(groups, dtype=jnp.int32)[None, None, :]
    coefficient = jnp.sum(jnp.where(chosen, route_gates[:, :, None], 0.0), axis=1)
    high = lax.reduce_precision(coefficient, 8, 7)
    middle = lax.reduce_precision(coefficient - high, 8, 7)
    low = coefficient - high - middle
    tail = jnp.concatenate([high, middle, low], axis=1).astype(jnp.bfloat16)
    spare = -tail.shape[1] % LANES
    rows = jnp.concatenate([hidden_rows, jnp.pad(tail, ((0, 0), (0, spare)))], axis=1)
    all_rows = lax.all_gather(rows, "ep", axis=0, tiled=True)

    own_lengths = lax.dynamic_slice_in_dim(cache_lengths, position * requests, requests)
    staying = jnp.arange(requests - 1, dtype=jnp.int32)
    staying = staying + (staying >= leaving).astype(jnp.int32)
    home_out = attend(
        staying, own_lengths[staying], query_t, new_latent, cache_t, True, requests
    )
    moved = leaving[None]
    away_out = attend(
        moved, own_lengths[moved], visiting_query, visiting_own, cache_t, False, 1
    )
    returned = shifted(away_out, "ep", 1)

    tokens = all_rows[:, :model_width]
    gate_part = jnp.dot(tokens, w_gate[0], preferred_element_type=jnp.float32)
    up_part = jnp.dot(tokens, w_up[0], preferred_element_type=jnp.float32)
    activated = (jax.nn.silu(gate_part) * up_part).astype(jnp.bfloat16)
    projected = jnp.dot(activated, w_down[0], preferred_element_type=jnp.float32)
    parts = all_rows[:, model_width:].astype(jnp.float32)
    lane = jnp.arange(parts.shape[1], dtype=jnp.int32)
    mine = (lane % groups == position // SPLIT) & (lane < 3 * groups)
    scale = jnp.sum(jnp.where(mine[None, :], parts, 0.0), axis=1, keepdims=True)
    partial = (projected * scale).astype(jnp.bfloat16)
    moe_out = lax.psum_scatter(partial, "ep", scatter_dimension=0, tiled=True)
    attn_out = lax.dynamic_update_slice_in_dim(home_out, returned, leaving, 0)
    return (moe_out, attn_out)


def solution(mesh):
    placed = (
        P(("group", "ep"), None),
        P(("group", "ep"), None),
        P(("group", "ep"), None),
        P("ep", None, None),
        P("ep", None, None),
        P("ep", None, None),
        P(("group", "ep"), None, None),
        P(("group", "ep"), None),
        P(("group", "ep"), None, None),
        P("group"),
        P("group"),
    )
    return jax.shard_map(
        per_device,
        mesh=mesh,
        in_specs=placed,
        out_specs=(P(("group", "ep"), None), P(("group", "ep"), None, None)),
        check_vma=False,
    )
```

```python
import functools
import math

import jax
import jax.numpy as jnp
from jax import lax
from jax.experimental import pallas as pl
from jax.experimental.pallas import tpu as pltpu
from jax.sharding import PartitionSpec as P

NOPE = 512
SPLIT = 8
LANES = 128

score_scale = 1.0 / math.sqrt(192.0)


def shifted(value, axis, steps):
    count = lax.axis_size(axis)
    pairs = [(source, (source + steps) % count) for source in range(count)]
    return lax.ppermute(value, axis, pairs)


def rotated(value, axis, steps):
    return shifted(value, axis, 4 * steps)


def swapped(value, axis, bit):
    pairs = [(source, source ^ bit) for source in range(lax.axis_size(axis))]
    return lax.ppermute(value, axis, pairs)


def gathered(rows, axis):
    turns = lax.axis_size(axis) // 4
    columns = [rows] + [rotated(rows, axis, r) for r in range(1, turns)]
    pairs = [jnp.concatenate([own, swapped(own, axis, 2)], axis=0) for own in columns]
    others = [swapped(pair, axis, 1) for pair in pairs]
    return jnp.concatenate(pairs + others, axis=0)


def added(*terms):
    return sum(term.astype(jnp.float32) for term in terms).astype(jnp.bfloat16)


def summed(partial, axis):
    turns = lax.axis_size(axis) // 4
    count = partial.shape[0] // (4 * turns)
    blocks = partial.reshape(2, turns, 2 * count, partial.shape[1])
    terms = []
    for r in list(range(1, turns)) + [0]:
        chip = added(blocks[0, r], swapped(blocks[1, r], axis, 1))
        both = added(chip[:count], swapped(chip[count:], axis, 2))
        terms.append(both if r == 0 else rotated(both, axis, -r))
    return added(*terms)


def attend_body(slots, valid, query_ref, own_ref, cache_ref, out_ref):
    step = pl.program_id(0)
    query = query_ref[0].T
    keys = cache_ref[0]
    own = own_ref[0]
    scores = jnp.dot(query, keys, preferred_element_type=jnp.float32) * score_scale
    own_score = (
        jnp.sum(query.astype(jnp.float32) * own.astype(jnp.float32), axis=1, keepdims=True)
        * score_scale
    )
    places = lax.broadcasted_iota(jnp.int32, scores.shape, 1)
    scores = jnp.where(places < valid[step], scores, -jnp.inf)
    top_score = jnp.maximum(jnp.max(scores, axis=1, keepdims=True), own_score)
    raised = jnp.exp(scores - top_score)
    raised_own = jnp.exp(own_score - top_score)
    totals = jnp.sum(raised, axis=1, keepdims=True) + raised_own
    weights = (raised / totals).astype(jnp.bfloat16)
    weight_own = (raised_own / totals).astype(jnp.bfloat16).astype(jnp.float32)
    mixed = lax.dot_general(
        weights, keys[:NOPE], (((1,), (1,)), ((), ())), preferred_element_type=jnp.float32
    )
    mixed = mixed + weight_own * own[:, :NOPE].astype(jnp.float32)
    out_ref[0] = mixed.astype(jnp.bfloat16)


def attend(slots, valid, query_t, own_keys, cache_t, query_slots, out_count):
    steps = slots.shape[0]
    width, heads = query_t.shape[1:]
    positions = cache_t.shape[2]
    if query_slots:
        place = lambda i, s, v: (s[i], 0, 0)
    else:
        place = lambda i, s, v: (i, 0, 0)
    return pl.pallas_call(
        attend_body,
        out_shape=jax.ShapeDtypeStruct((out_count, heads, NOPE), jnp.bfloat16),
        grid_spec=pltpu.PrefetchScalarGridSpec(
            num_scalar_prefetch=2,
            grid=(steps,),
            in_specs=[
                pl.BlockSpec((1, width, heads), place),
                pl.BlockSpec((1, 1, width), place),
                pl.BlockSpec((1, width, positions), lambda i, s, v: (s[i], 0, 0)),
            ],
            out_specs=pl.BlockSpec((1, heads, NOPE), place),
        ),
        compiler_params=pltpu.CompilerParams(vmem_limit_bytes=24 * 1024 * 1024),
        cost_estimate=pl.CostEstimate(
            flops=2 * steps * heads * positions * (width + NOPE),
            bytes_accessed=2 * steps * width * positions,
            transcendentals=steps * heads * positions,
        ),
    )(slots, valid, query_t, own_keys[:, None, :], cache_t)


def per_device(
    hidden_rows,
    group_ids,
    route_gates,
    w_gate,
    w_up,
    w_down,
    queries,
    new_latent,
    latent_cache,
    cache_lengths,
    moved_slot,
):
    model_width = hidden_rows.shape[1]
    rank_count = lax.axis_size("ep")
    position = lax.axis_index("ep")
    groups = rank_count // SPLIT
    requests = latent_cache.shape[0]

    leaving = lax.dynamic_index_in_dim(moved_slot, position, 0, keepdims=False)
    query_t = jnp.swapaxes(queries, 1, 2)
    cache_t = jnp.swapaxes(latent_cache, 1, 2)
    sent_query = lax.dynamic_index_in_dim(query_t, leaving, 0, keepdims=True)
    sent_own = lax.dynamic_index_in_dim(new_latent, leaving, 0, keepdims=True)
    visiting_query = shifted(sent_query, "ep", -1)
    visiting_own = shifted(sent_own, "ep", -1)

    chosen = group_ids[:, :, None] == jnp.arange(groups, dtype=jnp.int32)[None, None, :]
    coefficient = jnp.sum(jnp.where(chosen, route_gates[:, :, None], 0.0), axis=1)
    high = lax.reduce_precision(coefficient, 8, 7)
    middle = lax.reduce_precision(coefficient - high, 8, 7)
    low = coefficient - high - middle
    tail = jnp.concatenate([high, middle, low], axis=1).astype(jnp.bfloat16)
    spare = -tail.shape[1] % LANES
    rows = jnp.concatenate([hidden_rows, jnp.pad(tail, ((0, 0), (0, spare)))], axis=1)
    all_rows = gathered(rows, "ep")

    own_lengths = lax.dynamic_slice_in_dim(cache_lengths, position * requests, requests)
    staying = jnp.arange(requests - 1, dtype=jnp.int32)
    staying = staying + (staying >= leaving).astype(jnp.int32)
    home_out = attend(
        staying, own_lengths[staying], query_t, new_latent, cache_t, True, requests
    )
    moved = leaving[None]
    away_out = attend(
        moved, own_lengths[moved], visiting_query, visiting_own, cache_t, False, 1
    )
    returned = shifted(away_out, "ep", 1)

    tokens = all_rows[:, :model_width]
    gate_part = jnp.dot(tokens, w_gate[0], preferred_element_type=jnp.float32)
    up_part = jnp.dot(tokens, w_up[0], preferred_element_type=jnp.float32)
    activated = (jax.nn.silu(gate_part) * up_part).astype(jnp.bfloat16)
    projected = jnp.dot(activated, w_down[0], preferred_element_type=jnp.float32)
    parts = all_rows[:, model_width:].astype(jnp.float32)
    lane = jnp.arange(parts.shape[1], dtype=jnp.int32)
    mine = (lane % groups == position // SPLIT) & (lane < 3 * groups)
    scale = jnp.sum(jnp.where(mine[None, :], parts, 0.0), axis=1, keepdims=True)
    partial = (projected * scale).astype(jnp.bfloat16)
    moe_out = summed(partial, "ep")
    attn_out = lax.dynamic_update_slice_in_dim(home_out, returned, leaving, 0)
    return (moe_out, attn_out)


def solution(mesh):
    placed = (
        P(("group", "ep"), None),
        P(("group", "ep"), None),
        P(("group", "ep"), None),
        P("ep", None, None),
        P("ep", None, None),
        P("ep", None, None),
        P(("group", "ep"), None, None),
        P(("group", "ep"), None),
        P(("group", "ep"), None, None),
        P("group"),
        P("group"),
    )
    return jax.shard_map(
        per_device,
        mesh=mesh,
        in_specs=placed,
        out_specs=(P(("group", "ep"), None), P(("group", "ep"), None, None)),
        check_vma=False,
    )
```

```python
import functools
import math

import jax
import jax.numpy as jnp
from jax import lax
from jax.experimental import pallas as pl
from jax.experimental.pallas import tpu as pltpu
from jax.sharding import PartitionSpec as P

NOPE = 512
SPLIT = 8
LANES = 128
CHUNK = 1024
MIB = 1024 * 1024

score_scale = 1.0 / math.sqrt(192.0)

WHOLE = pl.BlockSpec(memory_space=pltpu.VMEM)
SCALARS = pl.BlockSpec(memory_space=pltpu.SMEM)
APART = pl.BlockSpec(memory_space=pl.ANY)
MAIN = pl.BlockSpec(memory_space=pltpu.HBM)


def shifted(value, axis, steps):
    count = lax.axis_size(axis)
    pairs = [(source, (source + steps) % count) for source in range(count)]
    return lax.ppermute(value, axis, pairs)


def rotated(value, axis, steps):
    return shifted(value, axis, 4 * steps)


def swapped(value, axis, bit):
    pairs = [(source, source ^ bit) for source in range(lax.axis_size(axis))]
    return lax.ppermute(value, axis, pairs)


def prepare_body(groups, place, moved, hidden, ids, gates, query, own, rows, payload, sem):
    leaving = moved[place[0]]
    width = query.shape[1]
    copy = pltpu.make_async_copy(query.at[leaving], payload.at[pl.ds(0, width)], sem)
    copy.start()
    tokens, model_width = hidden.shape
    rows[:, :model_width] = hidden[...]
    lane = lax.broadcasted_iota(jnp.int32, (tokens, rows.shape[1] - model_width), 1)
    part = (lane >= groups).astype(jnp.int32) + (lane >= 2 * groups).astype(jnp.int32)
    group = lane - groups * part
    coefficient = jnp.zeros(lane.shape, jnp.float32)
    for k in range(ids.shape[1]):
        coefficient += jnp.where(ids[:, k : k + 1] == group, gates[:, k : k + 1], 0.0)
    high = coefficient.astype(jnp.bfloat16).astype(jnp.float32)
    middle = (coefficient - high).astype(jnp.bfloat16).astype(jnp.float32)
    low = coefficient - high - middle
    pieces = jnp.where(part == 0, high, jnp.where(part == 1, middle, low))
    rows[:, model_width:] = jnp.where(lane < 3 * groups, pieces, 0.0).astype(jnp.bfloat16)
    slots = lax.broadcasted_iota(jnp.int32, own.shape, 0)
    latent = jnp.sum(
        jnp.where(slots == leaving, own[...].astype(jnp.float32), 0.0), axis=0, keepdims=True
    )
    extra = payload.shape[0] - width
    row = lax.broadcasted_iota(jnp.int32, (extra, LANES), 0)
    block = jnp.zeros((extra, LANES), jnp.float32)
    latent = jnp.concatenate([latent, jnp.zeros((1, -width % LANES), jnp.float32)], axis=1)
    for r in range(latent.shape[1] // LANES):
        block = jnp.where(row == r, latent[:, r * LANES : (r + 1) * LANES], block)
    payload[width:, :] = block.astype(jnp.bfloat16)
    copy.wait()


def prepare(place, moved, hidden, ids, gates, query_t, own, groups):
    tokens, model_width = hidden.shape
    requests, width, heads = query_t.shape
    tail = -(-3 * groups // LANES) * LANES
    extra = -(-width // (16 * LANES)) * 16
    return pl.pallas_call(
        functools.partial(prepare_body, groups),
        out_shape=[
            jax.ShapeDtypeStruct((tokens, model_width + tail), jnp.bfloat16),
            jax.ShapeDtypeStruct((width + extra, heads), jnp.bfloat16),
        ],
        in_specs=[SCALARS, SCALARS, WHOLE, WHOLE, WHOLE, MAIN, WHOLE],
        out_specs=[WHOLE, WHOLE],
        scratch_shapes=[pltpu.SemaphoreType.DMA],
        compiler_params=pltpu.CompilerParams(vmem_limit_bytes=8 * MIB),
    )(place, moved, hidden, ids, gates, query_t, own)


def attend_body(place, moved, lengths, query, own, payload, cache, after, home, away, keys, sems):
    requests, width, positions = cache.shape
    copies = [
        pltpu.make_async_copy(cache.at[j], keys.at[j], sems.at[j]) for j in range(requests)
    ]
    for copy in copies:
        copy.start()
    leaving = moved[place[0]]
    tail = payload[width:, :].astype(jnp.float32)
    visiting = jnp.concatenate([tail[r : r + 1] for r in range(-(-width // LANES))], axis=1)
    visiting = visiting[:, :width]
    for j in range(requests):
        here = leaving == j
        asked = jnp.where(here, payload[:width, :], query[j]).T
        latent = jnp.where(here, visiting, own[j : j + 1, :].astype(jnp.float32))
        copies[j].wait()
        scores = jnp.dot(asked, keys[j], preferred_element_type=jnp.float32) * score_scale
        own_score = (
            jnp.sum(asked.astype(jnp.float32) * latent, axis=1, keepdims=True) * score_scale
        )
        live = lax.broadcasted_iota(jnp.int32, scores.shape, 1)
        scores = jnp.where(live < lengths[place[0] * requests + j], scores, -jnp.inf)
        top_score = jnp.maximum(jnp.max(scores, axis=1, keepdims=True), own_score)
        raised = jnp.exp(scores - top_score)
        raised_own = jnp.exp(own_score - top_score)
        share = 1.0 / (jnp.sum(raised, axis=1, keepdims=True) + raised_own)
        weights = (raised * share).astype(jnp.bfloat16)
        weight_own = (raised_own * share).astype(jnp.bfloat16).astype(jnp.float32)
        mixed = lax.dot_general(
            weights,
            keys[j, :NOPE],
            (((1,), (1,)), ((), ())),
            preferred_element_type=jnp.float32,
        )
        result = (mixed + weight_own * latent[:, :NOPE]).astype(jnp.bfloat16)
        home[j] = result

        @pl.when(here)
        def _():
            away[...] = result


def attend(place, moved, lengths, query_t, own, payload, cache_t, after):
    requests, width, heads = query_t.shape
    positions = cache_t.shape[2]
    return pl.pallas_call(
        attend_body,
        out_shape=[
            jax.ShapeDtypeStruct((requests, heads, NOPE), jnp.bfloat16),
            jax.ShapeDtypeStruct((heads, NOPE), jnp.bfloat16),
        ],
        in_specs=[SCALARS, SCALARS, SCALARS, WHOLE, WHOLE, WHOLE, MAIN, APART],
        out_specs=[WHOLE, WHOLE],
        scratch_shapes=[
            pltpu.VMEM((requests, width, positions), jnp.bfloat16),
            pltpu.SemaphoreType.DMA((requests,)),
        ],
        compiler_params=pltpu.CompilerParams(vmem_limit_bytes=24 * MIB),
        cost_estimate=pl.CostEstimate(
            flops=2 * requests * heads * positions * (width + NOPE),
            bytes_accessed=2 * requests * width * positions,
            transcendentals=requests * heads * positions,
        ),
    )(place, moved, lengths, query_t, own, payload, cache_t, after)


def expert_body(count, groups, place, w_gate, w_up, w_down, after, *refs):
    blocks, outs = refs[:count], refs[count:-4]
    first, second, sems, last_sem = refs[-4:]
    keeps, sends = outs[: count // 2], outs[count // 2 :]
    model_width = w_gate.shape[1]
    hidden = w_gate.shape[2]
    steps = model_width // CHUNK
    copies = []
    for s in range(steps):
        at = pl.ds(s * CHUNK, CHUNK)
        copies.append(
            [
                pltpu.make_async_copy(w_gate.at[0, at], first.at[at, :hidden], sems.at[2 * s]),
                pltpu.make_async_copy(w_up.at[0, at], first.at[at, hidden:], sems.at[2 * s + 1]),
            ]
        )
    for pair in copies:
        for copy in pair:
            copy.start()
    last = pltpu.make_async_copy(w_down.at[0], second, last_sem)
    last.start()

    def joined(at):
        return jnp.concatenate([block[:, at].astype(jnp.float32) for block in blocks], axis=0)

    total = None
    for s in range(steps):
        at = slice(s * CHUNK, (s + 1) * CHUNK)
        rows = joined(at).astype(jnp.bfloat16)
        for copy in copies[s]:
            copy.wait()
        term = jnp.dot(rows, first[at, :], preferred_element_type=jnp.float32)
        total = term if total is None else total + term
    gate, up = total[:, :hidden], total[:, hidden:]
    activated = (gate / (1.0 + jnp.exp(-gate)) * up).astype(jnp.bfloat16)
    parts = joined(slice(model_width, blocks[0].shape[1]))
    lane = lax.broadcasted_iota(jnp.int32, parts.shape, 1)
    mine = place[0] // SPLIT
    picked = (lane == mine) | (lane == mine + groups) | (lane == mine + 2 * groups)
    scale = jnp.sum(jnp.where(picked, parts, 0.0), axis=1, keepdims=True)
    tokens = blocks[0].shape[0]
    half = count // 2 * tokens
    last.wait()
    for s in range(steps):
        at = slice(s * CHUNK, (s + 1) * CHUNK)
        part = jnp.dot(activated, second[:, at], preferred_element_type=jnp.float32) * scale
        for i, send in enumerate(sends):
            low = half + 2 * tokens * i
            send[:, at] = part[low : low + 2 * tokens].astype(jnp.bfloat16)
        for i, keep in enumerate(keeps):
            keep[:, at] = part[tokens * i : tokens * (i + 1)].astype(jnp.bfloat16)


def expert(place, w_gate, w_up, w_down, after, blocks, groups):
    count = len(blocks)
    tokens = blocks[0].shape[0]
    _, model_width, hidden = w_gate.shape
    keep = jax.ShapeDtypeStruct((tokens, model_width), jnp.bfloat16)
    send = jax.ShapeDtypeStruct((2 * tokens, model_width), jnp.bfloat16)
    outs = pl.pallas_call(
        functools.partial(expert_body, count, groups),
        out_shape=[keep] * (count // 2) + [send] * (count // 4),
        in_specs=[SCALARS, MAIN, MAIN, MAIN, APART] + [WHOLE] * count,
        out_specs=[WHOLE] * (count // 2 + count // 4),
        scratch_shapes=[
            pltpu.VMEM((model_width, 2 * hidden), jnp.bfloat16),
            pltpu.VMEM((hidden, model_width), jnp.bfloat16),
            pltpu.SemaphoreType.DMA((2 * (model_width // CHUNK),)),
            pltpu.SemaphoreType.DMA,
        ],
        compiler_params=pltpu.CompilerParams(vmem_limit_bytes=40 * MIB),
        cost_estimate=pl.CostEstimate(
            flops=6 * count * tokens * model_width * hidden,
            bytes_accessed=6 * model_width * hidden,
            transcendentals=count * tokens * hidden,
        ),
    )(place, w_gate, w_up, w_down, after, *blocks)
    return outs[: count // 2], outs[count // 2 :]


def added(*terms):
    return sum(term.astype(jnp.float32) for term in terms).astype(jnp.bfloat16)


def per_device(
    hidden_rows,
    group_ids,
    route_gates,
    w_gate,
    w_up,
    w_down,
    queries,
    new_latent,
    latent_cache,
    cache_lengths,
    moved_slot,
):
    axis = "ep"
    ranks = lax.axis_size(axis)
    turns = ranks // 4
    groups = ranks // SPLIT
    tokens = hidden_rows.shape[0]
    position = lax.axis_index(axis)
    place = position[None]
    query_t = jnp.swapaxes(queries, 1, 2)
    cache_t = jnp.swapaxes(latent_cache, 1, 2)

    rows, payload = prepare(
        place, moved_slot, hidden_rows, group_ids, route_gates, query_t, new_latent, groups
    )

    columns = [rows] + [rotated(rows, axis, r) for r in range(1, turns)]
    across = [swapped(own, axis, 2) for own in columns]
    near = [block for pair in zip(columns, across) for block in pair]
    blocks = near + [swapped(block, axis, 1) for block in near]

    visiting = shifted(payload, axis, -1)
    home, away = attend(
        place, moved_slot, cache_lengths, query_t, new_latent, visiting, cache_t, columns[-1]
    )
    returned = shifted(away, axis, 1)

    keeps, sends = expert(place, w_gate, w_up, w_down, away, blocks, groups)
    terms = []
    for r in list(range(1, turns)) + [0]:
        chip = swapped(sends[r], axis, 1)
        crossed = swapped(added(keeps[2 * r + 1], chip[tokens:]), axis, 2)
        both = [keeps[2 * r], chip[:tokens], crossed]
        terms += both if r == 0 else [rotated(added(*both), axis, -r)]
    moe_out = added(*terms)
    leaving = lax.dynamic_index_in_dim(moved_slot, position, 0, keepdims=False)
    attn_out = lax.dynamic_update_slice_in_dim(home, returned[None], leaving, 0)
    return (moe_out, attn_out)


def solution(mesh):
    placed = (
        P(("group", "ep"), None),
        P(("group", "ep"), None),
        P(("group", "ep"), None),
        P("ep", None, None),
        P("ep", None, None),
        P("ep", None, None),
        P(("group", "ep"), None, None),
        P(("group", "ep"), None),
        P(("group", "ep"), None, None),
        P("group"),
        P("group"),
    )
    return jax.shard_map(
        per_device,
        mesh=mesh,
        in_specs=placed,
        out_specs=(P(("group", "ep"), None), P(("group", "ep"), None, None)),
        check_vma=False,
    )
```

```python
import functools
import math

import jax
import jax.numpy as jnp
from jax import lax
from jax.experimental import pallas as pl
from jax.experimental.pallas import tpu as pltpu
from jax.sharding import PartitionSpec as P

NOPE = 512
SPLIT = 8
LANES = 128
CHUNK = 1024
MIB = 1024 * 1024

score_scale = 1.0 / math.sqrt(192.0)

WHOLE = pl.BlockSpec(memory_space=pltpu.VMEM)
SCALARS = pl.BlockSpec(memory_space=pltpu.SMEM)
MAIN = pl.BlockSpec(memory_space=pltpu.HBM)


def shifted(value, axis, steps):
    count = lax.axis_size(axis)
    pairs = [(source, (source + steps) % count) for source in range(count)]
    return lax.ppermute(value, axis, pairs)


def rotated(value, axis, steps):
    return shifted(value, axis, 4 * steps)


def swapped(value, axis, bit):
    pairs = [(source, source ^ bit) for source in range(lax.axis_size(axis))]
    return lax.ppermute(value, axis, pairs)


def prepare_body(groups, place, moved, hidden, ids, gates, query, own, rows, payload, *scratch):
    moves, sems = scratch
    tokens, model_width = hidden.shape
    width = query.shape[1]
    fetch = pltpu.make_async_copy(moved, moves, sems.at[0])
    fetch.start()
    fetch.wait()
    leaving = moves[place[0]]
    copy = pltpu.make_async_copy(query.at[leaving], payload.at[pl.ds(0, width)], sems.at[1])
    copy.start()
    rows[:, :model_width] = hidden[...]
    chosen, weight = ids[...].T, gates[...].T
    lane = lax.broadcasted_iota(jnp.int32, (tokens, rows.shape[1] - model_width), 1)
    part = (lane >= groups).astype(jnp.int32) + (lane >= 2 * groups).astype(jnp.int32)
    group = lane - groups * part
    coefficient = jnp.zeros(lane.shape, jnp.float32)
    for k in range(chosen.shape[1]):
        coefficient += jnp.where(chosen[:, k : k + 1] == group, weight[:, k : k + 1], 0.0)
    high = coefficient.astype(jnp.bfloat16).astype(jnp.float32)
    middle = (coefficient - high).astype(jnp.bfloat16).astype(jnp.float32)
    low = coefficient - high - middle
    pieces = jnp.where(part == 0, high, jnp.where(part == 1, middle, low))
    rows[:, model_width:] = jnp.where(lane < 3 * groups, pieces, 0.0).astype(jnp.bfloat16)
    slots = lax.broadcasted_iota(jnp.int32, own.shape, 0)
    latent = jnp.sum(
        jnp.where(slots == leaving, own[...].astype(jnp.float32), 0.0), axis=0, keepdims=True
    )
    extra = payload.shape[0] - width
    row = lax.broadcasted_iota(jnp.int32, (extra, LANES), 0)
    block = jnp.zeros((extra, LANES), jnp.float32)
    latent = jnp.concatenate([latent, jnp.zeros((1, -width % LANES), jnp.float32)], axis=1)
    for r in range(latent.shape[1] // LANES):
        block = jnp.where(row == r, latent[:, r * LANES : (r + 1) * LANES], block)
    payload[width:, :] = block.astype(jnp.bfloat16)
    copy.wait()


def prepare(place, moved, hidden, ids_t, gates_t, query_t, own, groups):
    tokens, model_width = hidden.shape
    requests, width, heads = query_t.shape
    tail = -(-3 * groups // LANES) * LANES
    extra = -(-width // (16 * LANES)) * 16
    return pl.pallas_call(
        functools.partial(prepare_body, groups),
        out_shape=[
            jax.ShapeDtypeStruct((tokens, model_width + tail), jnp.bfloat16),
            jax.ShapeDtypeStruct((width + extra, heads), jnp.bfloat16),
        ],
        in_specs=[SCALARS, MAIN, WHOLE, WHOLE, WHOLE, MAIN, WHOLE],
        out_specs=[WHOLE, WHOLE],
        scratch_shapes=[
            pltpu.SMEM(moved.shape, moved.dtype),
            pltpu.SemaphoreType.DMA((2,)),
        ],
        compiler_params=pltpu.CompilerParams(vmem_limit_bytes=60 * MIB),
        cost_estimate=pl.CostEstimate(flops=0, bytes_accessed=0, transcendentals=0),
    )(place, moved, hidden, ids_t, gates_t, query_t, own)


def attend_body(place, moved, lengths, query, own, payload, cache, home, away, mark, *scratch):
    moves, extents, asking, keys, sems = scratch
    requests, width, positions = cache.shape
    fetches = [
        pltpu.make_async_copy(moved, moves, sems.at[0]),
        pltpu.make_async_copy(lengths, extents, sems.at[1]),
        pltpu.make_async_copy(query, asking, sems.at[2]),
    ]
    copies = [
        pltpu.make_async_copy(cache.at[j], keys.at[j], sems.at[3 + j]) for j in range(requests)
    ]
    for fetch in fetches + copies:
        fetch.start()
    for fetch in fetches:
        fetch.wait()
    leaving = moves[place[0]]
    mark[...] = jnp.full(mark.shape, leaving, jnp.int32)
    tail = payload[width:, :].astype(jnp.float32)
    visiting = jnp.concatenate([tail[r : r + 1] for r in range(-(-width // LANES))], axis=1)
    visiting = visiting[:, :width]
    for j in range(requests):
        here = leaving == j
        asked = jnp.where(here, payload[:width, :], asking[j]).T
        latent = jnp.where(here, visiting, own[j : j + 1, :].astype(jnp.float32))
        copies[j].wait()
        scores = jnp.dot(asked, keys[j], preferred_element_type=jnp.float32) * score_scale
        own_score = (
            jnp.sum(asked.astype(jnp.float32) * latent, axis=1, keepdims=True) * score_scale
        )
        live = lax.broadcasted_iota(jnp.int32, scores.shape, 1)
        scores = jnp.where(live < extents[place[0] * requests + j], scores, -jnp.inf)
        top_score = jnp.maximum(jnp.max(scores, axis=1, keepdims=True), own_score)
        raised = jnp.exp(scores - top_score)
        raised_own = jnp.exp(own_score - top_score)
        share = 1.0 / (jnp.sum(raised, axis=1, keepdims=True) + raised_own)
        weights = (raised * share).astype(jnp.bfloat16)
        weight_own = (raised_own * share).astype(jnp.bfloat16).astype(jnp.float32)
        mixed = lax.dot_general(
            weights,
            keys[j, :NOPE],
            (((1,), (1,)), ((), ())),
            preferred_element_type=jnp.float32,
        )
        result = (mixed + weight_own * latent[:, :NOPE]).astype(jnp.bfloat16)
        home[j] = result

        @pl.when(here)
        def _():
            away[...] = result


def attend(place, moved, lengths, query_t, own, payload, cache_t):
    requests, width, heads = query_t.shape
    positions = cache_t.shape[2]
    return pl.pallas_call(
        attend_body,
        out_shape=[
            jax.ShapeDtypeStruct((requests, heads, NOPE), jnp.bfloat16),
            jax.ShapeDtypeStruct((heads, NOPE), jnp.bfloat16),
            jax.ShapeDtypeStruct((8, LANES), jnp.int32),
        ],
        in_specs=[SCALARS, MAIN, MAIN, MAIN, WHOLE, WHOLE, MAIN],
        out_specs=[WHOLE, WHOLE, WHOLE],
        scratch_shapes=[
            pltpu.SMEM(moved.shape, moved.dtype),
            pltpu.SMEM(lengths.shape, lengths.dtype),
            pltpu.VMEM(query_t.shape, query_t.dtype),
            pltpu.VMEM(cache_t.shape, cache_t.dtype),
            pltpu.SemaphoreType.DMA((3 + requests,)),
        ],
        compiler_params=pltpu.CompilerParams(vmem_limit_bytes=58 * MIB),
        cost_estimate=pl.CostEstimate(
            flops=2 * requests * heads * positions * (width + NOPE),
            bytes_accessed=0,
            transcendentals=0,
        ),
    )(place, moved, lengths, query_t, own, payload, cache_t)


def expert_body(count, groups, place, w_gate, w_up, w_down, *refs):
    blocks, outs = refs[:count], refs[count:-4]
    first, second, sems, last_sem = refs[-4:]
    keeps, sends = outs[: count // 2], outs[count // 2 :]
    model_width = w_gate.shape[1]
    hidden = w_gate.shape[2]
    steps = model_width // CHUNK
    copies = []
    for s in range(steps):
        at = pl.ds(s * CHUNK, CHUNK)
        copies.append(
            [
                pltpu.make_async_copy(w_gate.at[0, at], first.at[at, :hidden], sems.at[2 * s]),
                pltpu.make_async_copy(w_up.at[0, at], first.at[at, hidden:], sems.at[2 * s + 1]),
            ]
        )
    for pair in copies:
        for copy in pair:
            copy.start()
    last = pltpu.make_async_copy(w_down.at[0], second, last_sem)
    last.start()

    def joined(at):
        return jnp.concatenate([block[:, at].astype(jnp.float32) for block in blocks], axis=0)

    total = None
    for s in range(steps):
        at = slice(s * CHUNK, (s + 1) * CHUNK)
        rows = joined(at).astype(jnp.bfloat16)
        for copy in copies[s]:
            copy.wait()
        term = jnp.dot(rows, first[at, :], preferred_element_type=jnp.float32)
        total = term if total is None else total + term
    gate, up = total[:, :hidden], total[:, hidden:]
    activated = (gate / (1.0 + jnp.exp(-gate)) * up).astype(jnp.bfloat16)
    parts = joined(slice(model_width, blocks[0].shape[1]))
    lane = lax.broadcasted_iota(jnp.int32, parts.shape, 1)
    mine = place[0] // SPLIT
    picked = (lane == mine) | (lane == mine + groups) | (lane == mine + 2 * groups)
    scale = jnp.sum(jnp.where(picked, parts, 0.0), axis=1, keepdims=True)
    tokens = blocks[0].shape[0]
    half = count // 2 * tokens
    last.wait()
    for s in range(steps):
        at = slice(s * CHUNK, (s + 1) * CHUNK)
        part = jnp.dot(activated, second[:, at], preferred_element_type=jnp.float32) * scale
        low = half
        for send in sends:
            send[:, at] = part[low : low + send.shape[0]].astype(jnp.bfloat16)
            low += send.shape[0]
        for i, keep in enumerate(keeps):
            keep[:, at] = part[tokens * i : tokens * (i + 1)].astype(jnp.bfloat16)


def expert(place, w_gate, w_up, w_down, blocks, groups):
    count = len(blocks)
    tokens = blocks[0].shape[0]
    _, model_width, hidden = w_gate.shape
    keep = jax.ShapeDtypeStruct((tokens, model_width), jnp.bfloat16)
    sends = [
        jax.ShapeDtypeStruct((size * tokens, model_width), jnp.bfloat16)
        for size in (2, count // 2 - 2)
    ]
    outs = pl.pallas_call(
        functools.partial(expert_body, count, groups),
        out_shape=[keep] * (count // 2) + sends,
        in_specs=[SCALARS, MAIN, MAIN, MAIN] + [WHOLE] * count,
        out_specs=[WHOLE] * (count // 2 + 2),
        scratch_shapes=[
            pltpu.VMEM((model_width, 2 * hidden), jnp.bfloat16),
            pltpu.VMEM((hidden, model_width), jnp.bfloat16),
            pltpu.SemaphoreType.DMA((2 * (model_width // CHUNK),)),
            pltpu.SemaphoreType.DMA,
        ],
        compiler_params=pltpu.CompilerParams(vmem_limit_bytes=40 * MIB),
        cost_estimate=pl.CostEstimate(
            flops=6 * count * tokens * model_width * hidden,
            bytes_accessed=0,
            transcendentals=0,
        ),
    )(place, w_gate, w_up, w_down, *blocks)
    return outs[: count // 2], outs[count // 2 :]


def added(*terms):
    return sum(term.astype(jnp.float32) for term in terms).astype(jnp.bfloat16)


def per_device(
    hidden_rows,
    group_ids,
    route_gates,
    w_gate,
    w_up,
    w_down,
    queries,
    new_latent,
    latent_cache,
    cache_lengths,
    moved_slot,
):
    axis = "ep"
    ranks = lax.axis_size(axis)
    turns = ranks // 4
    groups = ranks // SPLIT
    tokens = hidden_rows.shape[0]
    position = lax.axis_index(axis)
    place = position[None]
    query_t = jnp.swapaxes(queries, 1, 2)
    cache_t = jnp.swapaxes(latent_cache, 1, 2)

    rows, payload = prepare(
        place, moved_slot, hidden_rows, group_ids.T, route_gates.T, query_t, new_latent, groups
    )

    visiting = shifted(payload, axis, -1)
    columns = {r: rotated(rows, axis, r) for r in range(1, turns) if r != 2}
    across = {0: swapped(rows, axis, 2)}

    home, away, mark = attend(
        place, moved_slot, cache_lengths, query_t, new_latent, visiting, cache_t
    )
    columns, across, away = lax.optimization_barrier((columns, across, away))
    columns[0] = rows
    returned = shifted(away, axis, 1)

    order = list(range(turns))
    if turns > 2:
        columns[2] = rotated(columns[1], axis, 1)
        order.remove(2)
        order = [2] + order
    for r in order[1:] + order[:1]:
        if r:
            across[r] = swapped(columns[r], axis, 2)
    near = [block for r in order for block in (columns[r], across[r])]
    blocks = near + [swapped(block, axis, 1) for block in near]

    keeps, sends = expert(place, w_gate, w_up, w_down, blocks, groups)
    first, rest = (swapped(send, axis, 1) for send in sends)

    def chip(i, m):
        if i == 0:
            return [keeps[m], first[m * tokens : (m + 1) * tokens]]
        low = (2 * (i - 1) + m) * tokens
        return [keeps[2 * i + m], rest[low : low + tokens]]

    crossed = [swapped(added(*chip(i, 1)), axis, 2) for i in range(turns)]
    sums = {r: chip(i, 0) + [crossed[i]] for i, r in enumerate(order)}
    if turns > 2:
        sums[1] = sums[1] + [rotated(added(*sums.pop(2)), axis, -1)]
    terms = sums.pop(0)
    for r in sums:
        terms = terms + [rotated(added(*sums[r]), axis, -r)]
    moe_out = added(*terms)
    slots = jnp.arange(home.shape[0], dtype=jnp.int32)[:, None, None]
    attn_out = jnp.where(slots == mark[:1, :1][None], returned[None], home)
    return (moe_out, attn_out)


def solution(mesh):
    placed = (
        P(("group", "ep"), None),
        P(("group", "ep"), None),
        P(("group", "ep"), None),
        P("ep", None, None),
        P("ep", None, None),
        P("ep", None, None),
        P(("group", "ep"), None, None),
        P(("group", "ep"), None),
        P(("group", "ep"), None, None),
        P("group"),
        P("group"),
    )
    return jax.shard_map(
        per_device,
        mesh=mesh,
        in_specs=placed,
        out_specs=(P(("group", "ep"), None), P(("group", "ep"), None, None)),
        check_vma=False,
    )
```

```python
import functools
import math

import jax
import jax.numpy as jnp
from jax import lax
from jax.experimental import pallas as pl
from jax.experimental.pallas import tpu as pltpu
from jax.sharding import PartitionSpec as P

NOPE = 512
SPLIT = 8
LANES = 128
CHUNK = 1024
MIB = 1024 * 1024

score_scale = 1.0 / math.sqrt(192.0)

WHOLE = pl.BlockSpec(memory_space=pltpu.VMEM)
SCALARS = pl.BlockSpec(memory_space=pltpu.SMEM)
MAIN = pl.BlockSpec(memory_space=pltpu.HBM)


def shifted(value, axis, steps):
    count = lax.axis_size(axis)
    pairs = [(source, (source + steps) % count) for source in range(count)]
    return lax.ppermute(value, axis, pairs)


def rotated(value, axis, steps):
    return shifted(value, axis, 4 * steps)


def swapped(value, axis, bit):
    pairs = [(source, source ^ bit) for source in range(lax.axis_size(axis))]
    return lax.ppermute(value, axis, pairs)


def prepare_body(groups, place, moved, hidden, ids, gates, query, own, rows, payload):
    tokens, model_width = hidden.shape
    requests, width, _ = query.shape
    rows[:, :model_width] = hidden[...]
    chosen, weight = ids[...].T, gates[...].T
    lane = lax.broadcasted_iota(jnp.int32, (tokens, rows.shape[1] - model_width), 1)
    part = (lane >= groups).astype(jnp.int32) + (lane >= 2 * groups).astype(jnp.int32)
    group = lane - groups * part
    coefficient = jnp.zeros(lane.shape, jnp.float32)
    for k in range(chosen.shape[1]):
        coefficient += jnp.where(chosen[:, k : k + 1] == group, weight[:, k : k + 1], 0.0)
    high = coefficient.astype(jnp.bfloat16).astype(jnp.float32)
    middle = (coefficient - high).astype(jnp.bfloat16).astype(jnp.float32)
    low = coefficient - high - middle
    pieces = jnp.where(part == 0, high, jnp.where(part == 1, middle, low))
    rows[:, model_width:] = jnp.where(lane < 3 * groups, pieces, 0.0).astype(jnp.bfloat16)
    leaving = moved[place[0]]
    payload[:width, :] = query[leaving]
    slots = lax.broadcasted_iota(jnp.int32, own.shape, 0)
    latent = jnp.sum(
        jnp.where(slots == leaving, own[...].astype(jnp.float32), 0.0), axis=0, keepdims=True
    )
    extra = payload.shape[0] - width
    row = lax.broadcasted_iota(jnp.int32, (extra, LANES), 0)
    block = jnp.zeros((extra, LANES), jnp.float32)
    latent = jnp.concatenate([latent, jnp.zeros((1, -width % LANES), jnp.float32)], axis=1)
    for r in range(latent.shape[1] // LANES):
        block = jnp.where(row == r, latent[:, r * LANES : (r + 1) * LANES], block)
    payload[width:, :] = block.astype(jnp.bfloat16)


def prepare(place, moved, hidden, ids_t, gates_t, query_t, own, groups):
    tokens, model_width = hidden.shape
    requests, width, heads = query_t.shape
    tail = -(-3 * groups // LANES) * LANES
    extra = -(-width // (16 * LANES)) * 16
    return pl.pallas_call(
        functools.partial(prepare_body, groups),
        out_shape=[
            jax.ShapeDtypeStruct((tokens, model_width + tail), jnp.bfloat16),
            jax.ShapeDtypeStruct((width + extra, heads), jnp.bfloat16),
        ],
        in_specs=[SCALARS, SCALARS] + [WHOLE] * 5,
        out_specs=[WHOLE, WHOLE],
        compiler_params=pltpu.CompilerParams(vmem_limit_bytes=60 * MIB),
        cost_estimate=pl.CostEstimate(flops=0, bytes_accessed=0, transcendentals=0),
    )(place, moved, hidden, ids_t, gates_t, query_t, own)


def attend_body(place, moved, lengths, query, own, payload, cache, home, away, mark, *scratch):
    moves, extents, asking, keys, sems = scratch
    requests, width, positions = cache.shape
    fetches = [
        pltpu.make_async_copy(moved, moves, sems.at[0]),
        pltpu.make_async_copy(lengths, extents, sems.at[1]),
        pltpu.make_async_copy(query, asking, sems.at[2]),
    ]
    copies = [
        pltpu.make_async_copy(cache.at[j], keys.at[j], sems.at[3 + j]) for j in range(requests)
    ]
    for fetch in fetches + copies:
        fetch.start()
    for fetch in fetches:
        fetch.wait()
    leaving = moves[place[0]]
    mark[...] = jnp.full(mark.shape, leaving, jnp.int32)
    tail = payload[width:, :].astype(jnp.float32)
    visiting = jnp.concatenate([tail[r : r + 1] for r in range(-(-width // LANES))], axis=1)
    visiting = visiting[:, :width]
    for j in range(requests):
        here = leaving == j
        asked = jnp.where(here, payload[:width, :], asking[j]).T
        latent = jnp.where(here, visiting, own[j : j + 1, :].astype(jnp.float32))
        copies[j].wait()
        scores = jnp.dot(asked, keys[j], preferred_element_type=jnp.float32) * score_scale
        own_score = (
            jnp.sum(asked.astype(jnp.float32) * latent, axis=1, keepdims=True) * score_scale
        )
        live = lax.broadcasted_iota(jnp.int32, scores.shape, 1)
        scores = jnp.where(live < extents[place[0] * requests + j], scores, -jnp.inf)
        top_score = jnp.maximum(jnp.max(scores, axis=1, keepdims=True), own_score)
        raised = jnp.exp(scores - top_score)
        raised_own = jnp.exp(own_score - top_score)
        share = 1.0 / (jnp.sum(raised, axis=1, keepdims=True) + raised_own)
        weights = (raised * share).astype(jnp.bfloat16)
        weight_own = (raised_own * share).astype(jnp.bfloat16).astype(jnp.float32)
        mixed = lax.dot_general(
            weights,
            keys[j, :NOPE],
            (((1,), (1,)), ((), ())),
            preferred_element_type=jnp.float32,
        )
        result = (mixed + weight_own * latent[:, :NOPE]).astype(jnp.bfloat16)
        home[j] = result

        @pl.when(here)
        def _():
            away[...] = result


def attend(place, moved, lengths, query_t, own, payload, cache_t):
    requests, width, heads = query_t.shape
    positions = cache_t.shape[2]
    return pl.pallas_call(
        attend_body,
        out_shape=[
            jax.ShapeDtypeStruct((requests, heads, NOPE), jnp.bfloat16),
            jax.ShapeDtypeStruct((heads, NOPE), jnp.bfloat16),
            jax.ShapeDtypeStruct((8, LANES), jnp.int32),
        ],
        in_specs=[SCALARS, MAIN, MAIN, MAIN, WHOLE, WHOLE, MAIN],
        out_specs=[WHOLE, WHOLE, WHOLE],
        scratch_shapes=[
            pltpu.SMEM(moved.shape, moved.dtype),
            pltpu.SMEM(lengths.shape, lengths.dtype),
            pltpu.VMEM(query_t.shape, query_t.dtype),
            pltpu.VMEM(cache_t.shape, cache_t.dtype),
            pltpu.SemaphoreType.DMA((3 + requests,)),
        ],
        compiler_params=pltpu.CompilerParams(vmem_limit_bytes=58 * MIB),
        cost_estimate=pl.CostEstimate(
            flops=2 * requests * heads * positions * (width + NOPE),
            bytes_accessed=0,
            transcendentals=0,
        ),
    )(place, moved, lengths, query_t, own, payload, cache_t)


def expert_body(count, groups, sizes, place, w_gate, w_up, w_down, *refs):
    blocks, outs = refs[:count], refs[count:]
    model_width = w_gate.shape[1]
    steps = model_width // CHUNK

    def joined(at):
        return jnp.concatenate([block[:, at].astype(jnp.float32) for block in blocks], axis=0)

    gate = up = None
    for s in range(steps):
        at = slice(s * CHUNK, (s + 1) * CHUNK)
        rows = joined(at).astype(jnp.bfloat16)
        gate_term = jnp.dot(rows, w_gate[0, at, :], preferred_element_type=jnp.float32)
        up_term = jnp.dot(rows, w_up[0, at, :], preferred_element_type=jnp.float32)
        gate = gate_term if gate is None else gate + gate_term
        up = up_term if up is None else up + up_term
    activated = (gate / (1.0 + jnp.exp(-gate)) * up).astype(jnp.bfloat16)
    parts = joined(slice(model_width, blocks[0].shape[1]))
    lane = lax.broadcasted_iota(jnp.int32, parts.shape, 1)
    mine = place[0] // SPLIT
    picked = (lane == mine) | (lane == mine + groups) | (lane == mine + 2 * groups)
    scale = jnp.sum(jnp.where(picked, parts, 0.0), axis=1, keepdims=True)
    tokens = blocks[0].shape[0]
    for s in range(steps):
        at = slice(s * CHUNK, (s + 1) * CHUNK)
        part = jnp.dot(activated, w_down[0, :, at], preferred_element_type=jnp.float32) * scale
        low = 0
        for size, out in zip(sizes, outs):
            out[:, at] = part[low : low + size * tokens].astype(jnp.bfloat16)
            low += size * tokens


def expert(place, w_gate, w_up, w_down, blocks, groups, sizes):
    count = len(blocks)
    tokens = blocks[0].shape[0]
    _, model_width, hidden = w_gate.shape
    return pl.pallas_call(
        functools.partial(expert_body, count, groups, sizes),
        out_shape=[
            jax.ShapeDtypeStruct((size * tokens, model_width), jnp.bfloat16) for size in sizes
        ],
        in_specs=[SCALARS] + [WHOLE] * (3 + count),
        out_specs=[WHOLE] * len(sizes),
        compiler_params=pltpu.CompilerParams(vmem_limit_bytes=40 * MIB),
        cost_estimate=pl.CostEstimate(
            flops=6 * count * tokens * model_width * hidden,
            bytes_accessed=6 * model_width * hidden,
            transcendentals=0,
        ),
    )(place, w_gate, w_up, w_down, *blocks)


def added(*terms):
    return sum(term.astype(jnp.float32) for term in terms).astype(jnp.bfloat16)


def per_device(
    hidden_rows,
    group_ids,
    route_gates,
    w_gate,
    w_up,
    w_down,
    queries,
    new_latent,
    latent_cache,
    cache_lengths,
    moved_slot,
):
    axis = "ep"
    ranks = lax.axis_size(axis)
    turns = ranks // 4
    groups = ranks // SPLIT
    tokens = hidden_rows.shape[0]
    position = lax.axis_index(axis)
    place = position[None]
    query_t = jnp.swapaxes(queries, 1, 2)
    cache_t = jnp.swapaxes(latent_cache, 1, 2)

    rows, payload = prepare(
        place, moved_slot, hidden_rows, group_ids.T, route_gates.T, query_t, new_latent, groups
    )

    columns = {r: rotated(rows, axis, r) for r in range(1, turns) if r != 2}
    across = {0: swapped(rows, axis, 2)}
    order = list(range(turns))
    if turns > 2:
        columns[2] = rotated(columns[1], axis, 1)
        order = [2, 1] + order[3:] + [0]
    for r in order[1:-1]:
        across[r] = swapped(columns[r], axis, 2)

    visiting = shifted(payload, axis, -1)
    early = {r: columns.pop(r) for r in order[1:-1]}
    visiting, early = lax.optimization_barrier((visiting, early))
    home, away, mark = attend(
        place, moved_slot, cache_lengths, query_t, new_latent, visiting, cache_t
    )
    columns, across, away = lax.optimization_barrier((columns, across, away))
    columns.update(early)
    columns[0] = rows
    for r in order[:1]:
        across[r] = swapped(columns[r], axis, 2)
    returned = shifted(away, axis, 1)

    batches = [order[: turns // 2], order[turns // 2 :]]
    near = []
    for batch in batches:
        near += [across[r] for r in batch] + [columns[r] for r in batch]
    blocks = near + [swapped(block, axis, 1) for block in near]
    sizes = []
    for batch in batches:
        sizes += [len(batch)] + [1] * len(batch)
    outs = expert(
        place, w_gate, w_up, w_down, blocks, groups, sizes + [2 * len(b) for b in batches]
    )

    sends = [swapped(send, axis, 1) for send in outs[-2:]]
    sums = {}
    crossed = None
    for batch, chip in zip(batches, sends):
        mine, outs = outs[: 1 + len(batch)], outs[1 + len(batch) :]
        split = len(batch) * tokens
        crossing = added(mine[0], chip[:split])
        if crossed is not None:
            crossing, crossed = lax.optimization_barrier((crossing, crossed))
        crossed = swapped(crossing, axis, 2)
        for i, r in enumerate(batch):
            at = slice(i * tokens, (i + 1) * tokens)
            sums[r] = [mine[1 + i], chip[split:][at], crossed[at]]
    terms = sums.pop(0)
    for r in sums:
        terms = terms + [rotated(added(*sums[r]), axis, -r)]
    moe_out = added(*terms)
    slots = jnp.arange(home.shape[0], dtype=jnp.int32)[:, None, None]
    attn_out = jnp.where(slots == mark[:1, :1][None], returned[None], home)
    return (moe_out, attn_out)


def solution(mesh):
    placed = (
        P(("group", "ep"), None),
        P(("group", "ep"), None),
        P(("group", "ep"), None),
        P("ep", None, None),
        P("ep", None, None),
        P("ep", None, None),
        P(("group", "ep"), None, None),
        P(("group", "ep"), None),
        P(("group", "ep"), None, None),
        P("group"),
        P("group"),
    )
    return jax.shard_map(
        per_device,
        mesh=mesh,
        in_specs=placed,
        out_specs=(P(("group", "ep"), None), P(("group", "ep"), None, None)),
        check_vma=False,
    )
```

```python
import functools
import math

import jax
import jax.numpy as jnp
from jax import lax
from jax.experimental import pallas as pl
from jax.experimental.pallas import tpu as pltpu
from jax.sharding import PartitionSpec as P

NOPE = 512
SPLIT = 8
LANES = 128
CHUNK = 1024
MIB = 1024 * 1024

score_scale = 1.0 / math.sqrt(192.0)

WHOLE = pl.BlockSpec(memory_space=pltpu.VMEM)
SCALARS = pl.BlockSpec(memory_space=pltpu.SMEM)
MAIN = pl.BlockSpec(memory_space=pltpu.HBM)


def shifted(value, axis, steps):
    count = lax.axis_size(axis)
    pairs = [(source, (source + steps) % count) for source in range(count)]
    return lax.ppermute(value, axis, pairs)


def rotated(value, axis, steps):
    return shifted(value, axis, 4 * steps)


def swapped(value, axis, bit):
    pairs = [(source, source ^ bit) for source in range(lax.axis_size(axis))]
    return lax.ppermute(value, axis, pairs)


def prepare_body(groups, place, moved, hidden, ids, gates, query, own, rows, payload):
    tokens, model_width = hidden.shape
    requests, width, _ = query.shape
    rows[:, :model_width] = hidden[...]
    chosen, weight = ids[...].T, gates[...].T
    lane = lax.broadcasted_iota(jnp.int32, (tokens, rows.shape[1] - model_width), 1)
    part = (lane >= groups).astype(jnp.int32) + (lane >= 2 * groups).astype(jnp.int32)
    group = lane - groups * part
    coefficient = jnp.zeros(lane.shape, jnp.float32)
    for k in range(chosen.shape[1]):
        coefficient += jnp.where(chosen[:, k : k + 1] == group, weight[:, k : k + 1], 0.0)
    high = coefficient.astype(jnp.bfloat16).astype(jnp.float32)
    middle = (coefficient - high).astype(jnp.bfloat16).astype(jnp.float32)
    low = coefficient - high - middle
    pieces = jnp.where(part == 0, high, jnp.where(part == 1, middle, low))
    rows[:, model_width:] = jnp.where(lane < 3 * groups, pieces, 0.0).astype(jnp.bfloat16)
    leaving = moved[place[0]]
    payload[:width, :] = query[leaving]
    slots = lax.broadcasted_iota(jnp.int32, own.shape, 0)
    latent = jnp.sum(
        jnp.where(slots == leaving, own[...].astype(jnp.float32), 0.0), axis=0, keepdims=True
    )
    extra = payload.shape[0] - width
    row = lax.broadcasted_iota(jnp.int32, (extra, LANES), 0)
    block = jnp.zeros((extra, LANES), jnp.float32)
    latent = jnp.concatenate([latent, jnp.zeros((1, -width % LANES), jnp.float32)], axis=1)
    for r in range(latent.shape[1] // LANES):
        block = jnp.where(row == r, latent[:, r * LANES : (r + 1) * LANES], block)
    payload[width:, :] = block.astype(jnp.bfloat16)


def prepare(place, moved, hidden, ids_t, gates_t, query_t, own, groups):
    tokens, model_width = hidden.shape
    requests, width, heads = query_t.shape
    tail = -(-3 * groups // LANES) * LANES
    extra = -(-width // (16 * LANES)) * 16
    return pl.pallas_call(
        functools.partial(prepare_body, groups),
        out_shape=[
            jax.ShapeDtypeStruct((tokens, model_width + tail), jnp.bfloat16),
            jax.ShapeDtypeStruct((width + extra, heads), jnp.bfloat16),
        ],
        in_specs=[SCALARS, SCALARS] + [WHOLE] * 5,
        out_specs=[WHOLE, WHOLE],
        compiler_params=pltpu.CompilerParams(vmem_limit_bytes=60 * MIB),
        cost_estimate=pl.CostEstimate(flops=0, bytes_accessed=0, transcendentals=0),
    )(place, moved, hidden, ids_t, gates_t, query_t, own)


def attend_body(ranks, visits, place, moved, lengths, query, own, cache, *refs):
    if visits:
        payload, home, away, asking, keys, sems = refs
    else:
        home, asking, keys, sems = refs
    requests, width, positions = cache.shape
    leaving = moved[place[0]]
    slots = [rank + (leaving <= rank).astype(jnp.int32) for rank in ranks]
    copies = []
    for i, slot in enumerate(slots):
        pltpu.make_async_copy(query.at[slot], asking.at[i], sems.at[2 * i]).start()
        pltpu.make_async_copy(cache.at[slot], keys.at[i], sems.at[2 * i + 1]).start()
    if visits:
        last = len(slots)
        slots.append(leaving)
        pltpu.make_async_copy(cache.at[leaving], keys.at[last], sems.at[2 * last + 1]).start()
    which = lax.broadcasted_iota(jnp.int32, own.shape, 0)
    own_rows = own[...].astype(jnp.float32)
    work = []
    for i, slot in enumerate(slots):
        if i < len(ranks):
            pltpu.make_async_copy(query.at[slot], asking.at[i], sems.at[2 * i]).wait()
            asked = asking[i].T
            latent = jnp.sum(jnp.where(which == slot, own_rows, 0.0), axis=0, keepdims=True)
        else:
            asked = payload[:width, :].T
            tail = payload[width:, :].astype(jnp.float32)
            pieces = [tail[r : r + 1] for r in range(-(-width // LANES))]
            latent = jnp.concatenate(pieces, axis=1)[:, :width]
        pltpu.make_async_copy(cache.at[slot], keys.at[i], sems.at[2 * i + 1]).wait()
        scores = jnp.dot(asked, keys[i], preferred_element_type=jnp.float32) * score_scale
        own_score = (
            jnp.sum(asked.astype(jnp.float32) * latent, axis=1, keepdims=True) * score_scale
        )
        work.append((slot, scores, own_score, latent))
    for i, (slot, scores, own_score, latent) in enumerate(work):
        live = lax.broadcasted_iota(jnp.int32, scores.shape, 1)
        scores = jnp.where(live < lengths[place[0] * requests + slot], scores, -jnp.inf)
        top_score = jnp.maximum(jnp.max(scores, axis=1, keepdims=True), own_score)
        raised = jnp.exp(scores - top_score)
        raised_own = jnp.exp(own_score - top_score)
        share = 1.0 / (jnp.sum(raised, axis=1, keepdims=True) + raised_own)
        weights = (raised * share).astype(jnp.bfloat16)
        weight_own = (raised_own * share).astype(jnp.bfloat16).astype(jnp.float32)
        mixed = lax.dot_general(
            weights,
            keys[i, :NOPE],
            (((1,), (1,)), ((), ())),
            preferred_element_type=jnp.float32,
        )
        result = (mixed + weight_own * latent[:, :NOPE]).astype(jnp.bfloat16)
        if i < len(ranks):
            home[i] = result
        else:
            away[...] = result


def attend(ranks, place, moved, lengths, query_t, own, cache_t, payload=None):
    requests, width, heads = query_t.shape
    positions = cache_t.shape[2]
    visits = payload is not None
    count = len(ranks) + int(visits)
    one = jax.ShapeDtypeStruct((heads, NOPE), jnp.bfloat16)
    many = jax.ShapeDtypeStruct((len(ranks), heads, NOPE), jnp.bfloat16)
    extra = [payload] if visits else []
    return pl.pallas_call(
        functools.partial(attend_body, ranks, visits),
        out_shape=[many] + [one] * len(extra),
        in_specs=[SCALARS] * 3 + [MAIN, WHOLE, MAIN] + [WHOLE] * len(extra),
        out_specs=[WHOLE] * (1 + len(extra)),
        scratch_shapes=[
            pltpu.VMEM((len(ranks), width, heads), jnp.bfloat16),
            pltpu.VMEM((count, width, positions), jnp.bfloat16),
            pltpu.SemaphoreType.DMA((2 * count,)),
        ],
        compiler_params=pltpu.CompilerParams(vmem_limit_bytes=58 * MIB),
        cost_estimate=pl.CostEstimate(
            flops=2 * count * heads * positions * (width + NOPE),
            bytes_accessed=0,
            transcendentals=0,
        ),
    )(place, moved, lengths, query_t, own, cache_t, *extra)


def settle_body(place, moved, first, second, returned, out):
    leaving = moved[place[0]]
    stay = [first[i] for i in range(first.shape[0])] + [second[i] for i in range(second.shape[0])]
    for j in range(out.shape[0]):
        below = stay[max(j - 1, 0)]
        same = stay[min(j, len(stay) - 1)]
        here = jnp.where(leaving < j, below, same)
        out[j] = jnp.where(leaving == j, returned[...], here)


def settle(place, moved, first, second, returned):
    count = first.shape[0] + second.shape[0] + 1
    return pl.pallas_call(
        settle_body,
        out_shape=jax.ShapeDtypeStruct((count,) + returned.shape, returned.dtype),
        in_specs=[SCALARS, SCALARS] + [WHOLE] * 3,
        out_specs=WHOLE,
        compiler_params=pltpu.CompilerParams(vmem_limit_bytes=40 * MIB),
        cost_estimate=pl.CostEstimate(flops=0, bytes_accessed=0, transcendentals=0),
    )(place, moved, first, second, returned)


def expert_body(count, groups, sizes, place, w_gate, w_up, w_down, *refs):
    blocks, outs = refs[:count], refs[count:]
    model_width = w_gate.shape[1]
    steps = model_width // CHUNK

    def joined(at):
        return jnp.concatenate([block[:, at].astype(jnp.float32) for block in blocks], axis=0)

    gate = up = None
    for s in range(steps):
        at = slice(s * CHUNK, (s + 1) * CHUNK)
        rows = joined(at).astype(jnp.bfloat16)
        gate_term = jnp.dot(rows, w_gate[0, at, :], preferred_element_type=jnp.float32)
        up_term = jnp.dot(rows, w_up[0, at, :], preferred_element_type=jnp.float32)
        gate = gate_term if gate is None else gate + gate_term
        up = up_term if up is None else up + up_term
    activated = (gate / (1.0 + jnp.exp(-gate)) * up).astype(jnp.bfloat16)
    parts = joined(slice(model_width, blocks[0].shape[1]))
    lane = lax.broadcasted_iota(jnp.int32, parts.shape, 1)
    mine = place[0] // SPLIT
    picked = (lane == mine) | (lane == mine + groups) | (lane == mine + 2 * groups)
    scale = jnp.sum(jnp.where(picked, parts, 0.0), axis=1, keepdims=True)
    tokens = blocks[0].shape[0]
    for s in range(steps):
        at = slice(s * CHUNK, (s + 1) * CHUNK)
        part = jnp.dot(activated, w_down[0, :, at], preferred_element_type=jnp.float32) * scale
        low = 0
        for size, out in zip(sizes, outs):
            out[:, at] = part[low : low + size * tokens].astype(jnp.bfloat16)
            low += size * tokens


def expert(place, w_gate, w_up, w_down, blocks, groups, sizes):
    count = len(blocks)
    tokens = blocks[0].shape[0]
    _, model_width, hidden = w_gate.shape
    return pl.pallas_call(
        functools.partial(expert_body, count, groups, sizes),
        out_shape=[
            jax.ShapeDtypeStruct((size * tokens, model_width), jnp.bfloat16) for size in sizes
        ],
        in_specs=[SCALARS] + [WHOLE] * (3 + count),
        out_specs=[WHOLE] * len(sizes),
        compiler_params=pltpu.CompilerParams(vmem_limit_bytes=40 * MIB),
        cost_estimate=pl.CostEstimate(
            flops=6 * count * tokens * model_width * hidden,
            bytes_accessed=6 * model_width * hidden,
            transcendentals=0,
        ),
    )(place, w_gate, w_up, w_down, *blocks)


def added(*terms):
    return sum(term.astype(jnp.float32) for term in terms).astype(jnp.bfloat16)


def per_device(
    hidden_rows,
    group_ids,
    route_gates,
    w_gate,
    w_up,
    w_down,
    queries,
    new_latent,
    latent_cache,
    cache_lengths,
    moved_slot,
):
    axis = "ep"
    ranks = lax.axis_size(axis)
    turns = ranks // 4
    groups = ranks // SPLIT
    tokens = hidden_rows.shape[0]
    requests = latent_cache.shape[0]
    position = lax.axis_index(axis)
    place = position[None]
    query_t = jnp.swapaxes(queries, 1, 2)
    cache_t = jnp.swapaxes(latent_cache, 1, 2)

    rows, payload = prepare(
        place, moved_slot, hidden_rows, group_ids.T, route_gates.T, query_t, new_latent, groups
    )

    visiting = shifted(payload, axis, -1)
    columns = {r: rotated(rows, axis, r) for r in range(1, turns) if r != 2}
    across = {0: swapped(rows, axis, 2)}

    half = requests // 2
    scalars = (place, moved_slot, cache_lengths)
    new_here, _ = lax.optimization_barrier((new_latent, rows))
    (first,) = attend(tuple(range(half)), *scalars, query_t, new_here, cache_t)
    columns, across, visiting, first = lax.optimization_barrier((columns, across, visiting, first))
    late = {}
    if turns > 2:
        late[2] = rotated(columns[1], axis, 1)
    crossing = {r: swapped(columns[r], axis, 2) for r in columns}

    second, away = attend(
        tuple(range(half, requests - 1)), *scalars, query_t, new_latent, cache_t, visiting
    )
    late, crossing, away = lax.optimization_barrier((late, crossing, away))
    across.update(crossing)
    columns[0] = rows
    returned = shifted(away, axis, 1)
    late_across = {r: swapped(late[r], axis, 2) for r in late}

    sums = {}
    latest = []

    def sent(outs, batches):
        for i, batch in enumerate(batches):
            mine, outs = outs[: 1 + len(batch)], outs[1 + len(batch) :]
            send = outs[sum(1 + len(b) for b in batches[i + 1 :]) + i]
            if latest:
                _, send = lax.optimization_barrier((latest[0], send))
            chip = swapped(send, axis, 1)
            split = len(batch) * tokens
            leaves = added(mine[0], chip[:split])
            if batch == [0]:
                _, leaves = lax.optimization_barrier((latest[1], leaves))
            crossed = swapped(leaves, axis, 2)
            if not latest:
                latest.extend([leaves, crossed])
            for k, r in enumerate(batch):
                at = slice(k * tokens, (k + 1) * tokens)
                sums[r] = [mine[1 + k], chip[split:][at], crossed[at]]

    def through_experts(batches, columns, across):
        near, sizes = [], []
        for batch in batches:
            near += [across[r] for r in batch] + [columns[r] for r in batch]
            sizes += [len(batch)] + [1] * len(batch)
        blocks = near + [swapped(block, axis, 1) for block in near]
        if latest:
            _, blocks = lax.optimization_barrier((latest[1], blocks))
        sizes += [2 * len(batch) for batch in batches]
        sent(expert(place, w_gate, w_up, w_down, blocks, groups, sizes), batches)

    through_experts([sorted(crossing), [0]], columns, across)
    if late:
        through_experts([sorted(late)], late, late_across)
    terms = sums.pop(0)
    for r in sums:
        terms = terms + [rotated(added(*sums[r]), axis, -r)]
    moe_out = added(*terms)
    attn_out = settle(place, moved_slot, first, second, returned)
    return (moe_out, attn_out)


def solution(mesh):
    placed = (
        P(("group", "ep"), None),
        P(("group", "ep"), None),
        P(("group", "ep"), None),
        P("ep", None, None),
        P("ep", None, None),
        P("ep", None, None),
        P(("group", "ep"), None, None),
        P(("group", "ep"), None),
        P(("group", "ep"), None, None),
        P("group"),
        P("group"),
    )
    return jax.shard_map(
        per_device,
        mesh=mesh,
        in_specs=placed,
        out_specs=(P(("group", "ep"), None), P(("group", "ep"), None, None)),
        check_vma=False,
    )
```

```python
import functools
import math

import jax
import jax.numpy as jnp
from jax import lax
from jax.experimental import pallas as pl
from jax.experimental.pallas import tpu as pltpu
from jax.sharding import PartitionSpec as P

NOPE = 512
SPLIT = 8
LANES = 128
CHUNK = 1024
MIB = 1024 * 1024

score_scale = 1.0 / math.sqrt(192.0)

WHOLE = pl.BlockSpec(memory_space=pltpu.VMEM)
SCALARS = pl.BlockSpec(memory_space=pltpu.SMEM)
MAIN = pl.BlockSpec(memory_space=pltpu.HBM)


def shifted(value, axis, steps):
    count = lax.axis_size(axis)
    pairs = [(source, (source + steps) % count) for source in range(count)]
    return lax.ppermute(value, axis, pairs)


def rotated(value, axis, steps):
    return shifted(value, axis, 4 * steps)


def swapped(value, axis, bit):
    pairs = [(source, source ^ bit) for source in range(lax.axis_size(axis))]
    return lax.ppermute(value, axis, pairs)


def prepare_body(groups, place, moved, hidden, ids, gates, query, own, rows, payload):
    tokens, model_width = hidden.shape
    requests, width, _ = query.shape
    rows[:, :model_width] = hidden[...]
    chosen, weight = ids[...].T, gates[...].T
    lane = lax.broadcasted_iota(jnp.int32, (tokens, rows.shape[1] - model_width), 1)
    part = (lane >= groups).astype(jnp.int32) + (lane >= 2 * groups).astype(jnp.int32)
    group = lane - groups * part
    coefficient = jnp.zeros(lane.shape, jnp.float32)
    for k in range(chosen.shape[1]):
        coefficient += jnp.where(chosen[:, k : k + 1] == group, weight[:, k : k + 1], 0.0)
    high = coefficient.astype(jnp.bfloat16).astype(jnp.float32)
    middle = (coefficient - high).astype(jnp.bfloat16).astype(jnp.float32)
    low = coefficient - high - middle
    pieces = jnp.where(part == 0, high, jnp.where(part == 1, middle, low))
    rows[:, model_width:] = jnp.where(lane < 3 * groups, pieces, 0.0).astype(jnp.bfloat16)
    leaving = moved[place[0]]
    payload[:width, :] = query[leaving]
    slots = lax.broadcasted_iota(jnp.int32, own.shape, 0)
    latent = jnp.sum(
        jnp.where(slots == leaving, own[...].astype(jnp.float32), 0.0), axis=0, keepdims=True
    )
    extra = payload.shape[0] - width
    row = lax.broadcasted_iota(jnp.int32, (extra, LANES), 0)
    block = jnp.zeros((extra, LANES), jnp.float32)
    latent = jnp.concatenate([latent, jnp.zeros((1, -width % LANES), jnp.float32)], axis=1)
    for r in range(latent.shape[1] // LANES):
        block = jnp.where(row == r, latent[:, r * LANES : (r + 1) * LANES], block)
    payload[width:, :] = block.astype(jnp.bfloat16)


def prepare(place, moved, hidden, ids_t, gates_t, query_t, own, groups):
    tokens, model_width = hidden.shape
    requests, width, heads = query_t.shape
    tail = -(-3 * groups // LANES) * LANES
    extra = -(-width // (16 * LANES)) * 16
    return pl.pallas_call(
        functools.partial(prepare_body, groups),
        out_shape=[
            jax.ShapeDtypeStruct((tokens, model_width + tail), jnp.bfloat16),
            jax.ShapeDtypeStruct((width + extra, heads), jnp.bfloat16),
        ],
        in_specs=[SCALARS, SCALARS] + [WHOLE] * 5,
        out_specs=[WHOLE, WHOLE],
        compiler_params=pltpu.CompilerParams(vmem_limit_bytes=60 * MIB),
        cost_estimate=pl.CostEstimate(flops=0, bytes_accessed=0, transcendentals=0),
    )(place, moved, hidden, ids_t, gates_t, query_t, own)


def attend_body(ranks, visits, place, moved, lengths, query, own, cache, *refs):
    if visits:
        payload, home, away, asking, keys, sems = refs
    else:
        home, asking, keys, sems = refs
    requests, width, positions = cache.shape
    leaving = moved[place[0]]
    slots = [rank + (leaving <= rank).astype(jnp.int32) for rank in ranks]
    copies = []
    for i, slot in enumerate(slots):
        pltpu.make_async_copy(query.at[slot], asking.at[i], sems.at[2 * i]).start()
        pltpu.make_async_copy(cache.at[slot], keys.at[i], sems.at[2 * i + 1]).start()
    if visits:
        last = len(slots)
        slots.append(leaving)
        pltpu.make_async_copy(cache.at[leaving], keys.at[last], sems.at[2 * last + 1]).start()
    which = lax.broadcasted_iota(jnp.int32, own.shape, 0)
    own_rows = own[...].astype(jnp.float32)
    work = []
    for i, slot in enumerate(slots):
        if i < len(ranks):
            pltpu.make_async_copy(query.at[slot], asking.at[i], sems.at[2 * i]).wait()
            asked = asking[i].T
            latent = jnp.sum(jnp.where(which == slot, own_rows, 0.0), axis=0, keepdims=True)
        else:
            asked = payload[:width, :].T
            tail = payload[width:, :].astype(jnp.float32)
            pieces = [tail[r : r + 1] for r in range(-(-width // LANES))]
            latent = jnp.concatenate(pieces, axis=1)[:, :width]
        pltpu.make_async_copy(cache.at[slot], keys.at[i], sems.at[2 * i + 1]).wait()
        scores = jnp.dot(asked, keys[i], preferred_element_type=jnp.float32) * score_scale
        own_score = (
            jnp.sum(asked.astype(jnp.float32) * latent, axis=1, keepdims=True) * score_scale
        )
        work.append((slot, scores, own_score, latent))
    for i, (slot, scores, own_score, latent) in enumerate(work):
        live = lax.broadcasted_iota(jnp.int32, scores.shape, 1)
        scores = jnp.where(live < lengths[place[0] * requests + slot], scores, -jnp.inf)
        top_score = jnp.maximum(jnp.max(scores, axis=1, keepdims=True), own_score)
        raised = jnp.exp(scores - top_score)
        raised_own = jnp.exp(own_score - top_score)
        share = 1.0 / (jnp.sum(raised, axis=1, keepdims=True) + raised_own)
        weights = (raised * share).astype(jnp.bfloat16)
        weight_own = (raised_own * share).astype(jnp.bfloat16).astype(jnp.float32)
        mixed = lax.dot_general(
            weights,
            keys[i, :NOPE],
            (((1,), (1,)), ((), ())),
            preferred_element_type=jnp.float32,
        )
        result = (mixed + weight_own * latent[:, :NOPE]).astype(jnp.bfloat16)
        if i < len(ranks):
            home[i] = result
        else:
            away[...] = result


def attend(ranks, place, moved, lengths, query_t, own, cache_t, payload=None):
    requests, width, heads = query_t.shape
    positions = cache_t.shape[2]
    visits = payload is not None
    count = len(ranks) + int(visits)
    one = jax.ShapeDtypeStruct((heads, NOPE), jnp.bfloat16)
    many = jax.ShapeDtypeStruct((len(ranks), heads, NOPE), jnp.bfloat16)
    extra = [payload] if visits else []
    return pl.pallas_call(
        functools.partial(attend_body, ranks, visits),
        out_shape=[many] + [one] * len(extra),
        in_specs=[SCALARS] * 3 + [MAIN, WHOLE, MAIN] + [WHOLE] * len(extra),
        out_specs=[WHOLE] * (1 + len(extra)),
        scratch_shapes=[
            pltpu.VMEM((len(ranks), width, heads), jnp.bfloat16),
            pltpu.VMEM((count, width, positions), jnp.bfloat16),
            pltpu.SemaphoreType.DMA((2 * count,)),
        ],
        compiler_params=pltpu.CompilerParams(vmem_limit_bytes=58 * MIB),
        cost_estimate=pl.CostEstimate(
            flops=2 * count * heads * positions * (width + NOPE),
            bytes_accessed=0,
            transcendentals=0,
        ),
    )(place, moved, lengths, query_t, own, cache_t, *extra)


def settle_body(place, moved, first, second, returned, out):
    leaving = moved[place[0]]
    stay = [first[i] for i in range(first.shape[0])] + [second[i] for i in range(second.shape[0])]
    for j in range(out.shape[0]):
        below = stay[max(j - 1, 0)]
        same = stay[min(j, len(stay) - 1)]
        here = jnp.where(leaving < j, below, same)
        out[j] = jnp.where(leaving == j, returned[...], here)


def settle(place, moved, first, second, returned):
    count = first.shape[0] + second.shape[0] + 1
    return pl.pallas_call(
        settle_body,
        out_shape=jax.ShapeDtypeStruct((count,) + returned.shape, returned.dtype),
        in_specs=[SCALARS, SCALARS] + [WHOLE] * 3,
        out_specs=WHOLE,
        compiler_params=pltpu.CompilerParams(vmem_limit_bytes=40 * MIB),
        cost_estimate=pl.CostEstimate(flops=0, bytes_accessed=0, transcendentals=0),
    )(place, moved, first, second, returned)


def expert_body(count, groups, sizes, place, w_gate, w_up, w_down, *refs):
    blocks, outs = refs[:count], refs[count:]
    model_width = w_gate.shape[1]
    steps = model_width // CHUNK

    def joined(at):
        return jnp.concatenate([block[:, at].astype(jnp.float32) for block in blocks], axis=0)

    gate = up = None
    for s in range(steps):
        at = slice(s * CHUNK, (s + 1) * CHUNK)
        rows = joined(at).astype(jnp.bfloat16)
        gate_term = jnp.dot(rows, w_gate[0, at, :], preferred_element_type=jnp.float32)
        up_term = jnp.dot(rows, w_up[0, at, :], preferred_element_type=jnp.float32)
        gate = gate_term if gate is None else gate + gate_term
        up = up_term if up is None else up + up_term
    activated = (gate / (1.0 + jnp.exp(-gate)) * up).astype(jnp.bfloat16)
    parts = joined(slice(model_width, blocks[0].shape[1]))
    lane = lax.broadcasted_iota(jnp.int32, parts.shape, 1)
    mine = place[0] // SPLIT
    picked = (lane == mine) | (lane == mine + groups) | (lane == mine + 2 * groups)
    scale = jnp.sum(jnp.where(picked, parts, 0.0), axis=1, keepdims=True)
    tokens = blocks[0].shape[0]
    for s in range(steps):
        at = slice(s * CHUNK, (s + 1) * CHUNK)
        part = jnp.dot(activated, w_down[0, :, at], preferred_element_type=jnp.float32) * scale
        low = 0
        for size, out in zip(sizes, outs):
            out[:, at] = part[low : low + size * tokens].astype(jnp.bfloat16)
            low += size * tokens


def expert(place, w_gate, w_up, w_down, blocks, groups, sizes):
    count = len(blocks)
    tokens = blocks[0].shape[0]
    _, model_width, hidden = w_gate.shape
    return pl.pallas_call(
        functools.partial(expert_body, count, groups, sizes),
        out_shape=[
            jax.ShapeDtypeStruct((size * tokens, model_width), jnp.bfloat16) for size in sizes
        ],
        in_specs=[SCALARS] + [WHOLE] * (3 + count),
        out_specs=[WHOLE] * len(sizes),
        compiler_params=pltpu.CompilerParams(vmem_limit_bytes=40 * MIB),
        cost_estimate=pl.CostEstimate(
            flops=6 * count * tokens * model_width * hidden,
            bytes_accessed=6 * model_width * hidden,
            transcendentals=0,
        ),
    )(place, w_gate, w_up, w_down, *blocks)


def added(*terms):
    return sum(term.astype(jnp.float32) for term in terms).astype(jnp.bfloat16)


def per_device(
    hidden_rows,
    group_ids,
    route_gates,
    w_gate,
    w_up,
    w_down,
    queries,
    new_latent,
    latent_cache,
    cache_lengths,
    moved_slot,
):
    axis = "ep"
    ranks = lax.axis_size(axis)
    turns = ranks // 4
    groups = ranks // SPLIT
    tokens = hidden_rows.shape[0]
    requests = latent_cache.shape[0]
    position = lax.axis_index(axis)
    place = position[None]
    query_t = jnp.swapaxes(queries, 1, 2)
    cache_t = jnp.swapaxes(latent_cache, 1, 2)

    rows, payload = prepare(
        place, moved_slot, hidden_rows, group_ids.T, route_gates.T, query_t, new_latent, groups
    )

    visiting = shifted(payload, axis, -1)
    columns = {r: rotated(rows, axis, r) for r in range(1, turns) if r != 2}
    across = {0: swapped(rows, axis, 2)}

    half = requests // 2
    scalars = (place, moved_slot, cache_lengths)
    new_here, _ = lax.optimization_barrier((new_latent, rows))
    (first,) = attend(tuple(range(half)), *scalars, query_t, new_here, cache_t)
    columns, across, visiting, first = lax.optimization_barrier((columns, across, visiting, first))
    late = {}
    if turns > 2:
        late[2] = rotated(columns[1], axis, 1)
    crossing = {r: swapped(columns[r], axis, 2) for r in columns}

    second, away = attend(
        tuple(range(half, requests - 1)), *scalars, query_t, new_latent, cache_t, visiting
    )
    late, crossing, away = lax.optimization_barrier((late, crossing, away))
    across.update(crossing)
    across.update({r: swapped(late[r], axis, 2) for r in late})
    columns[0] = rows
    columns.update(late)

    batches = [sorted(late)] * bool(late) + [sorted(crossing), [0]]
    near, sizes = [], []
    for batch in batches:
        near += [across[r] for r in batch] + [columns[r] for r in batch]
        sizes += [len(batch)] + [1] * len(batch)
    others = [swapped(block, axis, 1) for block in near]
    sizes += [2 * len(batch) for batch in batches]
    outs = expert(place, w_gate, w_up, w_down, near + others, groups, sizes)
    sends = list(outs[len(outs) - len(batches) :])
    sends[0] = swapped(sends[0], axis, 1)

    sums = {}
    for i, batch in enumerate(batches):
        mine, outs = outs[: 1 + len(batch)], outs[1 + len(batch) :]
        split = len(batch) * tokens
        chip = sends[i]
        if i:
            _, chip = lax.optimization_barrier((leaves, chip))
            chip = swapped(chip, axis, 1)
        leaves = added(mine[0], chip[:split])
        crossed = swapped(leaves, axis, 2)
        if batch == batches[-2]:
            crossed, away = lax.optimization_barrier((crossed, away))
        for k, r in enumerate(batch):
            at = slice(k * tokens, (k + 1) * tokens)
            sums[r] = [mine[1 + k], chip[split:][at], crossed[at]]
    terms = sums.pop(0)
    for r in sums:
        terms = terms + [rotated(added(*sums[r]), axis, -r)]
    returned = shifted(away, axis, 1)
    attn_out = settle(place, moved_slot, first, second, returned)
    _, terms = lax.optimization_barrier((attn_out, terms))
    moe_out = added(*terms)
    return (moe_out, attn_out)


def solution(mesh):
    placed = (
        P(("group", "ep"), None),
        P(("group", "ep"), None),
        P(("group", "ep"), None),
        P("ep", None, None),
        P("ep", None, None),
        P("ep", None, None),
        P(("group", "ep"), None, None),
        P(("group", "ep"), None),
        P(("group", "ep"), None, None),
        P("group"),
        P("group"),
    )
    return jax.shard_map(
        per_device,
        mesh=mesh,
        in_specs=placed,
        out_specs=(P(("group", "ep"), None), P(("group", "ep"), None, None)),
        check_vma=False,
    )
```

```python
import functools
import math

import jax
import jax.numpy as jnp
from jax import lax
from jax.experimental import pallas as pl
from jax.experimental.pallas import tpu as pltpu
from jax.sharding import PartitionSpec as P

NOPE = 512
SPLIT = 8
LANES = 128
CHUNK = 1024
MIB = 1024 * 1024

score_scale = 1.0 / math.sqrt(192.0)

WHOLE = pl.BlockSpec(memory_space=pltpu.VMEM)
SCALARS = pl.BlockSpec(memory_space=pltpu.SMEM)
MAIN = pl.BlockSpec(memory_space=pltpu.HBM)


def shifted(value, axis, steps):
    count = lax.axis_size(axis)
    pairs = [(source, (source + steps) % count) for source in range(count)]
    return lax.ppermute(value, axis, pairs)


def rotated(value, axis, steps):
    return shifted(value, axis, 4 * steps)


def swapped(value, axis, bit):
    pairs = [(source, source ^ bit) for source in range(lax.axis_size(axis))]
    return lax.ppermute(value, axis, pairs)


def prepare_body(groups, place, moved, hidden, ids, gates, query, own, rows, payload):
    tokens, model_width = hidden.shape
    requests, width, _ = query.shape
    rows[:, :model_width] = hidden[...]
    chosen, weight = ids[...].T, gates[...].T
    lane = lax.broadcasted_iota(jnp.int32, (tokens, rows.shape[1] - model_width), 1)
    part = (lane >= groups).astype(jnp.int32) + (lane >= 2 * groups).astype(jnp.int32)
    group = lane - groups * part
    coefficient = jnp.zeros(lane.shape, jnp.float32)
    for k in range(chosen.shape[1]):
        coefficient += jnp.where(chosen[:, k : k + 1] == group, weight[:, k : k + 1], 0.0)
    high = coefficient.astype(jnp.bfloat16).astype(jnp.float32)
    middle = (coefficient - high).astype(jnp.bfloat16).astype(jnp.float32)
    low = coefficient - high - middle
    pieces = jnp.where(part == 0, high, jnp.where(part == 1, middle, low))
    rows[:, model_width:] = jnp.where(lane < 3 * groups, pieces, 0.0).astype(jnp.bfloat16)
    leaving = moved[place[0]]
    payload[:width, :] = query[leaving]
    slots = lax.broadcasted_iota(jnp.int32, own.shape, 0)
    latent = jnp.sum(
        jnp.where(slots == leaving, own[...].astype(jnp.float32), 0.0), axis=0, keepdims=True
    )
    extra = payload.shape[0] - width
    row = lax.broadcasted_iota(jnp.int32, (extra, LANES), 0)
    block = jnp.zeros((extra, LANES), jnp.float32)
    latent = jnp.concatenate([latent, jnp.zeros((1, -width % LANES), jnp.float32)], axis=1)
    for r in range(latent.shape[1] // LANES):
        block = jnp.where(row == r, latent[:, r * LANES : (r + 1) * LANES], block)
    payload[width:, :] = block.astype(jnp.bfloat16)


def prepare(place, moved, hidden, ids_t, gates_t, query_t, own, groups):
    tokens, model_width = hidden.shape
    requests, width, heads = query_t.shape
    tail = -(-3 * groups // LANES) * LANES
    extra = -(-width // (16 * LANES)) * 16
    return pl.pallas_call(
        functools.partial(prepare_body, groups),
        out_shape=[
            jax.ShapeDtypeStruct((tokens, model_width + tail), jnp.bfloat16),
            jax.ShapeDtypeStruct((width + extra, heads), jnp.bfloat16),
        ],
        in_specs=[SCALARS, SCALARS] + [WHOLE] * 5,
        out_specs=[WHOLE, WHOLE],
        compiler_params=pltpu.CompilerParams(vmem_limit_bytes=60 * MIB),
        cost_estimate=pl.CostEstimate(flops=0, bytes_accessed=0, transcendentals=0),
    )(place, moved, hidden, ids_t, gates_t, query_t, own)


def crossed(value, axis, steps):
    count = lax.axis_size(axis)
    pairs = [(source, ((source + 4 * steps) % count) ^ 2) for source in range(count)]
    return lax.ppermute(value, axis, pairs)


def attend_body(ranks, visits, place, moved, lengths, query, own, cache, *refs):
    if visits:
        payload, home, away, asking, keys, sems = refs
    else:
        home, asking, keys, sems = refs
    requests, width, positions = cache.shape
    leaving = moved[place[0]]
    slots = [rank + (leaving <= rank).astype(jnp.int32) for rank in ranks]
    copies = []
    for i, slot in enumerate(slots):
        pltpu.make_async_copy(query.at[slot], asking.at[i], sems.at[2 * i]).start()
        pltpu.make_async_copy(cache.at[slot], keys.at[i], sems.at[2 * i + 1]).start()
    if visits:
        last = len(slots)
        slots.append(leaving)
        pltpu.make_async_copy(cache.at[leaving], keys.at[last], sems.at[2 * last + 1]).start()
    which = lax.broadcasted_iota(jnp.int32, own.shape, 0)
    own_rows = own[...].astype(jnp.float32)
    work = []
    for i, slot in enumerate(slots):
        if i < len(ranks):
            pltpu.make_async_copy(query.at[slot], asking.at[i], sems.at[2 * i]).wait()
            asked = asking[i].T
            latent = jnp.sum(jnp.where(which == slot, own_rows, 0.0), axis=0, keepdims=True)
        else:
            asked = payload[:width, :].T
            tail = payload[width:, :].astype(jnp.float32)
            pieces = [tail[r : r + 1] for r in range(-(-width // LANES))]
            latent = jnp.concatenate(pieces, axis=1)[:, :width]
        pltpu.make_async_copy(cache.at[slot], keys.at[i], sems.at[2 * i + 1]).wait()
        scores = jnp.dot(asked, keys[i], preferred_element_type=jnp.float32) * score_scale
        own_score = (
            jnp.sum(asked.astype(jnp.float32) * latent, axis=1, keepdims=True) * score_scale
        )
        work.append((slot, scores, own_score, latent))
    for i, (slot, scores, own_score, latent) in enumerate(work):
        live = lax.broadcasted_iota(jnp.int32, scores.shape, 1)
        scores = jnp.where(live < lengths[place[0] * requests + slot], scores, -jnp.inf)
        top_score = jnp.maximum(jnp.max(scores, axis=1, keepdims=True), own_score)
        raised = jnp.exp(scores - top_score)
        raised_own = jnp.exp(own_score - top_score)
        share = 1.0 / (jnp.sum(raised, axis=1, keepdims=True) + raised_own)
        weights = (raised * share).astype(jnp.bfloat16)
        weight_own = (raised_own * share).astype(jnp.bfloat16).astype(jnp.float32)
        mixed = lax.dot_general(
            weights,
            keys[i, :NOPE],
            (((1,), (1,)), ((), ())),
            preferred_element_type=jnp.float32,
        )
        result = (mixed + weight_own * latent[:, :NOPE]).astype(jnp.bfloat16)
        if i < len(ranks):
            home[i] = result
        else:
            away[...] = result


def attend(ranks, place, moved, lengths, query_t, own, cache_t, payload=None):
    requests, width, heads = query_t.shape
    positions = cache_t.shape[2]
    visits = payload is not None
    count = len(ranks) + int(visits)
    one = jax.ShapeDtypeStruct((heads, NOPE), jnp.bfloat16)
    many = jax.ShapeDtypeStruct((len(ranks), heads, NOPE), jnp.bfloat16)
    extra = [payload] if visits else []
    return pl.pallas_call(
        functools.partial(attend_body, ranks, visits),
        out_shape=[many] + [one] * len(extra),
        in_specs=[SCALARS] * 3 + [MAIN, WHOLE, MAIN] + [WHOLE] * len(extra),
        out_specs=[WHOLE] * (1 + len(extra)),
        scratch_shapes=[
            pltpu.VMEM((len(ranks), width, heads), jnp.bfloat16),
            pltpu.VMEM((count, width, positions), jnp.bfloat16),
            pltpu.SemaphoreType.DMA((2 * count,)),
        ],
        compiler_params=pltpu.CompilerParams(vmem_limit_bytes=58 * MIB),
        cost_estimate=pl.CostEstimate(
            flops=2 * count * heads * positions * (width + NOPE),
            bytes_accessed=0,
            transcendentals=0,
        ),
    )(place, moved, lengths, query_t, own, cache_t, *extra)


def settle_body(place, moved, first, second, returned, out):
    leaving = moved[place[0]]
    stay = [first[i] for i in range(first.shape[0])] + [second[i] for i in range(second.shape[0])]
    for j in range(out.shape[0]):
        below = stay[max(j - 1, 0)]
        same = stay[min(j, len(stay) - 1)]
        here = jnp.where(leaving < j, below, same)
        out[j] = jnp.where(leaving == j, returned[...], here)


def settle(place, moved, first, second, returned):
    count = first.shape[0] + second.shape[0] + 1
    return pl.pallas_call(
        settle_body,
        out_shape=jax.ShapeDtypeStruct((count,) + returned.shape, returned.dtype),
        in_specs=[SCALARS, SCALARS] + [WHOLE] * 3,
        out_specs=WHOLE,
        compiler_params=pltpu.CompilerParams(vmem_limit_bytes=40 * MIB),
        cost_estimate=pl.CostEstimate(flops=0, bytes_accessed=0, transcendentals=0),
    )(place, moved, first, second, returned)


def expert_body(count, groups, sizes, place, w_gate, w_up, w_down, *refs):
    blocks, outs = refs[:count], refs[count:]
    model_width = w_gate.shape[1]
    steps = model_width // CHUNK

    def joined(at):
        return jnp.concatenate([block[:, at].astype(jnp.float32) for block in blocks], axis=0)

    gate = up = None
    for s in range(steps):
        at = slice(s * CHUNK, (s + 1) * CHUNK)
        rows = joined(at).astype(jnp.bfloat16)
        gate_term = jnp.dot(rows, w_gate[0, at, :], preferred_element_type=jnp.float32)
        up_term = jnp.dot(rows, w_up[0, at, :], preferred_element_type=jnp.float32)
        gate = gate_term if gate is None else gate + gate_term
        up = up_term if up is None else up + up_term
    activated = (gate / (1.0 + jnp.exp(-gate)) * up).astype(jnp.bfloat16)
    parts = joined(slice(model_width, blocks[0].shape[1]))
    lane = lax.broadcasted_iota(jnp.int32, parts.shape, 1)
    mine = place[0] // SPLIT
    picked = (lane == mine) | (lane == mine + groups) | (lane == mine + 2 * groups)
    scale = jnp.sum(jnp.where(picked, parts, 0.0), axis=1, keepdims=True)
    tokens = blocks[0].shape[0]
    for s in range(steps):
        at = slice(s * CHUNK, (s + 1) * CHUNK)
        part = jnp.dot(activated, w_down[0, :, at], preferred_element_type=jnp.float32) * scale
        low = 0
        for size, out in zip(sizes, outs):
            out[:, at] = part[low : low + size * tokens].astype(jnp.bfloat16)
            low += size * tokens


def expert(place, w_gate, w_up, w_down, blocks, groups, sizes):
    count = len(blocks)
    tokens = blocks[0].shape[0]
    _, model_width, hidden = w_gate.shape
    return pl.pallas_call(
        functools.partial(expert_body, count, groups, sizes),
        out_shape=[
            jax.ShapeDtypeStruct((size * tokens, model_width), jnp.bfloat16) for size in sizes
        ],
        in_specs=[SCALARS] + [WHOLE] * (3 + count),
        out_specs=[WHOLE] * len(sizes),
        compiler_params=pltpu.CompilerParams(vmem_limit_bytes=40 * MIB),
        cost_estimate=pl.CostEstimate(
            flops=6 * count * tokens * model_width * hidden,
            bytes_accessed=6 * model_width * hidden,
            transcendentals=0,
        ),
    )(place, w_gate, w_up, w_down, *blocks)


def added(*terms):
    return sum(term.astype(jnp.float32) for term in terms).astype(jnp.bfloat16)


def per_device(
    hidden_rows,
    group_ids,
    route_gates,
    w_gate,
    w_up,
    w_down,
    queries,
    new_latent,
    latent_cache,
    cache_lengths,
    moved_slot,
):
    axis = "ep"
    ranks = lax.axis_size(axis)
    turns = ranks // 4
    groups = ranks // SPLIT
    tokens = hidden_rows.shape[0]
    requests = latent_cache.shape[0]
    position = lax.axis_index(axis)
    place = position[None]
    query_t = jnp.swapaxes(queries, 1, 2)
    cache_t = jnp.swapaxes(latent_cache, 1, 2)

    rows, payload = prepare(
        place, moved_slot, hidden_rows, group_ids.T, route_gates.T, query_t, new_latent, groups
    )

    visiting = shifted(payload, axis, -1)
    far = [2] if turns > 2 else []
    columns = {r: rotated(rows, axis, r) for r in far}
    across = {0: swapped(rows, axis, 2)}

    half = requests // 2
    scalars = (place, moved_slot, cache_lengths)
    new_here, _ = lax.optimization_barrier((new_latent, rows))
    (first,) = attend(tuple(range(half)), *scalars, query_t, new_here, cache_t)
    rows_then, first = lax.optimization_barrier((rows, first))
    straight = [r for r in range(1, turns) if r not in far]
    direct = {r: (crossed(rows_then, axis, r), rotated(rows_then, axis, r)) for r in straight}

    columns, visiting = lax.optimization_barrier((columns, visiting))
    across.update({r: swapped(columns[r], axis, 2) for r in far})
    second, away = attend(
        tuple(range(half, requests - 1)), *scalars, query_t, new_latent, cache_t, visiting
    )
    returned = shifted(away, axis, 1)
    columns[0] = rows
    pairs = {r: (across[r], columns[r]) for r in columns}
    pairs, direct, _ = lax.optimization_barrier((pairs, direct, away))
    pairs.update(direct)

    order = far + straight + [0]
    near = [block for r in order for block in pairs[r]]
    blocks = near + [swapped(block, axis, 1) for block in near]
    ahead = 2 * len(far)
    sizes = [1] * len(near) + [size for size in (ahead, len(near) - ahead) if size]
    outs = expert(place, w_gate, w_up, w_down, blocks, groups, sizes)
    chips = [swapped(send, axis, 1) for send in outs[len(near) :]]
    chip_blocks = []
    for chip in chips:
        chip_blocks += [chip[i : i + tokens] for i in range(0, chip.shape[0], tokens)]

    halves = [[outs[i], chip_blocks[i]] for i in range(len(near))]
    sums = {r: (halves[2 * i], halves[2 * i + 1]) for i, r in enumerate(order)}
    over = {r: swapped(added(*sums[r][0]), axis, 2) for r in far}
    terms = sums[0][1]
    for r in straight:
        terms = terms + [
            crossed(added(*sums[r][0]), axis, -r),
            rotated(added(*sums[r][1]), axis, -r),
        ]
    over, terms = lax.optimization_barrier((over, terms))
    terms = terms + [swapped(added(*sums[0][0]), axis, 2)]
    for r in far:
        terms = terms + [rotated(added(*sums[r][1], over[r]), axis, -r)]
    attn_out = settle(place, moved_slot, first, second, returned)
    _, terms = lax.optimization_barrier((attn_out, terms))
    moe_out = added(*terms)
    return (moe_out, attn_out)


def solution(mesh):
    placed = (
        P(("group", "ep"), None),
        P(("group", "ep"), None),
        P(("group", "ep"), None),
        P("ep", None, None),
        P("ep", None, None),
        P("ep", None, None),
        P(("group", "ep"), None, None),
        P(("group", "ep"), None),
        P(("group", "ep"), None, None),
        P("group"),
        P("group"),
    )
    return jax.shard_map(
        per_device,
        mesh=mesh,
        in_specs=placed,
        out_specs=(P(("group", "ep"), None), P(("group", "ep"), None, None)),
        check_vma=False,
    )
```

```python
import functools
import math

import jax
import jax.numpy as jnp
from jax import lax
from jax.experimental import pallas as pl
from jax.experimental.pallas import tpu as pltpu
from jax.sharding import PartitionSpec as P

NOPE = 512
SPLIT = 8
LANES = 128
CHUNK = 1024
MIB = 1024 * 1024

score_scale = 1.0 / math.sqrt(192.0)

WHOLE = pl.BlockSpec(memory_space=pltpu.VMEM)
SCALARS = pl.BlockSpec(memory_space=pltpu.SMEM)
MAIN = pl.BlockSpec(memory_space=pltpu.HBM)


def shifted(value, axis, steps):
    count = lax.axis_size(axis)
    pairs = [(source, (source + steps) % count) for source in range(count)]
    return lax.ppermute(value, axis, pairs)


def rotated(value, axis, steps):
    return shifted(value, axis, 4 * steps)


def swapped(value, axis, bit):
    pairs = [(source, source ^ bit) for source in range(lax.axis_size(axis))]
    return lax.ppermute(value, axis, pairs)


def prepare_body(groups, place, moved, hidden, ids, gates, query, own, rows, payload):
    tokens, model_width = hidden.shape
    requests, width, _ = query.shape
    rows[:, :model_width] = hidden[...]
    chosen, weight = ids[...].T, gates[...].T
    lane = lax.broadcasted_iota(jnp.int32, (tokens, rows.shape[1] - model_width), 1)
    part = (lane >= groups).astype(jnp.int32) + (lane >= 2 * groups).astype(jnp.int32)
    group = lane - groups * part
    coefficient = jnp.zeros(lane.shape, jnp.float32)
    for k in range(chosen.shape[1]):
        coefficient += jnp.where(chosen[:, k : k + 1] == group, weight[:, k : k + 1], 0.0)
    high = coefficient.astype(jnp.bfloat16).astype(jnp.float32)
    middle = (coefficient - high).astype(jnp.bfloat16).astype(jnp.float32)
    low = coefficient - high - middle
    pieces = jnp.where(part == 0, high, jnp.where(part == 1, middle, low))
    rows[:, model_width:] = jnp.where(lane < 3 * groups, pieces, 0.0).astype(jnp.bfloat16)
    leaving = moved[place[0]]
    payload[:width, :] = query[leaving]
    slots = lax.broadcasted_iota(jnp.int32, own.shape, 0)
    latent = jnp.sum(
        jnp.where(slots == leaving, own[...].astype(jnp.float32), 0.0), axis=0, keepdims=True
    )
    extra = payload.shape[0] - width
    row = lax.broadcasted_iota(jnp.int32, (extra, LANES), 0)
    block = jnp.zeros((extra, LANES), jnp.float32)
    latent = jnp.concatenate([latent, jnp.zeros((1, -width % LANES), jnp.float32)], axis=1)
    for r in range(latent.shape[1] // LANES):
        block = jnp.where(row == r, latent[:, r * LANES : (r + 1) * LANES], block)
    payload[width:, :] = block.astype(jnp.bfloat16)


def prepare(place, moved, hidden, ids_t, gates_t, query_t, own, groups):
    tokens, model_width = hidden.shape
    requests, width, heads = query_t.shape
    tail = -(-3 * groups // LANES) * LANES
    extra = -(-width // (16 * LANES)) * 16
    return pl.pallas_call(
        functools.partial(prepare_body, groups),
        out_shape=[
            jax.ShapeDtypeStruct((tokens, model_width + tail), jnp.bfloat16),
            jax.ShapeDtypeStruct((width + extra, heads), jnp.bfloat16),
        ],
        in_specs=[SCALARS, SCALARS] + [WHOLE] * 5,
        out_specs=[WHOLE, WHOLE],
        compiler_params=pltpu.CompilerParams(vmem_limit_bytes=60 * MIB),
        cost_estimate=pl.CostEstimate(flops=0, bytes_accessed=0, transcendentals=0),
    )(place, moved, hidden, ids_t, gates_t, query_t, own)


def attend_body(ranks, visits, place, moved, lengths, query, own, cache, *refs):
    if visits:
        payload, home, away, asking, keys, sems = refs
    else:
        home, asking, keys, sems = refs
    requests, width, positions = cache.shape
    leaving = moved[place[0]]
    slots = [rank + (leaving <= rank).astype(jnp.int32) for rank in ranks]
    copies = []
    for i, slot in enumerate(slots):
        pltpu.make_async_copy(query.at[slot], asking.at[i], sems.at[2 * i]).start()
        pltpu.make_async_copy(cache.at[slot], keys.at[i], sems.at[2 * i + 1]).start()
    if visits:
        last = len(slots)
        slots.append(leaving)
        pltpu.make_async_copy(cache.at[leaving], keys.at[last], sems.at[2 * last + 1]).start()
    which = lax.broadcasted_iota(jnp.int32, own.shape, 0)
    own_rows = own[...].astype(jnp.float32)
    work = []
    for i, slot in enumerate(slots):
        if i < len(ranks):
            pltpu.make_async_copy(query.at[slot], asking.at[i], sems.at[2 * i]).wait()
            asked = asking[i].T
            latent = jnp.sum(jnp.where(which == slot, own_rows, 0.0), axis=0, keepdims=True)
        else:
            asked = payload[:width, :].T
            tail = payload[width:, :].astype(jnp.float32)
            pieces = [tail[r : r + 1] for r in range(-(-width // LANES))]
            latent = jnp.concatenate(pieces, axis=1)[:, :width]
        pltpu.make_async_copy(cache.at[slot], keys.at[i], sems.at[2 * i + 1]).wait()
        scores = jnp.dot(asked, keys[i], preferred_element_type=jnp.float32) * score_scale
        own_score = (
            jnp.sum(asked.astype(jnp.float32) * latent, axis=1, keepdims=True) * score_scale
        )
        work.append((slot, scores, own_score, latent))
    for i, (slot, scores, own_score, latent) in enumerate(work):
        live = lax.broadcasted_iota(jnp.int32, scores.shape, 1)
        scores = jnp.where(live < lengths[place[0] * requests + slot], scores, -jnp.inf)
        top_score = jnp.maximum(jnp.max(scores, axis=1, keepdims=True), own_score)
        raised = jnp.exp(scores - top_score)
        raised_own = jnp.exp(own_score - top_score)
        share = 1.0 / (jnp.sum(raised, axis=1, keepdims=True) + raised_own)
        weights = (raised * share).astype(jnp.bfloat16)
        weight_own = (raised_own * share).astype(jnp.bfloat16).astype(jnp.float32)
        mixed = lax.dot_general(
            weights,
            keys[i, :NOPE],
            (((1,), (1,)), ((), ())),
            preferred_element_type=jnp.float32,
        )
        result = (mixed + weight_own * latent[:, :NOPE]).astype(jnp.bfloat16)
        if i < len(ranks):
            home[i] = result
        else:
            away[...] = result


def attend(ranks, place, moved, lengths, query_t, own, cache_t, payload=None):
    requests, width, heads = query_t.shape
    positions = cache_t.shape[2]
    visits = payload is not None
    count = len(ranks) + int(visits)
    one = jax.ShapeDtypeStruct((heads, NOPE), jnp.bfloat16)
    many = jax.ShapeDtypeStruct((len(ranks), heads, NOPE), jnp.bfloat16)
    extra = [payload] if visits else []
    return pl.pallas_call(
        functools.partial(attend_body, ranks, visits),
        out_shape=[many] + [one] * len(extra),
        in_specs=[SCALARS] * 3 + [MAIN, WHOLE, MAIN] + [WHOLE] * len(extra),
        out_specs=[WHOLE] * (1 + len(extra)),
        scratch_shapes=[
            pltpu.VMEM((len(ranks), width, heads), jnp.bfloat16),
            pltpu.VMEM((count, width, positions), jnp.bfloat16),
            pltpu.SemaphoreType.DMA((2 * count,)),
        ],
        compiler_params=pltpu.CompilerParams(vmem_limit_bytes=58 * MIB),
        cost_estimate=pl.CostEstimate(
            flops=2 * count * heads * positions * (width + NOPE),
            bytes_accessed=0,
            transcendentals=0,
        ),
    )(place, moved, lengths, query_t, own, cache_t, *extra)


def settle_body(place, moved, first, second, returned, out):
    leaving = moved[place[0]]
    stay = [first[i] for i in range(first.shape[0])] + [second[i] for i in range(second.shape[0])]
    for j in range(out.shape[0]):
        below = stay[max(j - 1, 0)]
        same = stay[min(j, len(stay) - 1)]
        here = jnp.where(leaving < j, below, same)
        out[j] = jnp.where(leaving == j, returned[...], here)


def settle(place, moved, first, second, returned):
    count = first.shape[0] + second.shape[0] + 1
    return pl.pallas_call(
        settle_body,
        out_shape=jax.ShapeDtypeStruct((count,) + returned.shape, returned.dtype),
        in_specs=[SCALARS, SCALARS] + [WHOLE] * 3,
        out_specs=WHOLE,
        compiler_params=pltpu.CompilerParams(vmem_limit_bytes=40 * MIB),
        cost_estimate=pl.CostEstimate(flops=0, bytes_accessed=0, transcendentals=0),
    )(place, moved, first, second, returned)


def expert_body(count, groups, sizes, place, w_gate, w_up, w_down, *refs):
    blocks, outs = refs[:count], refs[count:]
    model_width = w_gate.shape[1]
    steps = model_width // CHUNK

    def joined(at):
        return jnp.concatenate([block[:, at].astype(jnp.float32) for block in blocks], axis=0)

    gate = up = None
    for s in range(steps):
        at = slice(s * CHUNK, (s + 1) * CHUNK)
        rows = joined(at).astype(jnp.bfloat16)
        gate_term = jnp.dot(rows, w_gate[0, at, :], preferred_element_type=jnp.float32)
        up_term = jnp.dot(rows, w_up[0, at, :], preferred_element_type=jnp.float32)
        gate = gate_term if gate is None else gate + gate_term
        up = up_term if up is None else up + up_term
    activated = (gate / (1.0 + jnp.exp(-gate)) * up).astype(jnp.bfloat16)
    parts = joined(slice(model_width, blocks[0].shape[1]))
    lane = lax.broadcasted_iota(jnp.int32, parts.shape, 1)
    mine = place[0] // SPLIT
    picked = (lane == mine) | (lane == mine + groups) | (lane == mine + 2 * groups)
    scale = jnp.sum(jnp.where(picked, parts, 0.0), axis=1, keepdims=True)
    tokens = blocks[0].shape[0]
    for s in range(steps):
        at = slice(s * CHUNK, (s + 1) * CHUNK)
        part = jnp.dot(activated, w_down[0, :, at], preferred_element_type=jnp.float32) * scale
        low = 0
        for size, out in zip(sizes, outs):
            out[:, at] = part[low : low + size * tokens].astype(jnp.bfloat16)
            low += size * tokens


def expert(place, w_gate, w_up, w_down, blocks, groups, sizes):
    count = len(blocks)
    tokens = blocks[0].shape[0]
    _, model_width, hidden = w_gate.shape
    return pl.pallas_call(
        functools.partial(expert_body, count, groups, sizes),
        out_shape=[
            jax.ShapeDtypeStruct((size * tokens, model_width), jnp.bfloat16) for size in sizes
        ],
        in_specs=[SCALARS] + [WHOLE] * (3 + count),
        out_specs=[WHOLE] * len(sizes),
        compiler_params=pltpu.CompilerParams(vmem_limit_bytes=40 * MIB),
        cost_estimate=pl.CostEstimate(
            flops=6 * count * tokens * model_width * hidden,
            bytes_accessed=6 * model_width * hidden,
            transcendentals=0,
        ),
    )(place, w_gate, w_up, w_down, *blocks)


def added(*terms):
    return sum(term.astype(jnp.float32) for term in terms).astype(jnp.bfloat16)


def per_device(
    hidden_rows,
    group_ids,
    route_gates,
    w_gate,
    w_up,
    w_down,
    queries,
    new_latent,
    latent_cache,
    cache_lengths,
    moved_slot,
):
    axis = "ep"
    ranks = lax.axis_size(axis)
    turns = ranks // 4
    groups = ranks // SPLIT
    tokens = hidden_rows.shape[0]
    requests = latent_cache.shape[0]
    position = lax.axis_index(axis)
    place = position[None]
    query_t = jnp.swapaxes(queries, 1, 2)
    cache_t = jnp.swapaxes(latent_cache, 1, 2)

    rows, payload = prepare(
        place, moved_slot, hidden_rows, group_ids.T, route_gates.T, query_t, new_latent, groups
    )

    visiting = shifted(payload, axis, -1)
    order = list(range(1, turns))
    order = order[1:2] + order[:1] + order[2:]
    columns = {r: rotated(rows, axis, r) for r in order}
    across = {0: swapped(rows, axis, 2)}

    half = requests // 2
    scalars = (place, moved_slot, cache_lengths)
    new_here, _ = lax.optimization_barrier((new_latent, rows))
    (first,) = attend(tuple(range(half)), *scalars, query_t, new_here, cache_t)
    columns, across, visiting, first = lax.optimization_barrier((columns, across, visiting, first))

    later = {r: swapped(columns[r], axis, 2) for r in order}
    second, away = attend(
        tuple(range(half, requests - 1)), *scalars, query_t, new_latent, cache_t, visiting
    )
    later, away = lax.optimization_barrier((later, away))
    across.update(later)
    columns[0] = rows

    order = order + [0]
    near = [block for r in order for block in (across[r], columns[r])]
    blocks = near + [swapped(block, axis, 1) for block in near]
    sizes = [1] * len(near) + [2] * len(order)
    outs = expert(place, w_gate, w_up, w_down, blocks, groups, sizes)
    keeps, sends = outs[: len(near)], outs[len(near) :]

    sums = {}
    for i, r in enumerate(order):
        chip = swapped(sends[i], axis, 1)
        over = swapped(added(keeps[2 * i], chip[:tokens]), axis, 2)
        if i == len(order) - 2:
            over, away = lax.optimization_barrier((over, away))
        sums[r] = [keeps[2 * i + 1], chip[tokens:], over]
    terms = sums.pop(0)
    for r in sums:
        terms = terms + [rotated(added(*sums[r]), axis, -r)]
    returned = shifted(away, axis, 1)
    attn_out = settle(place, moved_slot, first, second, returned)
    _, terms = lax.optimization_barrier((attn_out, terms))
    moe_out = added(*terms)
    return (moe_out, attn_out)


def solution(mesh):
    placed = (
        P(("group", "ep"), None),
        P(("group", "ep"), None),
        P(("group", "ep"), None),
        P("ep", None, None),
        P("ep", None, None),
        P("ep", None, None),
        P(("group", "ep"), None, None),
        P(("group", "ep"), None),
        P(("group", "ep"), None, None),
        P("group"),
        P("group"),
    )
    return jax.shard_map(
        per_device,
        mesh=mesh,
        in_specs=placed,
        out_specs=(P(("group", "ep"), None), P(("group", "ep"), None, None)),
        check_vma=False,
    )
```

```python
import functools
import math

import jax
import jax.numpy as jnp
from jax import lax
from jax.experimental import pallas as pl
from jax.experimental.pallas import tpu as pltpu
from jax.sharding import PartitionSpec as P

NOPE = 512
SPLIT = 8
LANES = 128
CHUNK = 1024
MIB = 1024 * 1024

score_scale = 1.0 / math.sqrt(192.0)

WHOLE = pl.BlockSpec(memory_space=pltpu.VMEM)
SCALARS = pl.BlockSpec(memory_space=pltpu.SMEM)
MAIN = pl.BlockSpec(memory_space=pltpu.HBM)


def shifted(value, axis, steps):
    count = lax.axis_size(axis)
    pairs = [(source, (source + steps) % count) for source in range(count)]
    return lax.ppermute(value, axis, pairs)


def rotated(value, axis, steps):
    return shifted(value, axis, 4 * steps)


def swapped(value, axis, bit):
    pairs = [(source, source ^ bit) for source in range(lax.axis_size(axis))]
    return lax.ppermute(value, axis, pairs)


def prepare_body(groups, place, moved, hidden, ids, gates, query, own, rows, payload):
    tokens, model_width = hidden.shape
    requests, width, _ = query.shape
    rows[:, :model_width] = hidden[...]
    chosen, weight = ids[...].T, gates[...].T
    lane = lax.broadcasted_iota(jnp.int32, (tokens, rows.shape[1] - model_width), 1)
    part = (lane >= groups).astype(jnp.int32) + (lane >= 2 * groups).astype(jnp.int32)
    group = lane - groups * part
    coefficient = jnp.zeros(lane.shape, jnp.float32)
    for k in range(chosen.shape[1]):
        coefficient += jnp.where(chosen[:, k : k + 1] == group, weight[:, k : k + 1], 0.0)
    high = coefficient.astype(jnp.bfloat16).astype(jnp.float32)
    middle = (coefficient - high).astype(jnp.bfloat16).astype(jnp.float32)
    low = coefficient - high - middle
    pieces = jnp.where(part == 0, high, jnp.where(part == 1, middle, low))
    rows[:, model_width:] = jnp.where(lane < 3 * groups, pieces, 0.0).astype(jnp.bfloat16)
    leaving = moved[place[0]]
    payload[:width, :] = query[leaving]
    slots = lax.broadcasted_iota(jnp.int32, own.shape, 0)
    latent = jnp.sum(
        jnp.where(slots == leaving, own[...].astype(jnp.float32), 0.0), axis=0, keepdims=True
    )
    extra = payload.shape[0] - width
    row = lax.broadcasted_iota(jnp.int32, (extra, LANES), 0)
    block = jnp.zeros((extra, LANES), jnp.float32)
    latent = jnp.concatenate([latent, jnp.zeros((1, -width % LANES), jnp.float32)], axis=1)
    for r in range(latent.shape[1] // LANES):
        block = jnp.where(row == r, latent[:, r * LANES : (r + 1) * LANES], block)
    payload[width:, :] = block.astype(jnp.bfloat16)


def prepare(place, moved, hidden, ids_t, gates_t, query_t, own, groups):
    tokens, model_width = hidden.shape
    requests, width, heads = query_t.shape
    tail = -(-3 * groups // LANES) * LANES
    extra = -(-width // (16 * LANES)) * 16
    return pl.pallas_call(
        functools.partial(prepare_body, groups),
        out_shape=[
            jax.ShapeDtypeStruct((tokens, model_width + tail), jnp.bfloat16),
            jax.ShapeDtypeStruct((width + extra, heads), jnp.bfloat16),
        ],
        in_specs=[SCALARS, SCALARS] + [WHOLE] * 5,
        out_specs=[WHOLE, WHOLE],
        compiler_params=pltpu.CompilerParams(vmem_limit_bytes=60 * MIB),
        cost_estimate=pl.CostEstimate(flops=0, bytes_accessed=0, transcendentals=0),
    )(place, moved, hidden, ids_t, gates_t, query_t, own)


def attend_body(ranks, visits, place, moved, lengths, query, own, cache, *refs):
    if visits:
        payload, home, away, asking, keys, sems = refs
    else:
        home, asking, keys, sems = refs
    requests, width, positions = cache.shape
    leaving = moved[place[0]]
    slots = [rank + (leaving <= rank).astype(jnp.int32) for rank in ranks]
    copies = []
    for i, slot in enumerate(slots):
        pltpu.make_async_copy(query.at[slot], asking.at[i], sems.at[2 * i]).start()
        pltpu.make_async_copy(cache.at[slot], keys.at[i], sems.at[2 * i + 1]).start()
    if visits:
        last = len(slots)
        slots.append(leaving)
        pltpu.make_async_copy(cache.at[leaving], keys.at[last], sems.at[2 * last + 1]).start()
    which = lax.broadcasted_iota(jnp.int32, own.shape, 0)
    own_rows = own[...].astype(jnp.float32)
    work = []
    for i, slot in enumerate(slots):
        if i < len(ranks):
            pltpu.make_async_copy(query.at[slot], asking.at[i], sems.at[2 * i]).wait()
            asked = asking[i].T
            latent = jnp.sum(jnp.where(which == slot, own_rows, 0.0), axis=0, keepdims=True)
        else:
            asked = payload[:width, :].T
            tail = payload[width:, :].astype(jnp.float32)
            pieces = [tail[r : r + 1] for r in range(-(-width // LANES))]
            latent = jnp.concatenate(pieces, axis=1)[:, :width]
        pltpu.make_async_copy(cache.at[slot], keys.at[i], sems.at[2 * i + 1]).wait()
        scores = jnp.dot(asked, keys[i], preferred_element_type=jnp.float32) * score_scale
        own_score = (
            jnp.sum(asked.astype(jnp.float32) * latent, axis=1, keepdims=True) * score_scale
        )
        work.append((slot, scores, own_score, latent))
    for i, (slot, scores, own_score, latent) in enumerate(work):
        live = lax.broadcasted_iota(jnp.int32, scores.shape, 1)
        scores = jnp.where(live < lengths[place[0] * requests + slot], scores, -jnp.inf)
        top_score = jnp.maximum(jnp.max(scores, axis=1, keepdims=True), own_score)
        raised = jnp.exp(scores - top_score)
        raised_own = jnp.exp(own_score - top_score)
        share = 1.0 / (jnp.sum(raised, axis=1, keepdims=True) + raised_own)
        weights = (raised * share).astype(jnp.bfloat16)
        weight_own = (raised_own * share).astype(jnp.bfloat16).astype(jnp.float32)
        mixed = lax.dot_general(
            weights,
            keys[i, :NOPE],
            (((1,), (1,)), ((), ())),
            preferred_element_type=jnp.float32,
        )
        result = (mixed + weight_own * latent[:, :NOPE]).astype(jnp.bfloat16)
        if i < len(ranks):
            home[i] = result
        else:
            away[...] = result


def attend(ranks, place, moved, lengths, query_t, own, cache_t, payload=None):
    requests, width, heads = query_t.shape
    positions = cache_t.shape[2]
    visits = payload is not None
    count = len(ranks) + int(visits)
    one = jax.ShapeDtypeStruct((heads, NOPE), jnp.bfloat16)
    many = jax.ShapeDtypeStruct((len(ranks), heads, NOPE), jnp.bfloat16)
    extra = [payload] if visits else []
    return pl.pallas_call(
        functools.partial(attend_body, ranks, visits),
        out_shape=[many] + [one] * len(extra),
        in_specs=[SCALARS] * 3 + [MAIN, WHOLE, MAIN] + [WHOLE] * len(extra),
        out_specs=[WHOLE] * (1 + len(extra)),
        scratch_shapes=[
            pltpu.VMEM((len(ranks), width, heads), jnp.bfloat16),
            pltpu.VMEM((count, width, positions), jnp.bfloat16),
            pltpu.SemaphoreType.DMA((2 * count,)),
        ],
        compiler_params=pltpu.CompilerParams(vmem_limit_bytes=58 * MIB),
        cost_estimate=pl.CostEstimate(
            flops=2 * count * heads * positions * (width + NOPE),
            bytes_accessed=0,
            transcendentals=0,
        ),
    )(place, moved, lengths, query_t, own, cache_t, *extra)


def settle_body(place, moved, stay, returned, out):
    leaving = moved[place[0]]
    for j in range(out.shape[0]):
        below = stay[max(j - 1, 0)]
        same = stay[min(j, stay.shape[0] - 1)]
        here = jnp.where(leaving < j, below, same)
        out[j] = jnp.where(leaving == j, returned[...], here)


def settle(place, moved, stay, returned):
    return pl.pallas_call(
        settle_body,
        out_shape=jax.ShapeDtypeStruct((stay.shape[0] + 1,) + returned.shape, returned.dtype),
        in_specs=[SCALARS, SCALARS, WHOLE, WHOLE],
        out_specs=WHOLE,
        compiler_params=pltpu.CompilerParams(vmem_limit_bytes=40 * MIB),
        cost_estimate=pl.CostEstimate(flops=0, bytes_accessed=0, transcendentals=0),
    )(place, moved, stay, returned)


def expert_body(count, groups, sizes, place, w_gate, w_up, w_down, *refs):
    blocks, outs = refs[:count], refs[count:]
    model_width = w_gate.shape[1]
    steps = model_width // CHUNK

    def joined(at):
        return jnp.concatenate([block[:, at].astype(jnp.float32) for block in blocks], axis=0)

    gate = up = None
    for s in range(steps):
        at = slice(s * CHUNK, (s + 1) * CHUNK)
        rows = joined(at).astype(jnp.bfloat16)
        gate_term = jnp.dot(rows, w_gate[0, at, :], preferred_element_type=jnp.float32)
        up_term = jnp.dot(rows, w_up[0, at, :], preferred_element_type=jnp.float32)
        gate = gate_term if gate is None else gate + gate_term
        up = up_term if up is None else up + up_term
    activated = (gate / (1.0 + jnp.exp(-gate)) * up).astype(jnp.bfloat16)
    parts = joined(slice(model_width, blocks[0].shape[1]))
    lane = lax.broadcasted_iota(jnp.int32, parts.shape, 1)
    mine = place[0] // SPLIT
    picked = (lane == mine) | (lane == mine + groups) | (lane == mine + 2 * groups)
    scale = jnp.sum(jnp.where(picked, parts, 0.0), axis=1, keepdims=True)
    tokens = blocks[0].shape[0]
    for s in range(steps):
        at = slice(s * CHUNK, (s + 1) * CHUNK)
        part = jnp.dot(activated, w_down[0, :, at], preferred_element_type=jnp.float32) * scale
        low = 0
        for size, out in zip(sizes, outs):
            out[:, at] = part[low : low + size * tokens].astype(jnp.bfloat16)
            low += size * tokens


def expert(place, w_gate, w_up, w_down, blocks, groups, sizes):
    count = len(blocks)
    tokens = blocks[0].shape[0]
    _, model_width, hidden = w_gate.shape
    return pl.pallas_call(
        functools.partial(expert_body, count, groups, sizes),
        out_shape=[
            jax.ShapeDtypeStruct((size * tokens, model_width), jnp.bfloat16) for size in sizes
        ],
        in_specs=[SCALARS] + [WHOLE] * (3 + count),
        out_specs=[WHOLE] * len(sizes),
        compiler_params=pltpu.CompilerParams(vmem_limit_bytes=40 * MIB),
        cost_estimate=pl.CostEstimate(
            flops=6 * count * tokens * model_width * hidden,
            bytes_accessed=6 * model_width * hidden,
            transcendentals=0,
        ),
    )(place, w_gate, w_up, w_down, *blocks)


def added(*terms):
    return sum(term.astype(jnp.float32) for term in terms).astype(jnp.bfloat16)


def per_device(
    hidden_rows,
    group_ids,
    route_gates,
    w_gate,
    w_up,
    w_down,
    queries,
    new_latent,
    latent_cache,
    cache_lengths,
    moved_slot,
):
    axis = "ep"
    ranks = lax.axis_size(axis)
    turns = ranks // 4
    groups = ranks // SPLIT
    tokens = hidden_rows.shape[0]
    requests = latent_cache.shape[0]
    position = lax.axis_index(axis)
    place = position[None]
    query_t = jnp.swapaxes(queries, 1, 2)
    cache_t = jnp.swapaxes(latent_cache, 1, 2)

    rows, payload = prepare(
        place, moved_slot, hidden_rows, group_ids.T, route_gates.T, query_t, new_latent, groups
    )

    visiting = shifted(payload, axis, -1)
    order = list(range(1, turns))
    order = order[1:2] + order[:1] + order[2:]
    columns = {r: rotated(rows, axis, r) for r in order}
    across = {0: swapped(rows, axis, 2)}

    stay, away = attend(
        tuple(range(requests - 1)),
        place,
        moved_slot,
        cache_lengths,
        query_t,
        new_latent,
        cache_t,
        visiting,
    )
    columns, across, away = lax.optimization_barrier((columns, across, away))
    later = {r: swapped(columns[r], axis, 2) for r in order}
    across.update(later)
    columns[0] = rows

    order = order + [0]
    near = [block for r in order for block in (across[r], columns[r])]
    blocks = near + [swapped(block, axis, 1) for block in near]
    sizes = [1] * len(near) + [2] * len(order)
    outs = expert(place, w_gate, w_up, w_down, blocks, groups, sizes)
    keeps, sends = outs[: len(near)], outs[len(near) :]

    chips = [swapped(send, axis, 1) for send in sends]
    leaves = [added(keeps[2 * i], chip[:tokens]) for i, chip in enumerate(chips)]
    overs = [swapped(leaf, axis, 2) for leaf in leaves[:-1]]
    overs[0], leaves[-1] = lax.optimization_barrier((overs[0], leaves[-1]))
    overs[-1], away = lax.optimization_barrier((overs[-1], away))
    overs.append(swapped(leaves[-1], axis, 2))
    sums = {
        r: [keeps[2 * i + 1], chips[i][tokens:], overs[i]] for i, r in enumerate(order)
    }
    terms = sums.pop(0)
    for r in sums:
        terms = terms + [rotated(added(*sums[r]), axis, -r)]
    returned = shifted(away, axis, 1)
    attn_out = settle(place, moved_slot, stay, returned)
    _, terms = lax.optimization_barrier((attn_out, terms))
    moe_out = added(*terms)
    return (moe_out, attn_out)


def solution(mesh):
    placed = (
        P(("group", "ep"), None),
        P(("group", "ep"), None),
        P(("group", "ep"), None),
        P("ep", None, None),
        P("ep", None, None),
        P("ep", None, None),
        P(("group", "ep"), None, None),
        P(("group", "ep"), None),
        P(("group", "ep"), None, None),
        P("group"),
        P("group"),
    )
    return jax.shard_map(
        per_device,
        mesh=mesh,
        in_specs=placed,
        out_specs=(P(("group", "ep"), None), P(("group", "ep"), None, None)),
        check_vma=False,
    )
```

```python
import functools
import math

import jax
import jax.numpy as jnp
from jax import lax
from jax.experimental import pallas as pl
from jax.experimental.pallas import tpu as pltpu
from jax.sharding import PartitionSpec as P

NOPE = 512
SPLIT = 8
LANES = 128
CHUNK = 1024
MIB = 1024 * 1024

score_scale = 1.0 / math.sqrt(192.0)

WHOLE = pl.BlockSpec(memory_space=pltpu.VMEM)
SCALARS = pl.BlockSpec(memory_space=pltpu.SMEM)
MAIN = pl.BlockSpec(memory_space=pltpu.HBM)


def shifted(value, axis, steps):
    count = lax.axis_size(axis)
    pairs = [(source, (source + steps) % count) for source in range(count)]
    return lax.ppermute(value, axis, pairs)


def rotated(value, axis, steps):
    return shifted(value, axis, 4 * steps)


def swapped(value, axis, bit):
    pairs = [(source, source ^ bit) for source in range(lax.axis_size(axis))]
    return lax.ppermute(value, axis, pairs)


def prepare_body(groups, place, moved, hidden, ids, gates, query, own, rows, payload):
    tokens, model_width = hidden.shape
    requests, width, _ = query.shape
    rows[:, :model_width] = hidden[...]
    chosen, weight = ids[...].T, gates[...].T
    lane = lax.broadcasted_iota(jnp.int32, (tokens, rows.shape[1] - model_width), 1)
    part = (lane >= groups).astype(jnp.int32) + (lane >= 2 * groups).astype(jnp.int32)
    group = lane - groups * part
    coefficient = jnp.zeros(lane.shape, jnp.float32)
    for k in range(chosen.shape[1]):
        coefficient += jnp.where(chosen[:, k : k + 1] == group, weight[:, k : k + 1], 0.0)
    high = coefficient.astype(jnp.bfloat16).astype(jnp.float32)
    middle = (coefficient - high).astype(jnp.bfloat16).astype(jnp.float32)
    low = coefficient - high - middle
    pieces = jnp.where(part == 0, high, jnp.where(part == 1, middle, low))
    rows[:, model_width:] = jnp.where(lane < 3 * groups, pieces, 0.0).astype(jnp.bfloat16)
    leaving = moved[place[0]]
    payload[:width, :] = query[leaving]
    slots = lax.broadcasted_iota(jnp.int32, own.shape, 0)
    latent = jnp.sum(
        jnp.where(slots == leaving, own[...].astype(jnp.float32), 0.0), axis=0, keepdims=True
    )
    extra = payload.shape[0] - width
    row = lax.broadcasted_iota(jnp.int32, (extra, LANES), 0)
    block = jnp.zeros((extra, LANES), jnp.float32)
    latent = jnp.concatenate([latent, jnp.zeros((1, -width % LANES), jnp.float32)], axis=1)
    for r in range(latent.shape[1] // LANES):
        block = jnp.where(row == r, latent[:, r * LANES : (r + 1) * LANES], block)
    payload[width:, :] = block.astype(jnp.bfloat16)


def prepare(place, moved, hidden, ids_t, gates_t, query_t, own, groups):
    tokens, model_width = hidden.shape
    requests, width, heads = query_t.shape
    tail = -(-3 * groups // LANES) * LANES
    extra = -(-width // (16 * LANES)) * 16
    return pl.pallas_call(
        functools.partial(prepare_body, groups),
        out_shape=[
            jax.ShapeDtypeStruct((tokens, model_width + tail), jnp.bfloat16),
            jax.ShapeDtypeStruct((width + extra, heads), jnp.bfloat16),
        ],
        in_specs=[SCALARS, SCALARS] + [WHOLE] * 5,
        out_specs=[WHOLE, WHOLE],
        compiler_params=pltpu.CompilerParams(vmem_limit_bytes=60 * MIB),
        cost_estimate=pl.CostEstimate(flops=0, bytes_accessed=0, transcendentals=0),
    )(place, moved, hidden, ids_t, gates_t, query_t, own)


def slanted(value, axis, steps):
    count = lax.axis_size(axis)
    pairs = [(source, ((source + 4 * steps) % count) ^ 2) for source in range(count)]
    return lax.ppermute(value, axis, pairs)


def attend_body(ranks, visits, place, moved, lengths, query, own, cache, *refs):
    if visits:
        payload, home, away, asking, keys, sems = refs
    else:
        home, asking, keys, sems = refs
    requests, width, positions = cache.shape
    leaving = moved[place[0]]
    slots = [rank + (leaving <= rank).astype(jnp.int32) for rank in ranks]
    copies = []
    for i, slot in enumerate(slots):
        pltpu.make_async_copy(query.at[slot], asking.at[i], sems.at[2 * i]).start()
        pltpu.make_async_copy(cache.at[slot], keys.at[i], sems.at[2 * i + 1]).start()
    if visits:
        last = len(slots)
        slots.append(leaving)
        pltpu.make_async_copy(cache.at[leaving], keys.at[last], sems.at[2 * last + 1]).start()
    which = lax.broadcasted_iota(jnp.int32, own.shape, 0)
    own_rows = own[...].astype(jnp.float32)
    work = []
    for i, slot in enumerate(slots):
        if i < len(ranks):
            pltpu.make_async_copy(query.at[slot], asking.at[i], sems.at[2 * i]).wait()
            asked = asking[i].T
            latent = jnp.sum(jnp.where(which == slot, own_rows, 0.0), axis=0, keepdims=True)
        else:
            asked = payload[:width, :].T
            tail = payload[width:, :].astype(jnp.float32)
            pieces = [tail[r : r + 1] for r in range(-(-width // LANES))]
            latent = jnp.concatenate(pieces, axis=1)[:, :width]
        pltpu.make_async_copy(cache.at[slot], keys.at[i], sems.at[2 * i + 1]).wait()
        scores = jnp.dot(asked, keys[i], preferred_element_type=jnp.float32) * score_scale
        own_score = (
            jnp.sum(asked.astype(jnp.float32) * latent, axis=1, keepdims=True) * score_scale
        )
        work.append((slot, scores, own_score, latent))
    for i, (slot, scores, own_score, latent) in enumerate(work):
        live = lax.broadcasted_iota(jnp.int32, scores.shape, 1)
        scores = jnp.where(live < lengths[place[0] * requests + slot], scores, -jnp.inf)
        top_score = jnp.maximum(jnp.max(scores, axis=1, keepdims=True), own_score)
        raised = jnp.exp(scores - top_score)
        raised_own = jnp.exp(own_score - top_score)
        share = 1.0 / (jnp.sum(raised, axis=1, keepdims=True) + raised_own)
        weights = (raised * share).astype(jnp.bfloat16)
        weight_own = (raised_own * share).astype(jnp.bfloat16).astype(jnp.float32)
        mixed = lax.dot_general(
            weights,
            keys[i, :NOPE],
            (((1,), (1,)), ((), ())),
            preferred_element_type=jnp.float32,
        )
        result = (mixed + weight_own * latent[:, :NOPE]).astype(jnp.bfloat16)
        if i < len(ranks):
            home[i] = result
        else:
            away[...] = result


def attend(ranks, place, moved, lengths, query_t, own, cache_t, payload=None):
    requests, width, heads = query_t.shape
    positions = cache_t.shape[2]
    visits = payload is not None
    count = len(ranks) + int(visits)
    one = jax.ShapeDtypeStruct((heads, NOPE), jnp.bfloat16)
    many = jax.ShapeDtypeStruct((len(ranks), heads, NOPE), jnp.bfloat16)
    extra = [payload] if visits else []
    return pl.pallas_call(
        functools.partial(attend_body, ranks, visits),
        out_shape=[many] + [one] * len(extra),
        in_specs=[SCALARS] * 3 + [MAIN, WHOLE, MAIN] + [WHOLE] * len(extra),
        out_specs=[WHOLE] * (1 + len(extra)),
        scratch_shapes=[
            pltpu.VMEM((len(ranks), width, heads), jnp.bfloat16),
            pltpu.VMEM((count, width, positions), jnp.bfloat16),
            pltpu.SemaphoreType.DMA((2 * count,)),
        ],
        compiler_params=pltpu.CompilerParams(vmem_limit_bytes=58 * MIB),
        cost_estimate=pl.CostEstimate(
            flops=2 * count * heads * positions * (width + NOPE),
            bytes_accessed=0,
            transcendentals=0,
        ),
    )(place, moved, lengths, query_t, own, cache_t, *extra)


def settle_body(place, moved, stay, returned, out):
    leaving = moved[place[0]]
    for j in range(out.shape[0]):
        below = stay[max(j - 1, 0)]
        same = stay[min(j, stay.shape[0] - 1)]
        here = jnp.where(leaving < j, below, same)
        out[j] = jnp.where(leaving == j, returned[...], here)


def settle(place, moved, stay, returned):
    return pl.pallas_call(
        settle_body,
        out_shape=jax.ShapeDtypeStruct((stay.shape[0] + 1,) + returned.shape, returned.dtype),
        in_specs=[SCALARS, SCALARS, WHOLE, WHOLE],
        out_specs=WHOLE,
        compiler_params=pltpu.CompilerParams(vmem_limit_bytes=40 * MIB),
        cost_estimate=pl.CostEstimate(flops=0, bytes_accessed=0, transcendentals=0),
    )(place, moved, stay, returned)


def expert_body(count, groups, sizes, place, w_gate, w_up, w_down, *refs):
    blocks, outs = refs[:count], refs[count:]
    model_width = w_gate.shape[1]
    steps = model_width // CHUNK

    def joined(at):
        return jnp.concatenate([block[:, at].astype(jnp.float32) for block in blocks], axis=0)

    gate = up = None
    for s in range(steps):
        at = slice(s * CHUNK, (s + 1) * CHUNK)
        rows = joined(at).astype(jnp.bfloat16)
        gate_term = jnp.dot(rows, w_gate[0, at, :], preferred_element_type=jnp.float32)
        up_term = jnp.dot(rows, w_up[0, at, :], preferred_element_type=jnp.float32)
        gate = gate_term if gate is None else gate + gate_term
        up = up_term if up is None else up + up_term
    activated = (gate / (1.0 + jnp.exp(-gate)) * up).astype(jnp.bfloat16)
    parts = joined(slice(model_width, blocks[0].shape[1]))
    lane = lax.broadcasted_iota(jnp.int32, parts.shape, 1)
    mine = place[0] // SPLIT
    picked = (lane == mine) | (lane == mine + groups) | (lane == mine + 2 * groups)
    scale = jnp.sum(jnp.where(picked, parts, 0.0), axis=1, keepdims=True)
    tokens = blocks[0].shape[0]
    for s in range(steps):
        at = slice(s * CHUNK, (s + 1) * CHUNK)
        part = jnp.dot(activated, w_down[0, :, at], preferred_element_type=jnp.float32) * scale
        low = 0
        for size, out in zip(sizes, outs):
            out[:, at] = part[low : low + size * tokens].astype(jnp.bfloat16)
            low += size * tokens


def expert(place, w_gate, w_up, w_down, blocks, groups, sizes):
    count = len(blocks)
    tokens = blocks[0].shape[0]
    _, model_width, hidden = w_gate.shape
    return pl.pallas_call(
        functools.partial(expert_body, count, groups, sizes),
        out_shape=[
            jax.ShapeDtypeStruct((size * tokens, model_width), jnp.bfloat16) for size in sizes
        ],
        in_specs=[SCALARS] + [WHOLE] * (3 + count),
        out_specs=[WHOLE] * len(sizes),
        compiler_params=pltpu.CompilerParams(vmem_limit_bytes=40 * MIB),
        cost_estimate=pl.CostEstimate(
            flops=6 * count * tokens * model_width * hidden,
            bytes_accessed=6 * model_width * hidden,
            transcendentals=0,
        ),
    )(place, w_gate, w_up, w_down, *blocks)


def added(*terms):
    return sum(term.astype(jnp.float32) for term in terms).astype(jnp.bfloat16)


def per_device(
    hidden_rows,
    group_ids,
    route_gates,
    w_gate,
    w_up,
    w_down,
    queries,
    new_latent,
    latent_cache,
    cache_lengths,
    moved_slot,
):
    axis = "ep"
    ranks = lax.axis_size(axis)
    turns = ranks // 4
    groups = ranks // SPLIT
    tokens = hidden_rows.shape[0]
    requests = latent_cache.shape[0]
    position = lax.axis_index(axis)
    place = position[None]
    query_t = jnp.swapaxes(queries, 1, 2)
    cache_t = jnp.swapaxes(latent_cache, 1, 2)

    rows, payload = prepare(
        place, moved_slot, hidden_rows, group_ids.T, route_gates.T, query_t, new_latent, groups
    )

    visiting = shifted(payload, axis, -1)
    far = list(range(2, turns))
    columns = {r: rotated(rows, axis, r) for r in far}
    across = {0: swapped(rows, axis, 2)}
    stay, away = attend(
        tuple(range(requests - 1)),
        place,
        moved_slot,
        cache_lengths,
        query_t,
        new_latent,
        cache_t,
        visiting,
    )
    columns, across, rows_then, away = lax.optimization_barrier((columns, across, rows, away))

    across.update({r: swapped(columns[r], axis, 2) for r in far})
    across[1], columns[1] = slanted(rows_then, axis, 1), rotated(rows_then, axis, 1)
    last = ({r: across.pop(r) for r in far + [1]}, columns.pop(1))
    last, columns[1] = lax.optimization_barrier(last)
    across.update(last)
    columns[0] = rows

    order = far + [1, 0]
    near = [block for r in order for block in (across[r], columns[r])]
    blocks = near + [swapped(block, axis, 1) for block in near]
    sizes = [1] * len(near) + [2] * len(order)
    outs = expert(place, w_gate, w_up, w_down, blocks, groups, sizes)
    keeps, sends = outs[: len(near)], outs[len(near) :]

    chips = [swapped(send, axis, 1) for send in sends]
    leaves = [added(keeps[2 * i], chip[:tokens]) for i, chip in enumerate(chips)]
    rests = [[keeps[2 * i + 1], chip[tokens:]] for i, chip in enumerate(chips)]
    overs = [swapped(leaf, axis, 2) for leaf in leaves[: len(far)]]
    terms = [slanted(leaves[-2], axis, -1), rotated(added(*rests[-2]), axis, -1)]
    overs[-1], terms = lax.optimization_barrier((overs[-1], terms))
    overs[0], leaves[-1], away = lax.optimization_barrier((overs[0], leaves[-1], away))
    terms = terms + rests[-1] + [swapped(leaves[-1], axis, 2)]
    for r, rest, over in zip(far, rests, overs):
        terms = terms + [rotated(added(*rest, over), axis, -r)]
    returned = shifted(away, axis, 1)
    attn_out = settle(place, moved_slot, stay, returned)
    _, terms = lax.optimization_barrier((attn_out, terms))
    moe_out = added(*terms)
    return (moe_out, attn_out)


def solution(mesh):
    placed = (
        P(("group", "ep"), None),
        P(("group", "ep"), None),
        P(("group", "ep"), None),
        P("ep", None, None),
        P("ep", None, None),
        P("ep", None, None),
        P(("group", "ep"), None, None),
        P(("group", "ep"), None),
        P(("group", "ep"), None, None),
        P("group"),
        P("group"),
    )
    return jax.shard_map(
        per_device,
        mesh=mesh,
        in_specs=placed,
        out_specs=(P(("group", "ep"), None), P(("group", "ep"), None, None)),
        check_vma=False,
    )
```

```python
import functools
import math

import jax
import jax.numpy as jnp
from jax import lax
from jax.experimental import pallas as pl
from jax.experimental.pallas import tpu as pltpu
from jax.sharding import PartitionSpec as P

NOPE = 512
SPLIT = 8
LANES = 128
CHUNK = 1024
MIB = 1024 * 1024

score_scale = 1.0 / math.sqrt(192.0)

WHOLE = pl.BlockSpec(memory_space=pltpu.VMEM)
SCALARS = pl.BlockSpec(memory_space=pltpu.SMEM)
MAIN = pl.BlockSpec(memory_space=pltpu.HBM)


def shifted(value, axis, steps):
    count = lax.axis_size(axis)
    pairs = [(source, (source + steps) % count) for source in range(count)]
    return lax.ppermute(value, axis, pairs)


def rotated(value, axis, steps):
    return shifted(value, axis, 4 * steps)


def swapped(value, axis, bit):
    pairs = [(source, source ^ bit) for source in range(lax.axis_size(axis))]
    return lax.ppermute(value, axis, pairs)


def prepare_body(groups, place, moved, hidden, ids, gates, query, own, rows, payload):
    tokens, model_width = hidden.shape
    requests, width, _ = query.shape
    rows[:, :model_width] = hidden[...]
    chosen, weight = ids[...].T, gates[...].T
    lane = lax.broadcasted_iota(jnp.int32, (tokens, rows.shape[1] - model_width), 1)
    part = (lane >= groups).astype(jnp.int32) + (lane >= 2 * groups).astype(jnp.int32)
    group = lane - groups * part
    coefficient = jnp.zeros(lane.shape, jnp.float32)
    for k in range(chosen.shape[1]):
        coefficient += jnp.where(chosen[:, k : k + 1] == group, weight[:, k : k + 1], 0.0)
    high = coefficient.astype(jnp.bfloat16).astype(jnp.float32)
    middle = (coefficient - high).astype(jnp.bfloat16).astype(jnp.float32)
    low = coefficient - high - middle
    pieces = jnp.where(part == 0, high, jnp.where(part == 1, middle, low))
    rows[:, model_width:] = jnp.where(lane < 3 * groups, pieces, 0.0).astype(jnp.bfloat16)
    leaving = moved[place[0]]
    payload[:width, :] = query[leaving]
    slots = lax.broadcasted_iota(jnp.int32, own.shape, 0)
    latent = jnp.sum(
        jnp.where(slots == leaving, own[...].astype(jnp.float32), 0.0), axis=0, keepdims=True
    )
    extra = payload.shape[0] - width
    row = lax.broadcasted_iota(jnp.int32, (extra, LANES), 0)
    block = jnp.zeros((extra, LANES), jnp.float32)
    latent = jnp.concatenate([latent, jnp.zeros((1, -width % LANES), jnp.float32)], axis=1)
    for r in range(latent.shape[1] // LANES):
        block = jnp.where(row == r, latent[:, r * LANES : (r + 1) * LANES], block)
    payload[width:, :] = block.astype(jnp.bfloat16)


def prepare(place, moved, hidden, ids_t, gates_t, query_t, own, groups):
    tokens, model_width = hidden.shape
    requests, width, heads = query_t.shape
    tail = -(-3 * groups // LANES) * LANES
    extra = -(-width // (16 * LANES)) * 16
    return pl.pallas_call(
        functools.partial(prepare_body, groups),
        out_shape=[
            jax.ShapeDtypeStruct((tokens, model_width + tail), jnp.bfloat16),
            jax.ShapeDtypeStruct((width + extra, heads), jnp.bfloat16),
        ],
        in_specs=[SCALARS, SCALARS] + [WHOLE] * 5,
        out_specs=[WHOLE, WHOLE],
        compiler_params=pltpu.CompilerParams(vmem_limit_bytes=60 * MIB),
        cost_estimate=pl.CostEstimate(flops=0, bytes_accessed=0, transcendentals=0),
    )(place, moved, hidden, ids_t, gates_t, query_t, own)


def slanted(value, axis, steps):
    count = lax.axis_size(axis)
    pairs = [(source, ((source + 4 * steps) % count) ^ 2) for source in range(count)]
    return lax.ppermute(value, axis, pairs)


def attend_body(ranks, visits, place, moved, lengths, query, own, cache, *refs):
    if visits:
        payload, home, away, asking, keys, sems = refs
    else:
        home, asking, keys, sems = refs
    requests, width, positions = cache.shape
    leaving = moved[place[0]]
    slots = [rank + (leaving <= rank).astype(jnp.int32) for rank in ranks]
    copies = []
    for i, slot in enumerate(slots):
        pltpu.make_async_copy(query.at[slot], asking.at[i], sems.at[2 * i]).start()
        pltpu.make_async_copy(cache.at[slot], keys.at[i], sems.at[2 * i + 1]).start()
    if visits:
        last = len(slots)
        slots.append(leaving)
        pltpu.make_async_copy(cache.at[leaving], keys.at[last], sems.at[2 * last + 1]).start()
    which = lax.broadcasted_iota(jnp.int32, own.shape, 0)
    own_rows = own[...].astype(jnp.float32)
    work = []
    for i, slot in enumerate(slots):
        if i < len(ranks):
            pltpu.make_async_copy(query.at[slot], asking.at[i], sems.at[2 * i]).wait()
            asked = asking[i].T
            latent = jnp.sum(jnp.where(which == slot, own_rows, 0.0), axis=0, keepdims=True)
        else:
            asked = payload[:width, :].T
            tail = payload[width:, :].astype(jnp.float32)
            pieces = [tail[r : r + 1] for r in range(-(-width // LANES))]
            latent = jnp.concatenate(pieces, axis=1)[:, :width]
        pltpu.make_async_copy(cache.at[slot], keys.at[i], sems.at[2 * i + 1]).wait()
        scores = jnp.dot(asked, keys[i], preferred_element_type=jnp.float32) * score_scale
        own_score = (
            jnp.sum(asked.astype(jnp.float32) * latent, axis=1, keepdims=True) * score_scale
        )
        work.append((slot, scores, own_score, latent))
    for i, (slot, scores, own_score, latent) in enumerate(work):
        live = lax.broadcasted_iota(jnp.int32, scores.shape, 1)
        scores = jnp.where(live < lengths[place[0] * requests + slot], scores, -jnp.inf)
        top_score = jnp.maximum(jnp.max(scores, axis=1, keepdims=True), own_score)
        raised = jnp.exp(scores - top_score)
        raised_own = jnp.exp(own_score - top_score)
        share = 1.0 / (jnp.sum(raised, axis=1, keepdims=True) + raised_own)
        weights = (raised * share).astype(jnp.bfloat16)
        weight_own = (raised_own * share).astype(jnp.bfloat16).astype(jnp.float32)
        mixed = lax.dot_general(
            weights,
            keys[i, :NOPE],
            (((1,), (1,)), ((), ())),
            preferred_element_type=jnp.float32,
        )
        result = (mixed + weight_own * latent[:, :NOPE]).astype(jnp.bfloat16)
        if i < len(ranks):
            home[i] = result
        else:
            away[...] = result


def attend(ranks, place, moved, lengths, query_t, own, cache_t, payload=None):
    requests, width, heads = query_t.shape
    positions = cache_t.shape[2]
    visits = payload is not None
    count = len(ranks) + int(visits)
    one = jax.ShapeDtypeStruct((heads, NOPE), jnp.bfloat16)
    many = jax.ShapeDtypeStruct((len(ranks), heads, NOPE), jnp.bfloat16)
    extra = [payload] if visits else []
    return pl.pallas_call(
        functools.partial(attend_body, ranks, visits),
        out_shape=[many] + [one] * len(extra),
        in_specs=[SCALARS] * 3 + [MAIN, WHOLE, MAIN] + [WHOLE] * len(extra),
        out_specs=[WHOLE] * (1 + len(extra)),
        scratch_shapes=[
            pltpu.VMEM((len(ranks), width, heads), jnp.bfloat16),
            pltpu.VMEM((count, width, positions), jnp.bfloat16),
            pltpu.SemaphoreType.DMA((2 * count,)),
        ],
        compiler_params=pltpu.CompilerParams(vmem_limit_bytes=58 * MIB),
        cost_estimate=pl.CostEstimate(
            flops=2 * count * heads * positions * (width + NOPE),
            bytes_accessed=0,
            transcendentals=0,
        ),
    )(place, moved, lengths, query_t, own, cache_t, *extra)


def settle_body(place, moved, stay, returned, out):
    leaving = moved[place[0]]
    for j in range(out.shape[0]):
        below = stay[max(j - 1, 0)]
        same = stay[min(j, stay.shape[0] - 1)]
        here = jnp.where(leaving < j, below, same)
        out[j] = jnp.where(leaving == j, returned[...], here)


def settle(place, moved, stay, returned):
    return pl.pallas_call(
        settle_body,
        out_shape=jax.ShapeDtypeStruct((stay.shape[0] + 1,) + returned.shape, returned.dtype),
        in_specs=[SCALARS, SCALARS, WHOLE, WHOLE],
        out_specs=WHOLE,
        compiler_params=pltpu.CompilerParams(vmem_limit_bytes=40 * MIB),
        cost_estimate=pl.CostEstimate(flops=0, bytes_accessed=0, transcendentals=0),
    )(place, moved, stay, returned)


def expert_body(count, groups, sizes, place, w_gate, w_up, w_down, *refs):
    blocks, outs = refs[:count], refs[count:]
    model_width = w_gate.shape[1]
    steps = model_width // CHUNK

    def joined(at):
        return jnp.concatenate([block[:, at].astype(jnp.float32) for block in blocks], axis=0)

    gate = up = None
    for s in range(steps):
        at = slice(s * CHUNK, (s + 1) * CHUNK)
        rows = joined(at).astype(jnp.bfloat16)
        gate_term = jnp.dot(rows, w_gate[0, at, :], preferred_element_type=jnp.float32)
        up_term = jnp.dot(rows, w_up[0, at, :], preferred_element_type=jnp.float32)
        gate = gate_term if gate is None else gate + gate_term
        up = up_term if up is None else up + up_term
    activated = (gate / (1.0 + jnp.exp(-gate)) * up).astype(jnp.bfloat16)
    parts = joined(slice(model_width, blocks[0].shape[1]))
    lane = lax.broadcasted_iota(jnp.int32, parts.shape, 1)
    mine = place[0] // SPLIT
    picked = (lane == mine) | (lane == mine + groups) | (lane == mine + 2 * groups)
    scale = jnp.sum(jnp.where(picked, parts, 0.0), axis=1, keepdims=True)
    tokens = blocks[0].shape[0]
    for s in range(steps):
        at = slice(s * CHUNK, (s + 1) * CHUNK)
        part = jnp.dot(activated, w_down[0, :, at], preferred_element_type=jnp.float32) * scale
        low = 0
        for size, out in zip(sizes, outs):
            out[:, at] = part[low : low + size * tokens].astype(jnp.bfloat16)
            low += size * tokens


def expert(place, w_gate, w_up, w_down, blocks, groups, sizes):
    count = len(blocks)
    tokens = blocks[0].shape[0]
    _, model_width, hidden = w_gate.shape
    return pl.pallas_call(
        functools.partial(expert_body, count, groups, sizes),
        out_shape=[
            jax.ShapeDtypeStruct((size * tokens, model_width), jnp.bfloat16) for size in sizes
        ],
        in_specs=[SCALARS] + [WHOLE] * (3 + count),
        out_specs=[WHOLE] * len(sizes),
        compiler_params=pltpu.CompilerParams(vmem_limit_bytes=40 * MIB),
        cost_estimate=pl.CostEstimate(
            flops=6 * count * tokens * model_width * hidden,
            bytes_accessed=6 * model_width * hidden,
            transcendentals=0,
        ),
    )(place, w_gate, w_up, w_down, *blocks)


def added(*terms):
    return sum(term.astype(jnp.float32) for term in terms).astype(jnp.bfloat16)


def per_device(
    hidden_rows,
    group_ids,
    route_gates,
    w_gate,
    w_up,
    w_down,
    queries,
    new_latent,
    latent_cache,
    cache_lengths,
    moved_slot,
):
    axis = "ep"
    ranks = lax.axis_size(axis)
    turns = ranks // 4
    groups = ranks // SPLIT
    tokens = hidden_rows.shape[0]
    requests = latent_cache.shape[0]
    position = lax.axis_index(axis)
    place = position[None]
    query_t = jnp.swapaxes(queries, 1, 2)
    cache_t = jnp.swapaxes(latent_cache, 1, 2)

    rows, payload = prepare(
        place, moved_slot, hidden_rows, group_ids.T, route_gates.T, query_t, new_latent, groups
    )

    visiting = shifted(payload, axis, -1)
    far = list(range(2, turns))
    columns = {r: rotated(rows, axis, r) for r in far}
    across = {0: swapped(rows, axis, 2)}
    stay, away = attend(
        tuple(range(requests - 1)),
        place,
        moved_slot,
        cache_lengths,
        query_t,
        new_latent,
        cache_t,
        visiting,
    )
    columns, across, rows_then, away = lax.optimization_barrier((columns, across, rows, away))

    across.update({r: swapped(columns[r], axis, 2) for r in far})
    across[1], columns[1] = slanted(rows_then, axis, 1), rotated(rows_then, axis, 1)
    last = ({r: across.pop(r) for r in far + [1]}, columns.pop(1))
    last, columns[1] = lax.optimization_barrier(last)
    across.update(last)
    columns[0] = rows

    order = far + [1, 0]
    near = [block for r in order for block in (across[r], columns[r])]
    blocks = near + [swapped(block, axis, 1) for block in near]
    sizes = [1] * len(near) + [2] * len(order)
    outs = expert(place, w_gate, w_up, w_down, blocks, groups, sizes)
    keeps, sends = outs[: len(near)], outs[len(near) :]

    chips = [swapped(send, axis, 1) for send in sends]
    leaves = [added(keeps[2 * i], chip[:tokens]) for i, chip in enumerate(chips)]
    leaves[0], away = lax.optimization_barrier((leaves[0], away))
    rests = [[keeps[2 * i + 1], chip[tokens:]] for i, chip in enumerate(chips)]
    overs = [swapped(leaf, axis, 2) for leaf in leaves[: len(far)]]
    terms = [slanted(leaves[-2], axis, -1), rotated(added(*rests[-2]), axis, -1)]
    returned = shifted(away, axis, 1)
    overs[-1], terms, returned = lax.optimization_barrier((overs[-1], terms, returned))
    overs[0], leaves[-1] = lax.optimization_barrier((overs[0], leaves[-1]))
    terms = terms + rests[-1] + [swapped(leaves[-1], axis, 2)]
    for r, rest, over in zip(far, rests, overs):
        terms = terms + [rotated(added(*rest, over), axis, -r)]
    attn_out = settle(place, moved_slot, stay, returned)
    _, terms = lax.optimization_barrier((attn_out, terms))
    moe_out = added(*terms)
    return (moe_out, attn_out)


def solution(mesh):
    placed = (
        P(("group", "ep"), None),
        P(("group", "ep"), None),
        P(("group", "ep"), None),
        P("ep", None, None),
        P("ep", None, None),
        P("ep", None, None),
        P(("group", "ep"), None, None),
        P(("group", "ep"), None),
        P(("group", "ep"), None, None),
        P("group"),
        P("group"),
    )
    return jax.shard_map(
        per_device,
        mesh=mesh,
        in_specs=placed,
        out_specs=(P(("group", "ep"), None), P(("group", "ep"), None, None)),
        check_vma=False,
    )
```

```python
import functools
import math

import jax
import jax.numpy as jnp
from jax import lax
from jax.experimental import pallas as pl
from jax.experimental.pallas import tpu as pltpu
from jax.sharding import PartitionSpec as P

NOPE = 512
SPLIT = 8
LANES = 128
CHUNK = 1024
MIB = 1024 * 1024

score_scale = 1.0 / math.sqrt(192.0)

WHOLE = pl.BlockSpec(memory_space=pltpu.VMEM)
SCALARS = pl.BlockSpec(memory_space=pltpu.SMEM)
MAIN = pl.BlockSpec(memory_space=pltpu.HBM)


def shifted(value, axis, steps):
    count = lax.axis_size(axis)
    pairs = [(source, (source + steps) % count) for source in range(count)]
    return lax.ppermute(value, axis, pairs)


def rotated(value, axis, steps):
    return shifted(value, axis, 4 * steps)


def swapped(value, axis, bit):
    pairs = [(source, source ^ bit) for source in range(lax.axis_size(axis))]
    return lax.ppermute(value, axis, pairs)


def prepare_body(groups, place, moved, hidden, ids, gates, query, own, rows, payload):
    tokens, model_width = hidden.shape
    requests, width, _ = query.shape
    rows[:, :model_width] = hidden[...]
    chosen, weight = ids[...].T, gates[...].T
    lane = lax.broadcasted_iota(jnp.int32, (tokens, rows.shape[1] - model_width), 1)
    part = (lane >= groups).astype(jnp.int32) + (lane >= 2 * groups).astype(jnp.int32)
    group = lane - groups * part
    coefficient = jnp.zeros(lane.shape, jnp.float32)
    for k in range(chosen.shape[1]):
        coefficient += jnp.where(chosen[:, k : k + 1] == group, weight[:, k : k + 1], 0.0)
    high = coefficient.astype(jnp.bfloat16).astype(jnp.float32)
    middle = (coefficient - high).astype(jnp.bfloat16).astype(jnp.float32)
    low = coefficient - high - middle
    pieces = jnp.where(part == 0, high, jnp.where(part == 1, middle, low))
    rows[:, model_width:] = jnp.where(lane < 3 * groups, pieces, 0.0).astype(jnp.bfloat16)
    leaving = moved[place[0]]
    payload[:width, :] = query[leaving]
    slots = lax.broadcasted_iota(jnp.int32, own.shape, 0)
    latent = jnp.sum(
        jnp.where(slots == leaving, own[...].astype(jnp.float32), 0.0), axis=0, keepdims=True
    )
    extra = payload.shape[0] - width
    row = lax.broadcasted_iota(jnp.int32, (extra, LANES), 0)
    block = jnp.zeros((extra, LANES), jnp.float32)
    latent = jnp.concatenate([latent, jnp.zeros((1, -width % LANES), jnp.float32)], axis=1)
    for r in range(latent.shape[1] // LANES):
        block = jnp.where(row == r, latent[:, r * LANES : (r + 1) * LANES], block)
    payload[width:, :] = block.astype(jnp.bfloat16)


def prepare(place, moved, hidden, ids_t, gates_t, query_t, own, groups):
    tokens, model_width = hidden.shape
    requests, width, heads = query_t.shape
    tail = -(-3 * groups // LANES) * LANES
    extra = -(-width // (16 * LANES)) * 16
    return pl.pallas_call(
        functools.partial(prepare_body, groups),
        out_shape=[
            jax.ShapeDtypeStruct((tokens, model_width + tail), jnp.bfloat16),
            jax.ShapeDtypeStruct((width + extra, heads), jnp.bfloat16),
        ],
        in_specs=[SCALARS, SCALARS] + [WHOLE] * 5,
        out_specs=[WHOLE, WHOLE],
        compiler_params=pltpu.CompilerParams(vmem_limit_bytes=60 * MIB),
        cost_estimate=pl.CostEstimate(flops=0, bytes_accessed=0, transcendentals=0),
    )(place, moved, hidden, ids_t, gates_t, query_t, own)


def attend_body(ranks, visits, place, moved, lengths, query, own, cache, *refs):
    if visits:
        payload, home, away, asking, keys, sems = refs
    else:
        home, asking, keys, sems = refs
    requests, width, positions = cache.shape
    leaving = moved[place[0]]
    slots = [rank + (leaving <= rank).astype(jnp.int32) for rank in ranks]
    copies = []
    for i, slot in enumerate(slots):
        pltpu.make_async_copy(query.at[slot], asking.at[i], sems.at[2 * i]).start()
        pltpu.make_async_copy(cache.at[slot], keys.at[i], sems.at[2 * i + 1]).start()
    if visits:
        last = len(slots)
        slots.append(leaving)
        pltpu.make_async_copy(cache.at[leaving], keys.at[last], sems.at[2 * last + 1]).start()
    which = lax.broadcasted_iota(jnp.int32, own.shape, 0)
    own_rows = own[...].astype(jnp.float32)
    work = []
    for i, slot in enumerate(slots):
        if i < len(ranks):
            pltpu.make_async_copy(query.at[slot], asking.at[i], sems.at[2 * i]).wait()
            asked = asking[i].T
            latent = jnp.sum(jnp.where(which == slot, own_rows, 0.0), axis=0, keepdims=True)
        else:
            asked = payload[:width, :].T
            tail = payload[width:, :].astype(jnp.float32)
            pieces = [tail[r : r + 1] for r in range(-(-width // LANES))]
            latent = jnp.concatenate(pieces, axis=1)[:, :width]
        pltpu.make_async_copy(cache.at[slot], keys.at[i], sems.at[2 * i + 1]).wait()
        scores = jnp.dot(asked, keys[i], preferred_element_type=jnp.float32) * score_scale
        own_score = (
            jnp.sum(asked.astype(jnp.float32) * latent, axis=1, keepdims=True) * score_scale
        )
        work.append((slot, scores, own_score, latent))
    for i, (slot, scores, own_score, latent) in enumerate(work):
        live = lax.broadcasted_iota(jnp.int32, scores.shape, 1)
        scores = jnp.where(live < lengths[place[0] * requests + slot], scores, -jnp.inf)
        top_score = jnp.maximum(jnp.max(scores, axis=1, keepdims=True), own_score)
        raised = jnp.exp(scores - top_score)
        raised_own = jnp.exp(own_score - top_score)
        share = 1.0 / (jnp.sum(raised, axis=1, keepdims=True) + raised_own)
        weights = (raised * share).astype(jnp.bfloat16)
        weight_own = (raised_own * share).astype(jnp.bfloat16).astype(jnp.float32)
        mixed = lax.dot_general(
            weights,
            keys[i, :NOPE],
            (((1,), (1,)), ((), ())),
            preferred_element_type=jnp.float32,
        )
        result = (mixed + weight_own * latent[:, :NOPE]).astype(jnp.bfloat16)
        if i < len(ranks):
            home[i] = result
        else:
            away[...] = result


def attend(ranks, place, moved, lengths, query_t, own, cache_t, payload=None):
    requests, width, heads = query_t.shape
    positions = cache_t.shape[2]
    visits = payload is not None
    count = len(ranks) + int(visits)
    one = jax.ShapeDtypeStruct((heads, NOPE), jnp.bfloat16)
    many = jax.ShapeDtypeStruct((len(ranks), heads, NOPE), jnp.bfloat16)
    extra = [payload] if visits else []
    return pl.pallas_call(
        functools.partial(attend_body, ranks, visits),
        out_shape=[many] + [one] * len(extra),
        in_specs=[SCALARS] * 3 + [MAIN, WHOLE, MAIN] + [WHOLE] * len(extra),
        out_specs=[WHOLE] * (1 + len(extra)),
        scratch_shapes=[
            pltpu.VMEM((len(ranks), width, heads), jnp.bfloat16),
            pltpu.VMEM((count, width, positions), jnp.bfloat16),
            pltpu.SemaphoreType.DMA((2 * count,)),
        ],
        compiler_params=pltpu.CompilerParams(vmem_limit_bytes=58 * MIB),
        cost_estimate=pl.CostEstimate(
            flops=2 * count * heads * positions * (width + NOPE),
            bytes_accessed=0,
            transcendentals=0,
        ),
    )(place, moved, lengths, query_t, own, cache_t, *extra)


def settle_body(place, moved, stay, returned, out):
    leaving = moved[place[0]]
    for j in range(out.shape[0]):
        below = stay[max(j - 1, 0)]
        same = stay[min(j, stay.shape[0] - 1)]
        here = jnp.where(leaving < j, below, same)
        out[j] = jnp.where(leaving == j, returned[...], here)


def settle(place, moved, stay, returned):
    return pl.pallas_call(
        settle_body,
        out_shape=jax.ShapeDtypeStruct((stay.shape[0] + 1,) + returned.shape, returned.dtype),
        in_specs=[SCALARS, SCALARS, WHOLE, WHOLE],
        out_specs=WHOLE,
        compiler_params=pltpu.CompilerParams(vmem_limit_bytes=40 * MIB),
        cost_estimate=pl.CostEstimate(flops=0, bytes_accessed=0, transcendentals=0),
    )(place, moved, stay, returned)


def expert_body(count, groups, sizes, place, w_gate, w_up, w_down, *refs):
    blocks, outs = refs[:count], refs[count:]
    model_width = w_gate.shape[1]
    steps = model_width // CHUNK

    def joined(at):
        return jnp.concatenate([block[:, at].astype(jnp.float32) for block in blocks], axis=0)

    gate = up = None
    for s in range(steps):
        at = slice(s * CHUNK, (s + 1) * CHUNK)
        rows = joined(at).astype(jnp.bfloat16)
        gate_term = jnp.dot(rows, w_gate[0, at, :], preferred_element_type=jnp.float32)
        up_term = jnp.dot(rows, w_up[0, at, :], preferred_element_type=jnp.float32)
        gate = gate_term if gate is None else gate + gate_term
        up = up_term if up is None else up + up_term
    activated = (gate / (1.0 + jnp.exp(-gate)) * up).astype(jnp.bfloat16)
    parts = joined(slice(model_width, blocks[0].shape[1]))
    lane = lax.broadcasted_iota(jnp.int32, parts.shape, 1)
    mine = place[0] // SPLIT
    picked = (lane == mine) | (lane == mine + groups) | (lane == mine + 2 * groups)
    scale = jnp.sum(jnp.where(picked, parts, 0.0), axis=1, keepdims=True)
    tokens = blocks[0].shape[0]
    for s in range(steps):
        at = slice(s * CHUNK, (s + 1) * CHUNK)
        part = jnp.dot(activated, w_down[0, :, at], preferred_element_type=jnp.float32) * scale
        low = 0
        for size, out in zip(sizes, outs):
            out[:, at] = part[low : low + size * tokens].astype(jnp.bfloat16)
            low += size * tokens


def expert(place, w_gate, w_up, w_down, blocks, groups, sizes):
    count = len(blocks)
    tokens = blocks[0].shape[0]
    _, model_width, hidden = w_gate.shape
    return pl.pallas_call(
        functools.partial(expert_body, count, groups, sizes),
        out_shape=[
            jax.ShapeDtypeStruct((size * tokens, model_width), jnp.bfloat16) for size in sizes
        ],
        in_specs=[SCALARS] + [WHOLE] * (3 + count),
        out_specs=[WHOLE] * len(sizes),
        compiler_params=pltpu.CompilerParams(vmem_limit_bytes=40 * MIB),
        cost_estimate=pl.CostEstimate(
            flops=6 * count * tokens * model_width * hidden,
            bytes_accessed=6 * model_width * hidden,
            transcendentals=0,
        ),
    )(place, w_gate, w_up, w_down, *blocks)


def added(*terms):
    return sum(term.astype(jnp.float32) for term in terms).astype(jnp.bfloat16)


def per_device(
    hidden_rows,
    group_ids,
    route_gates,
    w_gate,
    w_up,
    w_down,
    queries,
    new_latent,
    latent_cache,
    cache_lengths,
    moved_slot,
):
    axis = "ep"
    ranks = lax.axis_size(axis)
    turns = ranks // 4
    groups = ranks // SPLIT
    tokens = hidden_rows.shape[0]
    requests = latent_cache.shape[0]
    position = lax.axis_index(axis)
    place = position[None]
    query_t = jnp.swapaxes(queries, 1, 2)
    cache_t = jnp.swapaxes(latent_cache, 1, 2)

    rows, payload = prepare(
        place, moved_slot, hidden_rows, group_ids.T, route_gates.T, query_t, new_latent, groups
    )

    visiting = shifted(payload, axis, -1)
    order = list(range(1, turns))
    order = order[1:2] + order[:1] + order[2:]
    columns = {r: rotated(rows, axis, r) for r in order}
    across = {0: swapped(rows, axis, 2)}

    lead = order[-1]
    visiting, columns[lead] = lax.optimization_barrier((visiting, columns[lead]))
    ahead = {lead: columns.pop(lead)}
    crossing = swapped(ahead[lead], axis, 2)

    stay, away = attend(
        tuple(range(requests - 1)),
        place,
        moved_slot,
        cache_lengths,
        query_t,
        new_latent,
        cache_t,
        visiting,
    )
    columns, across, crossing, away = lax.optimization_barrier(
        (columns, across, crossing, away)
    )
    later = {r: swapped(columns[r], axis, 2) for r in columns}
    columns.update(ahead)
    across[lead] = crossing
    across.update(later)
    columns[0] = rows

    order = order + [0]
    near = [block for r in order for block in (across[r], columns[r])]
    blocks = near + [swapped(block, axis, 1) for block in near]
    sizes = [1] * len(near) + [2] * len(order)
    outs = expert(place, w_gate, w_up, w_down, blocks, groups, sizes)
    keeps, sends = outs[: len(near)], outs[len(near) :]

    chips = [swapped(send, axis, 1) for send in sends]
    leaves = [added(keeps[2 * i], chip[:tokens]) for i, chip in enumerate(chips)]
    overs = [swapped(leaf, axis, 2) for leaf in leaves[:-1]]
    overs[0], leaves[-1] = lax.optimization_barrier((overs[0], leaves[-1]))
    overs[-1], away = lax.optimization_barrier((overs[-1], away))
    overs.append(swapped(leaves[-1], axis, 2))
    sums = {
        r: [keeps[2 * i + 1], chips[i][tokens:], overs[i]] for i, r in enumerate(order)
    }
    terms = sums.pop(0)
    for r in sums:
        terms = terms + [rotated(added(*sums[r]), axis, -r)]
    returned = shifted(away, axis, 1)
    attn_out = settle(place, moved_slot, stay, returned)
    _, terms = lax.optimization_barrier((attn_out, terms))
    moe_out = added(*terms)
    return (moe_out, attn_out)


def solution(mesh):
    placed = (
        P(("group", "ep"), None),
        P(("group", "ep"), None),
        P(("group", "ep"), None),
        P("ep", None, None),
        P("ep", None, None),
        P("ep", None, None),
        P(("group", "ep"), None, None),
        P(("group", "ep"), None),
        P(("group", "ep"), None, None),
        P("group"),
        P("group"),
    )
    return jax.shard_map(
        per_device,
        mesh=mesh,
        in_specs=placed,
        out_specs=(P(("group", "ep"), None), P(("group", "ep"), None, None)),
        check_vma=False,
    )
```

```python
import functools
import math

import jax
import jax.numpy as jnp
from jax import lax
from jax.experimental import pallas as pl
from jax.experimental.pallas import tpu as pltpu
from jax.sharding import PartitionSpec as P

NOPE = 512
SPLIT = 8
LANES = 128
CHUNK = 1024
MIB = 1024 * 1024

score_scale = 1.0 / math.sqrt(192.0)

WHOLE = pl.BlockSpec(memory_space=pltpu.VMEM)
SCALARS = pl.BlockSpec(memory_space=pltpu.SMEM)
MAIN = pl.BlockSpec(memory_space=pltpu.HBM)


def shifted(value, axis, steps):
    count = lax.axis_size(axis)
    pairs = [(source, (source + steps) % count) for source in range(count)]
    return lax.ppermute(value, axis, pairs)


def rotated(value, axis, steps):
    return shifted(value, axis, 4 * steps)


def swapped(value, axis, bit):
    pairs = [(source, source ^ bit) for source in range(lax.axis_size(axis))]
    return lax.ppermute(value, axis, pairs)


def prepare_body(groups, place, moved, hidden, ids, gates, query, own, rows, payload):
    tokens, model_width = hidden.shape
    requests, width, _ = query.shape
    rows[:, :model_width] = hidden[...]
    chosen, weight = ids[...].T, gates[...].T
    lane = lax.broadcasted_iota(jnp.int32, (tokens, rows.shape[1] - model_width), 1)
    part = (lane >= groups).astype(jnp.int32) + (lane >= 2 * groups).astype(jnp.int32)
    group = lane - groups * part
    coefficient = jnp.zeros(lane.shape, jnp.float32)
    for k in range(chosen.shape[1]):
        coefficient += jnp.where(chosen[:, k : k + 1] == group, weight[:, k : k + 1], 0.0)
    high = coefficient.astype(jnp.bfloat16).astype(jnp.float32)
    middle = (coefficient - high).astype(jnp.bfloat16).astype(jnp.float32)
    low = coefficient - high - middle
    pieces = jnp.where(part == 0, high, jnp.where(part == 1, middle, low))
    rows[:, model_width:] = jnp.where(lane < 3 * groups, pieces, 0.0).astype(jnp.bfloat16)
    leaving = moved[place[0]]
    payload[:width, :] = query[leaving]
    slots = lax.broadcasted_iota(jnp.int32, own.shape, 0)
    latent = jnp.sum(
        jnp.where(slots == leaving, own[...].astype(jnp.float32), 0.0), axis=0, keepdims=True
    )
    extra = payload.shape[0] - width
    row = lax.broadcasted_iota(jnp.int32, (extra, LANES), 0)
    block = jnp.zeros((extra, LANES), jnp.float32)
    latent = jnp.concatenate([latent, jnp.zeros((1, -width % LANES), jnp.float32)], axis=1)
    for r in range(latent.shape[1] // LANES):
        block = jnp.where(row == r, latent[:, r * LANES : (r + 1) * LANES], block)
    payload[width:, :] = block.astype(jnp.bfloat16)


def prepare(place, moved, hidden, ids_t, gates_t, query_t, own, groups):
    tokens, model_width = hidden.shape
    requests, width, heads = query_t.shape
    tail = -(-3 * groups // LANES) * LANES
    extra = -(-width // (16 * LANES)) * 16
    return pl.pallas_call(
        functools.partial(prepare_body, groups),
        out_shape=[
            jax.ShapeDtypeStruct((tokens, model_width + tail), jnp.bfloat16),
            jax.ShapeDtypeStruct((width + extra, heads), jnp.bfloat16),
        ],
        in_specs=[SCALARS, SCALARS] + [WHOLE] * 5,
        out_specs=[WHOLE, WHOLE],
        compiler_params=pltpu.CompilerParams(vmem_limit_bytes=60 * MIB),
        cost_estimate=pl.CostEstimate(flops=0, bytes_accessed=0, transcendentals=0),
    )(place, moved, hidden, ids_t, gates_t, query_t, own)


def attend_body(ranks, visits, place, moved, lengths, query, own, cache, *refs):
    if visits:
        payload, home, away, asking, keys, sems = refs
    else:
        home, asking, keys, sems = refs
    requests, width, positions = cache.shape
    leaving = moved[place[0]]
    slots = [rank + (leaving <= rank).astype(jnp.int32) for rank in ranks]
    copies = []
    for i, slot in enumerate(slots):
        pltpu.make_async_copy(query.at[slot], asking.at[i], sems.at[2 * i]).start()
        pltpu.make_async_copy(cache.at[slot], keys.at[i], sems.at[2 * i + 1]).start()
    if visits:
        last = len(slots)
        slots.append(leaving)
        pltpu.make_async_copy(cache.at[leaving], keys.at[last], sems.at[2 * last + 1]).start()
    which = lax.broadcasted_iota(jnp.int32, own.shape, 0)
    own_rows = own[...].astype(jnp.float32)
    work = []
    for i, slot in enumerate(slots):
        if i < len(ranks):
            pltpu.make_async_copy(query.at[slot], asking.at[i], sems.at[2 * i]).wait()
            asked = asking[i].T
            latent = jnp.sum(jnp.where(which == slot, own_rows, 0.0), axis=0, keepdims=True)
        else:
            asked = payload[:width, :].T
            tail = payload[width:, :].astype(jnp.float32)
            pieces = [tail[r : r + 1] for r in range(-(-width // LANES))]
            latent = jnp.concatenate(pieces, axis=1)[:, :width]
        pltpu.make_async_copy(cache.at[slot], keys.at[i], sems.at[2 * i + 1]).wait()
        scores = jnp.dot(asked, keys[i], preferred_element_type=jnp.float32) * score_scale
        own_score = (
            jnp.sum(asked.astype(jnp.float32) * latent, axis=1, keepdims=True) * score_scale
        )
        work.append((slot, scores, own_score, latent))
    for i, (slot, scores, own_score, latent) in enumerate(work):
        live = lax.broadcasted_iota(jnp.int32, scores.shape, 1)
        scores = jnp.where(live < lengths[place[0] * requests + slot], scores, -jnp.inf)
        top_score = jnp.maximum(jnp.max(scores, axis=1, keepdims=True), own_score)
        raised = jnp.exp(scores - top_score)
        raised_own = jnp.exp(own_score - top_score)
        share = 1.0 / (jnp.sum(raised, axis=1, keepdims=True) + raised_own)
        weights = (raised * share).astype(jnp.bfloat16)
        weight_own = (raised_own * share).astype(jnp.bfloat16).astype(jnp.float32)
        mixed = lax.dot_general(
            weights,
            keys[i, :NOPE],
            (((1,), (1,)), ((), ())),
            preferred_element_type=jnp.float32,
        )
        result = (mixed + weight_own * latent[:, :NOPE]).astype(jnp.bfloat16)
        if i < len(ranks):
            home[i] = result
        else:
            away[...] = result


def attend(ranks, place, moved, lengths, query_t, own, cache_t, payload=None):
    requests, width, heads = query_t.shape
    positions = cache_t.shape[2]
    visits = payload is not None
    count = len(ranks) + int(visits)
    one = jax.ShapeDtypeStruct((heads, NOPE), jnp.bfloat16)
    many = jax.ShapeDtypeStruct((len(ranks), heads, NOPE), jnp.bfloat16)
    extra = [payload] if visits else []
    return pl.pallas_call(
        functools.partial(attend_body, ranks, visits),
        out_shape=[many] + [one] * len(extra),
        in_specs=[SCALARS] * 3 + [MAIN, WHOLE, MAIN] + [WHOLE] * len(extra),
        out_specs=[WHOLE] * (1 + len(extra)),
        scratch_shapes=[
            pltpu.VMEM((len(ranks), width, heads), jnp.bfloat16),
            pltpu.VMEM((count, width, positions), jnp.bfloat16),
            pltpu.SemaphoreType.DMA((2 * count,)),
        ],
        compiler_params=pltpu.CompilerParams(vmem_limit_bytes=57 * MIB),
        cost_estimate=pl.CostEstimate(
            flops=2 * count * heads * positions * (width + NOPE),
            bytes_accessed=0,
            transcendentals=0,
        ),
    )(place, moved, lengths, query_t, own, cache_t, *extra)


def settle_body(place, moved, stay, returned, out):
    leaving = moved[place[0]]
    for j in range(out.shape[0]):
        below = stay[max(j - 1, 0)]
        same = stay[min(j, stay.shape[0] - 1)]
        here = jnp.where(leaving < j, below, same)
        out[j] = jnp.where(leaving == j, returned[...], here)


def settle(place, moved, stay, returned):
    return pl.pallas_call(
        settle_body,
        out_shape=jax.ShapeDtypeStruct((stay.shape[0] + 1,) + returned.shape, returned.dtype),
        in_specs=[SCALARS, SCALARS, WHOLE, WHOLE],
        out_specs=WHOLE,
        compiler_params=pltpu.CompilerParams(vmem_limit_bytes=40 * MIB),
        cost_estimate=pl.CostEstimate(flops=0, bytes_accessed=0, transcendentals=0),
    )(place, moved, stay, returned)


def expert_body(count, groups, sizes, place, w_gate, w_up, w_down, *refs):
    blocks, outs = refs[:count], refs[count:]
    model_width = w_gate.shape[1]
    steps = model_width // CHUNK

    def joined(at):
        return jnp.concatenate([block[:, at].astype(jnp.float32) for block in blocks], axis=0)

    gate = up = None
    for s in range(steps):
        at = slice(s * CHUNK, (s + 1) * CHUNK)
        rows = joined(at).astype(jnp.bfloat16)
        gate_term = jnp.dot(rows, w_gate[0, at, :], preferred_element_type=jnp.float32)
        up_term = jnp.dot(rows, w_up[0, at, :], preferred_element_type=jnp.float32)
        gate = gate_term if gate is None else gate + gate_term
        up = up_term if up is None else up + up_term
    activated = (gate / (1.0 + jnp.exp(-gate)) * up).astype(jnp.bfloat16)
    parts = joined(slice(model_width, blocks[0].shape[1]))
    lane = lax.broadcasted_iota(jnp.int32, parts.shape, 1)
    mine = place[0] // SPLIT
    picked = (lane == mine) | (lane == mine + groups) | (lane == mine + 2 * groups)
    scale = jnp.sum(jnp.where(picked, parts, 0.0), axis=1, keepdims=True)
    tokens = blocks[0].shape[0]
    for s in range(steps):
        at = slice(s * CHUNK, (s + 1) * CHUNK)
        part = jnp.dot(activated, w_down[0, :, at], preferred_element_type=jnp.float32) * scale
        low = 0
        for size, out in zip(sizes, outs):
            out[:, at] = part[low : low + size * tokens].astype(jnp.bfloat16)
            low += size * tokens


def expert(place, w_gate, w_up, w_down, blocks, groups, sizes):
    count = len(blocks)
    tokens = blocks[0].shape[0]
    _, model_width, hidden = w_gate.shape
    return pl.pallas_call(
        functools.partial(expert_body, count, groups, sizes),
        out_shape=[
            jax.ShapeDtypeStruct((size * tokens, model_width), jnp.bfloat16) for size in sizes
        ],
        in_specs=[SCALARS] + [WHOLE] * (3 + count),
        out_specs=[WHOLE] * len(sizes),
        compiler_params=pltpu.CompilerParams(vmem_limit_bytes=40 * MIB),
        cost_estimate=pl.CostEstimate(
            flops=6 * count * tokens * model_width * hidden,
            bytes_accessed=6 * model_width * hidden,
            transcendentals=0,
        ),
    )(place, w_gate, w_up, w_down, *blocks)


def added(*terms):
    return sum(term.astype(jnp.float32) for term in terms).astype(jnp.bfloat16)


def per_device(
    hidden_rows,
    group_ids,
    route_gates,
    w_gate,
    w_up,
    w_down,
    queries,
    new_latent,
    latent_cache,
    cache_lengths,
    moved_slot,
):
    axis = "ep"
    ranks = lax.axis_size(axis)
    turns = ranks // 4
    groups = ranks // SPLIT
    tokens = hidden_rows.shape[0]
    requests = latent_cache.shape[0]
    position = lax.axis_index(axis)
    place = position[None]
    query_t = jnp.swapaxes(queries, 1, 2)
    cache_t = jnp.swapaxes(latent_cache, 1, 2)

    rows, payload = prepare(
        place, moved_slot, hidden_rows, group_ids.T, route_gates.T, query_t, new_latent, groups
    )

    visiting = shifted(payload, axis, -1)
    order = list(range(1, turns))
    order = order[1:2] + order[:1] + order[2:]
    columns = {r: rotated(rows, axis, r) for r in order}
    across = {0: swapped(rows, axis, 2)}

    lead = order[-1]
    visiting, columns[lead] = lax.optimization_barrier((visiting, columns[lead]))
    ahead = {lead: columns.pop(lead)}
    crossing = swapped(ahead[lead], axis, 2)

    stay, away = attend(
        tuple(range(requests - 1)),
        place,
        moved_slot,
        cache_lengths,
        query_t,
        new_latent,
        cache_t,
        visiting,
    )
    columns, across, crossing, away = lax.optimization_barrier(
        (columns, across, crossing, away)
    )
    later = {r: swapped(columns[r], axis, 2) for r in columns}
    columns.update(ahead)
    across[lead] = crossing
    across.update(later)
    columns[0] = rows

    order = order + [0]
    near = [block for r in order for block in (across[r], columns[r])]
    blocks = near + [swapped(block, axis, 1) for block in near]
    sizes = [1] * len(near) + [2] * len(order)
    outs = expert(place, w_gate, w_up, w_down, blocks, groups, sizes)
    keeps, sends = outs[: len(near)], outs[len(near) :]

    chips = [swapped(send, axis, 1) for send in sends]
    leaves = [added(keeps[2 * i], chip[:tokens]) for i, chip in enumerate(chips)]
    overs = [swapped(leaf, axis, 2) for leaf in leaves[:-1]]
    overs[0], leaves[-1] = lax.optimization_barrier((overs[0], leaves[-1]))
    overs[-1], away = lax.optimization_barrier((overs[-1], away))
    overs.append(swapped(leaves[-1], axis, 2))
    sums = {
        r: [keeps[2 * i + 1], chips[i][tokens:], overs[i]] for i, r in enumerate(order)
    }
    terms = sums.pop(0)
    for r in sums:
        terms = terms + [rotated(added(*sums[r]), axis, -r)]
    returned = shifted(away, axis, 1)
    attn_out = settle(place, moved_slot, stay, returned)
    _, terms = lax.optimization_barrier((attn_out, terms))
    moe_out = added(*terms)
    return (moe_out, attn_out)


def solution(mesh):
    placed = (
        P(("group", "ep"), None),
        P(("group", "ep"), None),
        P(("group", "ep"), None),
        P("ep", None, None),
        P("ep", None, None),
        P("ep", None, None),
        P(("group", "ep"), None, None),
        P(("group", "ep"), None),
        P(("group", "ep"), None, None),
        P("group"),
        P("group"),
    )
    return jax.shard_map(
        per_device,
        mesh=mesh,
        in_specs=placed,
        out_specs=(P(("group", "ep"), None), P(("group", "ep"), None, None)),
        check_vma=False,
    )
```

```python
import functools
import math

import jax
import jax.numpy as jnp
from jax import lax
from jax.experimental import pallas as pl
from jax.experimental.pallas import tpu as pltpu
from jax.sharding import PartitionSpec as P

NOPE = 512
SPLIT = 8
LANES = 128
CHUNK = 1024
MIB = 1024 * 1024

score_scale = 1.0 / math.sqrt(192.0)

WHOLE = pl.BlockSpec(memory_space=pltpu.VMEM)
SCALARS = pl.BlockSpec(memory_space=pltpu.SMEM)
MAIN = pl.BlockSpec(memory_space=pltpu.HBM)


def shifted(value, axis, steps):
    count = lax.axis_size(axis)
    pairs = [(source, (source + steps) % count) for source in range(count)]
    return lax.ppermute(value, axis, pairs)


def rotated(value, axis, steps):
    return shifted(value, axis, 4 * steps)


def swapped(value, axis, bit):
    pairs = [(source, source ^ bit) for source in range(lax.axis_size(axis))]
    return lax.ppermute(value, axis, pairs)


def prepare_body(groups, place, moved, hidden, ids, gates, query, own, rows, payload):
    tokens, model_width = hidden.shape
    requests, width, _ = query.shape
    rows[:, :model_width] = hidden[...]
    chosen, weight = ids[...].T, gates[...].T
    lane = lax.broadcasted_iota(jnp.int32, (tokens, rows.shape[1] - model_width), 1)
    part = (lane >= groups).astype(jnp.int32) + (lane >= 2 * groups).astype(jnp.int32)
    group = lane - groups * part
    coefficient = jnp.zeros(lane.shape, jnp.float32)
    for k in range(chosen.shape[1]):
        coefficient += jnp.where(chosen[:, k : k + 1] == group, weight[:, k : k + 1], 0.0)
    high = coefficient.astype(jnp.bfloat16).astype(jnp.float32)
    middle = (coefficient - high).astype(jnp.bfloat16).astype(jnp.float32)
    low = coefficient - high - middle
    pieces = jnp.where(part == 0, high, jnp.where(part == 1, middle, low))
    rows[:, model_width:] = jnp.where(lane < 3 * groups, pieces, 0.0).astype(jnp.bfloat16)
    leaving = moved[place[0]]
    payload[:width, :] = query[leaving]
    slots = lax.broadcasted_iota(jnp.int32, own.shape, 0)
    latent = jnp.sum(
        jnp.where(slots == leaving, own[...].astype(jnp.float32), 0.0), axis=0, keepdims=True
    )
    extra = payload.shape[0] - width
    row = lax.broadcasted_iota(jnp.int32, (extra, LANES), 0)
    block = jnp.zeros((extra, LANES), jnp.float32)
    latent = jnp.concatenate([latent, jnp.zeros((1, -width % LANES), jnp.float32)], axis=1)
    for r in range(latent.shape[1] // LANES):
        block = jnp.where(row == r, latent[:, r * LANES : (r + 1) * LANES], block)
    payload[width:, :] = block.astype(jnp.bfloat16)


def prepare(place, moved, hidden, ids_t, gates_t, query_t, own, groups):
    tokens, model_width = hidden.shape
    requests, width, heads = query_t.shape
    tail = -(-3 * groups // LANES) * LANES
    extra = -(-width // (16 * LANES)) * 16
    return pl.pallas_call(
        functools.partial(prepare_body, groups),
        out_shape=[
            jax.ShapeDtypeStruct((tokens, model_width + tail), jnp.bfloat16),
            jax.ShapeDtypeStruct((width + extra, heads), jnp.bfloat16),
        ],
        in_specs=[SCALARS, SCALARS] + [WHOLE] * 5,
        out_specs=[WHOLE, WHOLE],
        compiler_params=pltpu.CompilerParams(vmem_limit_bytes=60 * MIB),
        cost_estimate=pl.CostEstimate(flops=0, bytes_accessed=0, transcendentals=0),
    )(place, moved, hidden, ids_t, gates_t, query_t, own)


def attend_body(ranks, visits, place, moved, lengths, query, own, cache, *refs):
    if visits:
        payload, home, away, asking, keys, sems = refs
    else:
        home, asking, keys, sems = refs
    requests, width, positions = cache.shape
    leaving = moved[place[0]]
    slots = [rank + (leaving <= rank).astype(jnp.int32) for rank in ranks]
    copies = []
    for i, slot in enumerate(slots):
        pltpu.make_async_copy(query.at[slot], asking.at[i], sems.at[2 * i]).start()
        pltpu.make_async_copy(cache.at[slot], keys.at[i], sems.at[2 * i + 1]).start()
    if visits:
        last = len(slots)
        slots.append(leaving)
        pltpu.make_async_copy(cache.at[leaving], keys.at[last], sems.at[2 * last + 1]).start()
    which = lax.broadcasted_iota(jnp.int32, own.shape, 0)
    own_rows = own[...].astype(jnp.float32)
    work = []
    for i, slot in enumerate(slots):
        if i < len(ranks):
            pltpu.make_async_copy(query.at[slot], asking.at[i], sems.at[2 * i]).wait()
            asked = asking[i].T
            latent = jnp.sum(jnp.where(which == slot, own_rows, 0.0), axis=0, keepdims=True)
        else:
            asked = payload[:width, :].T
            tail = payload[width:, :].astype(jnp.float32)
            pieces = [tail[r : r + 1] for r in range(-(-width // LANES))]
            latent = jnp.concatenate(pieces, axis=1)[:, :width]
        pltpu.make_async_copy(cache.at[slot], keys.at[i], sems.at[2 * i + 1]).wait()
        scores = jnp.dot(asked, keys[i], preferred_element_type=jnp.float32) * score_scale
        own_score = (
            jnp.sum(asked.astype(jnp.float32) * latent, axis=1, keepdims=True) * score_scale
        )
        work.append((slot, scores, own_score, latent))
    for i, (slot, scores, own_score, latent) in enumerate(work):
        live = lax.broadcasted_iota(jnp.int32, scores.shape, 1)
        scores = jnp.where(live < lengths[place[0] * requests + slot], scores, -jnp.inf)
        top_score = jnp.maximum(jnp.max(scores, axis=1, keepdims=True), own_score)
        raised = jnp.exp(scores - top_score)
        raised_own = jnp.exp(own_score - top_score)
        share = 1.0 / (jnp.sum(raised, axis=1, keepdims=True) + raised_own)
        weights = (raised * share).astype(jnp.bfloat16)
        weight_own = (raised_own * share).astype(jnp.bfloat16).astype(jnp.float32)
        mixed = lax.dot_general(
            weights,
            keys[i, :NOPE],
            (((1,), (1,)), ((), ())),
            preferred_element_type=jnp.float32,
        )
        result = (mixed + weight_own * latent[:, :NOPE]).astype(jnp.bfloat16)
        if i < len(ranks):
            home[i] = result
        else:
            away[...] = result


def attend(ranks, place, moved, lengths, query_t, own, cache_t, payload=None):
    requests, width, heads = query_t.shape
    positions = cache_t.shape[2]
    visits = payload is not None
    count = len(ranks) + int(visits)
    one = jax.ShapeDtypeStruct((heads, NOPE), jnp.bfloat16)
    many = jax.ShapeDtypeStruct((len(ranks), heads, NOPE), jnp.bfloat16)
    extra = [payload] if visits else []
    return pl.pallas_call(
        functools.partial(attend_body, ranks, visits),
        out_shape=[many] + [one] * len(extra),
        in_specs=[SCALARS] * 3 + [MAIN, WHOLE, MAIN] + [WHOLE] * len(extra),
        out_specs=[WHOLE] * (1 + len(extra)),
        scratch_shapes=[
            pltpu.VMEM((len(ranks), width, heads), jnp.bfloat16),
            pltpu.VMEM((count, width, positions), jnp.bfloat16),
            pltpu.SemaphoreType.DMA((2 * count,)),
        ],
        compiler_params=pltpu.CompilerParams(vmem_limit_bytes=57 * MIB),
        cost_estimate=pl.CostEstimate(
            flops=2 * count * heads * positions * (width + NOPE),
            bytes_accessed=0,
            transcendentals=0,
        ),
    )(place, moved, lengths, query_t, own, cache_t, *extra)


def settle_body(place, moved, stay, returned, out):
    leaving = moved[place[0]]
    for j in range(out.shape[0]):
        below = stay[max(j - 1, 0)]
        same = stay[min(j, stay.shape[0] - 1)]
        here = jnp.where(leaving < j, below, same)
        out[j] = jnp.where(leaving == j, returned[...], here)


def settle(place, moved, stay, returned):
    return pl.pallas_call(
        settle_body,
        out_shape=jax.ShapeDtypeStruct((stay.shape[0] + 1,) + returned.shape, returned.dtype),
        in_specs=[SCALARS, SCALARS, WHOLE, WHOLE],
        out_specs=WHOLE,
        compiler_params=pltpu.CompilerParams(vmem_limit_bytes=40 * MIB),
        cost_estimate=pl.CostEstimate(flops=0, bytes_accessed=0, transcendentals=0),
    )(place, moved, stay, returned)


def expert_body(count, groups, sizes, place, w_gate, w_up, w_down, *refs):
    blocks, outs = refs[:count], refs[count:]
    model_width = w_gate.shape[1]
    steps = model_width // CHUNK

    def joined(at):
        return jnp.concatenate([block[:, at].astype(jnp.float32) for block in blocks], axis=0)

    gate = up = None
    for s in range(steps):
        at = slice(s * CHUNK, (s + 1) * CHUNK)
        rows = joined(at).astype(jnp.bfloat16)
        gate_term = jnp.dot(rows, w_gate[0, at, :], preferred_element_type=jnp.float32)
        up_term = jnp.dot(rows, w_up[0, at, :], preferred_element_type=jnp.float32)
        gate = gate_term if gate is None else gate + gate_term
        up = up_term if up is None else up + up_term
    activated = (gate / (1.0 + jnp.exp(-gate)) * up).astype(jnp.bfloat16)
    parts = joined(slice(model_width, blocks[0].shape[1]))
    lane = lax.broadcasted_iota(jnp.int32, parts.shape, 1)
    mine = place[0] // SPLIT
    picked = (lane == mine) | (lane == mine + groups) | (lane == mine + 2 * groups)
    scale = jnp.sum(jnp.where(picked, parts, 0.0), axis=1, keepdims=True)
    tokens = blocks[0].shape[0]
    for s in range(steps):
        at = slice(s * CHUNK, (s + 1) * CHUNK)
        part = jnp.dot(activated, w_down[0, :, at], preferred_element_type=jnp.float32) * scale
        low = 0
        for size, out in zip(sizes, outs):
            out[:, at] = part[low : low + size * tokens].astype(jnp.bfloat16)
            low += size * tokens


def expert(place, w_gate, w_up, w_down, blocks, groups, sizes):
    count = len(blocks)
    tokens = blocks[0].shape[0]
    _, model_width, hidden = w_gate.shape
    return pl.pallas_call(
        functools.partial(expert_body, count, groups, sizes),
        out_shape=[
            jax.ShapeDtypeStruct((size * tokens, model_width), jnp.bfloat16) for size in sizes
        ],
        in_specs=[SCALARS] + [WHOLE] * (3 + count),
        out_specs=[WHOLE] * len(sizes),
        compiler_params=pltpu.CompilerParams(vmem_limit_bytes=40 * MIB),
        cost_estimate=pl.CostEstimate(
            flops=6 * count * tokens * model_width * hidden,
            bytes_accessed=6 * model_width * hidden,
            transcendentals=0,
        ),
    )(place, w_gate, w_up, w_down, *blocks)


def added(*terms):
    return sum(term.astype(jnp.float32) for term in terms).astype(jnp.bfloat16)


def per_device(
    hidden_rows,
    group_ids,
    route_gates,
    w_gate,
    w_up,
    w_down,
    queries,
    new_latent,
    latent_cache,
    cache_lengths,
    moved_slot,
):
    axis = "ep"
    ranks = lax.axis_size(axis)
    turns = ranks // 4
    groups = ranks // SPLIT
    tokens = hidden_rows.shape[0]
    requests = latent_cache.shape[0]
    position = lax.axis_index(axis)
    place = position[None]
    query_t = jnp.swapaxes(queries, 1, 2)
    cache_t = jnp.swapaxes(latent_cache, 1, 2)

    rows, payload = prepare(
        place, moved_slot, hidden_rows, group_ids.T, route_gates.T, query_t, new_latent, groups
    )

    visiting = shifted(payload, axis, -1)
    order = list(range(1, turns))
    order = order[1:2] + order[:1] + order[2:]
    columns = {r: rotated(rows, axis, r) for r in order}
    across = {0: swapped(rows, axis, 2)}

    lead = order[0]
    visiting, columns[lead] = lax.optimization_barrier((visiting, columns[lead]))
    ahead = {lead: columns.pop(lead)}
    crossing = swapped(ahead[lead], axis, 2)

    stay, away = attend(
        tuple(range(requests - 1)),
        place,
        moved_slot,
        cache_lengths,
        query_t,
        new_latent,
        cache_t,
        visiting,
    )
    columns, across, crossing, away = lax.optimization_barrier(
        (columns, across, crossing, away)
    )
    later = {r: swapped(columns[r], axis, 2) for r in columns}
    columns.update(ahead)
    across[lead] = crossing
    across.update(later)
    columns[0] = rows

    order = order + [0]
    near = [block for r in order for block in (across[r], columns[r])]
    blocks = near + [swapped(block, axis, 1) for block in near]
    sizes = [1] * len(near) + [2] * len(order)
    outs = expert(place, w_gate, w_up, w_down, blocks, groups, sizes)
    keeps, sends = outs[: len(near)], outs[len(near) :]

    chips = [swapped(send, axis, 1) for send in sends]
    leaves = [added(keeps[2 * i], chip[:tokens]) for i, chip in enumerate(chips)]
    overs = [swapped(leaf, axis, 2) for leaf in leaves[:-1]]
    overs[0], leaves[-1] = lax.optimization_barrier((overs[0], leaves[-1]))
    overs[-1], away = lax.optimization_barrier((overs[-1], away))
    overs.append(swapped(leaves[-1], axis, 2))
    sums = {
        r: [keeps[2 * i + 1], chips[i][tokens:], overs[i]] for i, r in enumerate(order)
    }
    terms = sums.pop(0)
    for r in sums:
        terms = terms + [rotated(added(*sums[r]), axis, -r)]
    returned = shifted(away, axis, 1)
    attn_out = settle(place, moved_slot, stay, returned)
    _, terms = lax.optimization_barrier((attn_out, terms))
    moe_out = added(*terms)
    return (moe_out, attn_out)


def solution(mesh):
    placed = (
        P(("group", "ep"), None),
        P(("group", "ep"), None),
        P(("group", "ep"), None),
        P("ep", None, None),
        P("ep", None, None),
        P("ep", None, None),
        P(("group", "ep"), None, None),
        P(("group", "ep"), None),
        P(("group", "ep"), None, None),
        P("group"),
        P("group"),
    )
    return jax.shard_map(
        per_device,
        mesh=mesh,
        in_specs=placed,
        out_specs=(P(("group", "ep"), None), P(("group", "ep"), None, None)),
        check_vma=False,
    )
```
